32 devices in a mesh: fsdp: 2 (over x), heads: 4 (over z), tensor: 4 (over y, core).
Axes of the slice: x: 2, y: 2, z: 4, core: 2. Of those that a mesh axis runs over, the one named last changes fastest.
Arguments:
- tokens: bfloat16 [12608, 512], P(('fsdp', 'heads', 'tensor')), may hold values from -6 to 6
- gain_one: bfloat16 [512], P('fsdp'), may hold values from 0.5 to 1.5
- shift_one: bfloat16 [512], P('fsdp'), may hold values from -2 to 2
- w_qkv: bfloat16 [3, 512, 512], P(None, 'fsdp', 'heads'), may hold values from -0.25 to 0.25
- w_attn_out: bfloat16 [512, 512], P('heads', 'fsdp'), may hold values from -2 to 2
- gain_two: bfloat16 [512], P('fsdp'), may hold values from 0.5 to 1.5
- shift_two: bfloat16 [512], P('fsdp'), may hold values from -2 to 2
- w_router: bfloat16 [512, 4], P('fsdp'), may hold values from -0.26367188 to 0.26367188
- w_in: bfloat16 [4, 512, 2048], P(None, 'fsdp', 'tensor'), may hold values from -0.25 to 0.25
- w_out: bfloat16 [4, 2048, 512], P(None, 'tensor', 'fsdp'), may hold values from -0.375 to 0.375
- routes: int32 [12608, 2], P(('fsdp', 'heads')), may hold values from 0 to 3, all different within a row; in each aligned block of 394 rows (0 to 393, 394 to 787, ...) at most 246 rows name the same one
- cotangent: bfloat16 [12608, 512], P(('fsdp', 'heads', 'tensor')), may hold values from -6 to 6
Outputs:
- output: bfloat16 [12608, 512], P(('fsdp', 'heads', 'tensor'))
- input_grad: bfloat16 [12608, 512], P(('fsdp', 'heads', 'tensor'))
- gain_one_grad: float32 [512], P('fsdp')
- shift_one_grad: float32 [512], P('fsdp')
- w_qkv_grad: float32 [3, 512, 512], P(None, 'fsdp', 'heads')
- w_attn_out_grad: float32 [512, 512], P('heads', 'fsdp')
- gain_two_grad: float32 [512], P('fsdp')
- shift_two_grad: float32 [512], P('fsdp')
- w_router_grad: float32 [512, 4], P('fsdp')
- w_in_grad: float32 [4, 512, 2048], P(None, 'fsdp', 'tensor')
- w_out_grad: float32 [4, 2048, 512], P(None, 'tensor', 'fsdp')
The draws below stay inside these ranges and needn't reach their ends.
Inputs may be any that keep to these rules, and one draw needn't show every extreme that they name: `routes`: the two experts of a row differ; in each aligned block of 394 rows (the rows of one device) no expert is named by more than 246 rows, and in some blocks one is named by exactly 246.
All inputs are finite; a program needn't handle non-finite values.
Results may differ from the reference program's by a relative error of at most 0.025.
Values may be sent and summed in bfloat16 or wider, within the bound.
No kernel may reach another device: no remote copies, remote signals or barrier semaphores. Data moves between devices by JAX's collectives and lax.ppermute only.
A program may use at most 128 MiB of HBM per device.

```python
import math
import jax
import jax.numpy as jnp
import numpy as np
from jax import lax

D = 512
HEADS = 8
HD = 64
FF = 2048
SEQ = 197
EXPERTS = 4
TOK_DEV = 394
MOST = 246
IMAGES = 64
TOKENS = 12608


def shard_levels(own_key, extent, shards, low, high):
    loudness, own = 1.0, jax.random.fold_in(own_key, 6)
    for axis_at, shards_of in shards:
        draws = jnp.exp(jax.random.uniform(jax.random.fold_in(own, axis_at), (shards_of,), jnp.float32, low / len(shards), high / len(shards)))
        loudness = loudness * jnp.repeat(draws, extent[axis_at] // shards_of).reshape([-1 if axis == axis_at else 1 for axis in range(len(extent))])
    return loudness


def routed_block(key, own, number, rows, number_of, top, limit, skew):
    sequence = jax.random.permutation(key, number_of)
    crowded, common = portions_of(number_of, rows * top, limit, skew, True), portions_of(number_of, rows * top, limit, skew, False)
    places = jnp.arange(number_of)

    def named(lengths, turn):
        used = int((lengths > 0).sum())
        fixed = max(1, used // 4)
        shifted = fixed + (places - fixed + turn * (used - fixed)) % max(1, number_of - fixed)
        return jnp.zeros((number_of,), jnp.int32).at[sequence[jnp.where(places < fixed, places, shifted)]].set(jnp.asarray(lengths, jnp.int32))

    lengths = jnp.where(number % 4 == 0, named(crowded, number // 4), named(common, number - number // 4 - 1))
    mixed = jax.random.permutation(jax.random.fold_in(own, 3), number_of)
    donor, sink = mixed[0:number_of // 2 * 2:2], mixed[1:number_of // 2 * 2:2]
    margin = jnp.minimum(lengths[donor] - 1, limit - lengths[sink]) // 2
    margin = jnp.where((donor == sequence[0]) | (sink == sequence[0]) | (lengths[sink] == 0), 0, jnp.maximum(margin, 0))
    shifted = jax.random.randint(jax.random.fold_in(own, 4), (number_of // 2,), 0, 1 << 20) % (margin + 1)
    lengths = lengths.at[donor].add(-shifted).at[sink].add(shifted)
    members = jnp.searchsorted(jnp.cumsum(lengths), jnp.arange(rows * top), side="right").astype(jnp.int32)
    grid = members.reshape(top, rows).T
    grid = grid[jax.random.permutation(jax.random.fold_in(own, 1), rows)]
    turn = jax.random.randint(jax.random.fold_in(own, 2), (rows, 1), 0, top)
    return jnp.take_along_axis(grid, (jnp.arange(top)[None, :] + turn) % top, axis=1)


def portions_of(number_of, total, bound, lean, full):
    portions = [(1 << 20) // math.isqrt(standing ** lean) + 1 for standing in range(1, number_of + 1)]
    largest = bound if full else min(bound, max(-(-total // number_of), total * portions[0] // sum(portions)))
    least = 1 if total - largest >= number_of - 1 else 0
    given, rest = [largest] + [least] * (number_of - 1), total - largest - least * (number_of - 1)
    while rest > 0:
        candidates = [i for i in range(1, number_of) if given[i] < largest] or [i for i in range(1, number_of) if given[i] < bound]
        pool, budget = sum([portions[i] for i in candidates]), rest
        for i in candidates:
            addition = min(bound - given[i], max(1, budget * portions[i] // pool), rest)
            given[i] = given[i] + addition
            rest = rest - addition
    return np.array(given)


def normal_values(key, shape, scale, bound, split=(), kind=jnp.bfloat16):
    drawn = scale * jax.random.normal(key, shape, jnp.float32)
    if split:
        drawn = drawn * shard_levels(key, shape, split, -0.22, 0.18)
    return jnp.clip(drawn, -bound, bound).astype(kind)


def setup_inputs(seed: int = 0) -> dict:
    streams_of = jax.random.split(jax.random.key(seed), 13)
    tokens = normal_values(streams_of[0], (TOKENS, D), 1.0, 6.0, ((0, 32),))
    gain_one = jnp.clip(1.0 + 0.1 * jax.random.normal(streams_of[1], (D,), jnp.float32), 0.5, 1.5).astype(jnp.bfloat16)
    shift_one = normal_values(streams_of[2], (D,), 0.3, 2.0, ((0, 2),))
    w_qkv = normal_values(streams_of[3], (3, D, D), D ** -0.5, 0.25, ((1, 2), (2, 4)))
    w_attn_out = normal_values(streams_of[4], (D, D), (4 * D // SEQ) ** -0.5, 2.0, ((0, 4), (1, 2)))
    gain_two = jnp.clip(1.0 + 0.1 * jax.random.normal(streams_of[5], (D,), jnp.float32), 0.5, 1.5).astype(jnp.bfloat16)
    shift_two = normal_values(streams_of[6], (D,), 0.3, 2.0, ((0, 2),))
    w_router = normal_values(streams_of[7], (D, EXPERTS), (0.75 * D ** -0.5), 0.26367188, ((0, 2),))
    w_in = normal_values(streams_of[8], (EXPERTS, D, FF), D ** -0.5, 0.25, ((1, 2), (2, 4)))
    w_out = normal_values(streams_of[9], (EXPERTS, FF, D), (FF // 8) ** -0.5, 0.375, ((1, 4), (2, 2)))
    routes_keys = jax.random.split(jax.random.fold_in(streams_of[10], 1), TOKENS // TOK_DEV)
    routes_turns = jax.random.permutation(jax.random.fold_in(streams_of[10], 3), TOKENS // TOK_DEV)
    routes = jax.vmap(lambda own, number: routed_block(jax.random.fold_in(streams_of[10], 2), own, number, TOK_DEV, EXPERTS, 2, MOST, 1))(routes_keys, routes_turns).reshape((TOKENS, 2))
    cotangent = normal_values(streams_of[11], (TOKENS, D), 1.0, 6.0, ((0, 32),))
    return dict(tokens=tokens, gain_one=gain_one, shift_one=shift_one, w_qkv=w_qkv, w_attn_out=w_attn_out, gain_two=gain_two, shift_two=shift_two, w_router=w_router, w_in=w_in, w_out=w_out, routes=routes, cotangent=cotangent)


@jax.custom_vjp
def low(v):
    return lax.optimization_barrier(v.astype(jnp.bfloat16)).astype(jnp.float32)

@jax.custom_vjp
def low_back(v):
    return v

def low_keep(v):
    return (low(v), None)

def low_pass(kept, grad):
    return (grad,)

def back_keep(v):
    return (v, None)

def back_low(kept, grad):
    return (low(grad),)
low.defvjp(low_keep, low_pass)
low_back.defvjp(back_keep, back_low)
highest = lax.Precision.HIGHEST

def layer_norm(values, gain, shift):
    center = lax.optimization_barrier(jnp.mean(values, -1, keepdims=True))
    centered = values - center
    spread = lax.optimization_barrier(jnp.mean(centered * centered, -1, keepdims=True))
    return centered * lax.rsqrt(spread + 1e-06) * gain + shift

def block_forward(params, block_rows, block_routes):
    gain_one, shift_one, w_qkv, w_attn_out, gain_two, shift_two, w_router, w_in, w_out = params
    count = block_rows.shape[0]
    images = count // SEQ
    normed_one = low(layer_norm(block_rows, gain_one, shift_one))
    projected = jnp.einsum('td,cdk->ctk', normed_one, w_qkv, precision=highest)
    projected = low(low_back(projected))
    pieces = projected.reshape(3, images, SEQ, HEADS, HD)
    scores = jnp.einsum('ishd,ithd->ihst', pieces[0], pieces[1], precision=highest) * 0.125
    scores = low_back(scores)
    weights_att = jax.nn.softmax(scores, axis=-1)
    attn_mix = jnp.einsum('ihst,ithd->ishd', low(weights_att), pieces[2], precision=highest)
    attn_mix = low(low_back(attn_mix.reshape(count, D)))
    attended = low_back(jnp.dot(attn_mix, w_attn_out, precision=highest))
    resid = block_rows + attended
    normed_two = low(layer_norm(resid, gain_two, shift_two))
    logits = low_back(jnp.dot(normed_two, w_router, precision=highest))
    router = jax.nn.softmax(logits, axis=-1)
    chosen = (block_routes[:, :, None] == jnp.arange(EXPERTS, dtype=jnp.int32)).astype(jnp.float32)
    gates = lax.optimization_barrier(jnp.sum(router[:, None, :] * chosen, -1))
    per_expert = lax.optimization_barrier(jnp.sum(gates[:, :, None] * chosen, 1))
    mixture = jnp.zeros_like(resid)
    for expert in range(EXPERTS):
        inner = low_back(jnp.dot(normed_two, w_in[expert], precision=highest))
        hidden = low(jax.nn.gelu(inner))
        result = low_back(jnp.dot(hidden, w_out[expert], precision=highest))
        mixture = mixture + per_expert[:, expert:expert + 1] * result
    return resid + mixture

def reference(tokens, gain_one, shift_one, w_qkv, w_attn_out, gain_two, shift_two, w_router, w_in, w_out, routes, cotangent):
    params = tuple((item.astype(jnp.float32) for item in (gain_one, shift_one, w_qkv, w_attn_out, gain_two, shift_two, w_router, w_in, w_out)))
    rows_all = tokens.astype(jnp.float32)
    group = math.gcd(IMAGES, 16)
    blocks = IMAGES // group

    def forward(weights, rows):
        rows_blocked = rows.reshape(blocks, group * SEQ, D)
        routes_blocked = routes.reshape(blocks, group * SEQ, 2)

        def one_block(pair):
            return block_forward(weights, pair[0], pair[1])
        return lax.map(jax.checkpoint(one_block), (rows_blocked, routes_blocked)).reshape(TOKENS, D)
    result, pullback = jax.vjp(forward, params, rows_all)
    grads, rows_grad = pullback(cotangent.astype(jnp.float32))
    return (result.astype(jnp.bfloat16), rows_grad.astype(jnp.bfloat16), grads[0], grads[1], grads[2], grads[3], grads[4], grads[5], grads[6], grads[7], grads[8])
```

```python
import functools

import jax
import jax.numpy as jnp
from jax import lax
from jax.experimental import pallas as pl
from jax.experimental.pallas import tpu as pltpu
from jax.sharding import PartitionSpec as P

HD = 64
SEQ = 197
PAD = 208
ROWS = 2 * PAD
D = 512
FFT = 512
EXPERTS = 4
BF = jnp.bfloat16
F32 = jnp.float32
VMEM_LIMIT = 56 * 1024 * 1024
GELU_C = 0.7978845608028654


def nn(a, b):
    return lax.dot_general(a, b, (((1,), (0,)), ((), ())), preferred_element_type=F32)


def nt(a, b):
    return lax.dot_general(a, b, (((1,), (1,)), ((), ())), preferred_element_type=F32)


def tn(a, b):
    return lax.dot_general(a, b, (((0,), (0,)), ((), ())), preferred_element_type=F32)


def params(sem=None):
    return pltpu.CompilerParams(vmem_limit_bytes=VMEM_LIMIT, dimension_semantics=sem)


def smem():
    return pl.BlockSpec(memory_space=pltpu.SMEM)


def vmem():
    return pl.BlockSpec(memory_space=pltpu.VMEM)


def sds(shape, dtype):
    return jax.ShapeDtypeStruct(shape, dtype)


def call(kernel, outs, args, scratch=()):
    return pl.pallas_call(
        kernel,
        out_shape=outs,
        in_specs=[smem()] + [vmem()] * (len(args) - 1),
        out_specs=[vmem()] * len(outs),
        scratch_shapes=list(scratch),
        compiler_params=params(),
    )(*args)


def pack_kernel(idx, wqkv, wo, out):
    c = idx[1]
    rows = pl.ds(pl.multiple_of(c * 128, 128), 128)
    for i in range(3):
        out[i * 128 : (i + 1) * 128, :] = wqkv[i, rows, :]
    head = pl.ds(pl.multiple_of(c * 64, 64), 64)
    out[384:448, :] = wo[head, 0:128]
    out[448:512, :] = wo[head, 128:256]


def spread(v):
    zero = jnp.zeros((PAD - SEQ, v.shape[1]), v.dtype)
    return jnp.concatenate([v[:SEQ], zero, v[SEQ:], zero], axis=0)


def close(v):
    return jnp.concatenate([v[:SEQ], v[PAD : PAD + SEQ]], axis=0)


def pad_kernel(idx, tok, cot, tok_out, cot_out):
    tok_out[...] = spread(tok[...].astype(F32)).astype(BF)
    cot_out[...] = spread(cot[...].astype(F32)).astype(BF)


def norm_parts(x):
    center = jnp.mean(x, -1, keepdims=True)
    centered = x - center
    rstd = lax.rsqrt(jnp.mean(centered * centered, -1, keepdims=True) + 1e-06)
    return centered * rstd, rstd


def norm_back(xhat, rstd, grad, gain):
    dxhat = grad * gain
    m1 = jnp.mean(dxhat, -1, keepdims=True)
    m2 = jnp.mean(dxhat * xhat, -1, keepdims=True)
    return rstd * (dxhat - m1 - xhat * m2)


def attn_fwd_kernel(idx, tok, small, *refs):
    packs, (n1_ref, n2_ref, resid_ref, qkv_ref, mix_ref, wq_ref, wo_ref) = refs[:8], refs[8:]
    f, c = idx[0], idx[1]
    x = tok[...].astype(F32)
    xhat, _ = norm_parts(x)
    n1 = (xhat * small[4:5, :].astype(F32) + small[5:6, :].astype(F32)).astype(BF)
    n1_ref[...] = n1
    lane = lax.broadcasted_iota(jnp.int32, (PAD, 128), 1)
    key = lax.broadcasted_iota(jnp.int32, (PAD, PAD), 1)
    acc = [x[0:PAD], x[PAD:ROWS]]
    for j in range(4):
        for fr in range(2):
            fa = jnp.bitwise_xor(f, fr)
            for cr in range(2):
                ca = jnp.bitwise_xor(c, cr)
                src = packs[2 * j + cr]
                rows = pl.ds(pl.multiple_of(fa * 256 + ca * 128, 128), 128)
                for i in range(3):
                    wq_ref[j, rows, i * 128 : (i + 1) * 128] = src[fr, i * 128 : (i + 1) * 128, :]
                head = pl.ds(pl.multiple_of(ca * 64, 64), 64)
                for i in range(2):
                    cols = pl.ds(pl.multiple_of(fa * 256 + i * 128, 128), 128)
                    wo_ref[j, head, cols] = src[fr, 384 + 64 * i : 448 + 64 * i, :]
        qkv_ref[j] = nn(n1, wq_ref[j]).astype(BF)
        for im in range(2):
            r = slice(im * PAD, (im + 1) * PAD)
            q, k, v = (qkv_ref[j, r, i * 128 : (i + 1) * 128] for i in range(3))
            outs = []
            for head in range(2):
                s = nt(jnp.where(lane // HD == head, q, jnp.zeros_like(q)), k) * 0.125
                s = jnp.where(key < SEQ, s, -1e30)
                e = jnp.exp(s - jnp.max(s, -1, keepdims=True))
                p = e / jnp.sum(e, -1, keepdims=True)
                outs.append(nn(p.astype(BF), v))
            mix = jnp.where(lane < HD, outs[0], outs[1]).astype(BF)
            mix_ref[j, r, :] = mix
            acc[im] = acc[im] + nn(mix, wo_ref[j])
    for im in range(2):
        r = slice(im * PAD, (im + 1) * PAD)
        resid_ref[r, :] = acc[im]
        xhat, _ = norm_parts(acc[im])
        n2_ref[r, :] = (xhat * small[6:7, :].astype(F32) + small[7:8, :].astype(F32)).astype(BF)


def attn_bwd_kernel(idx, d0, d1, d2, resid, cot, tok, small, n1, qkv, mix, wq, wo, wrg, *refs):
    packs, (igrad, sgrad, dqkv_s, gq_s, go_s, dn1_s) = refs[:8], refs[8:]
    f, c = idx[0], idx[1]
    dn2 = d0[...].astype(F32) + d1[...].astype(F32) + d2[...].astype(F32)
    xhat, rstd = norm_parts(resid[...])
    sgrad[0:4, :] = wrg[0:4, :]
    sgrad[6:7, :] = jnp.sum(dn2 * xhat, 0, keepdims=True)
    sgrad[7:8, :] = jnp.sum(dn2, 0, keepdims=True)
    dresid = cot[...].astype(F32) + norm_back(xhat, rstd, dn2, small[6:7, :].astype(F32))
    resid_grad = dresid
    dattn = dresid.astype(BF)
    lane = lax.broadcasted_iota(jnp.int32, (PAD, 128), 1)
    key = lax.broadcasted_iota(jnp.int32, (PAD, PAD), 0)
    n1t = n1[...].T
    for j in range(4):
        go_s[...] = tn(mix[j], dattn).astype(BF)
        dmix = nt(dattn, wo[j]).astype(BF)
        for im in range(2):
            r = slice(im * PAD, (im + 1) * PAD)
            q, k, v = (qkv[j, r, i * 128 : (i + 1) * 128] for i in range(3))
            dm = dmix[r]
            dq, dk, dv = [], [], []
            for head in range(2):
                keep = lane // HD == head
                s = nt(k, jnp.where(keep, q, jnp.zeros_like(q))) * 0.125
                s = jnp.where(key < SEQ, s, -1e30)
                e = jnp.exp(s - jnp.max(s, 0, keepdims=True))
                p = e / jnp.sum(e, 0, keepdims=True)
                dp = nt(v, jnp.where(keep, dm, jnp.zeros_like(dm)))
                ds = (p * (dp - jnp.sum(p * dp, 0, keepdims=True))).astype(BF)
                dq.append(tn(ds, k))
                dk.append(nn(ds, q))
                dv.append(nn(p.astype(BF), dm))
            first = lane < HD
            dqkv_s[r, 0:128] = (jnp.where(first, dq[0], dq[1]) * 0.125).astype(BF)
            dqkv_s[r, 128:256] = (jnp.where(first, dk[0], dk[1]) * 0.125).astype(BF)
            dqkv_s[r, 256:384] = jnp.where(first, dv[0], dv[1]).astype(BF)
        dqkv = dqkv_s[...]
        gq_s[...] = nn(n1t, dqkv).astype(BF)
        part = nt(dqkv, wq[j])
        if j == 0:
            dn1_s[...] = part
        else:
            dn1_s[...] += part
        for fr in range(2):
            fa = jnp.bitwise_xor(f, fr)
            for cr in range(2):
                ca = jnp.bitwise_xor(c, cr)
                dst = packs[2 * j + cr]
                rows = pl.ds(pl.multiple_of(fa * 256 + ca * 128, 128), 128)
                for i in range(3):
                    dst[fr, i * 128 : (i + 1) * 128, :] = gq_s[rows, i * 128 : (i + 1) * 128]
                head = pl.ds(pl.multiple_of(ca * 64, 64), 64)
                for i in range(2):
                    cols = pl.ds(pl.multiple_of(fa * 256 + i * 128, 128), 128)
                    dst[fr, 384 + 64 * i : 448 + 64 * i, :] = go_s[head, cols]
    dn1 = dn1_s[...]
    xhat, rstd = norm_parts(tok[...].astype(F32))
    sgrad[4:5, :] = jnp.sum(dn1 * xhat, 0, keepdims=True)
    sgrad[5:6, :] = jnp.sum(dn1, 0, keepdims=True)
    grad = resid_grad + norm_back(xhat, rstd, dn1, small[4:5, :].astype(F32))
    igrad[...] = close(grad).astype(BF)


def out_kernel(idx, resid, m0, m1, m2, out):
    total = resid[...] + m0[...].astype(F32) + m1[...].astype(F32) + m2[...].astype(F32)
    out[...] = close(total).astype(BF)


def moe_kernel(final, idx, x0, x1, g0, g1, sel, small, win_a, win_b, wout_a, wout_b, *refs):
    if final:
        gin_in, gout_in, refs = refs[0], refs[1], refs[2:]
        keep, send, refs = refs[0], refs[1], refs[2:]
    else:
        gin_out, gout_out, refs = refs[0], refs[1], refs[2:]
    mix0, mix1, dn0, dn1, wrg, win, wout, xt, gt, gates, router, dprob, mix_s, dn_s, gin_s, gout_s = refs
    e = pl.program_id(0)
    f, t = idx[0], idx[2]
    xs, gs = (x0, x1), (g0, g1)
    base = 2 if final else 0
    lane = lax.broadcasted_iota(jnp.int32, (ROWS, 8), 1)

    @pl.when(e == 0)
    def _():
        dprob[...] = jnp.zeros_like(dprob)
        mix_s[...] = jnp.zeros_like(mix_s)
        dn_s[...] = jnp.zeros_like(dn_s)
        for b in range(2):
            xt[b] = xs[b][...].T
            gt[b] = gs[b][...].T
            logits = nt(xs[b][...], small[...])
            logits = jnp.where(lane < EXPERTS, logits, -1e30)
            ex = jnp.exp(logits - jnp.max(logits, -1, keepdims=True))
            prob = ex / jnp.sum(ex, -1, keepdims=True)
            router[b] = prob
            gates[b] = prob * sel[jnp.bitwise_xor(t, base + b)]

    own = pl.ds(pl.multiple_of(f * 256, 256), 256)
    oth = pl.ds(pl.multiple_of((1 - f) * 256, 256), 256)
    win[own, :] = win_a[0]
    win[oth, :] = win_b[0]
    wout[:, own] = wout_a[0]
    wout[:, oth] = wout_b[0]
    gin = gout = None
    for b in range(2):
        inner = nn(xs[b][...], win[...])
        back = nt(gs[b][...], wout[...])
        gate = jnp.sum(jnp.where(lane == e, gates[b], 0.0), -1, keepdims=True)
        square = inner * inner
        th = jnp.tanh(GELU_C * inner * (1.0 + 0.044715 * square))
        half = 0.5 * (1.0 + th)
        hidden = inner * half
        slope = half + 0.5 * inner * (1.0 - th * th) * (GELU_C * (1.0 + (3 * 0.044715) * square))
        dprob[b] += jnp.where(lane == e, jnp.sum(hidden * back, -1, keepdims=True), 0.0)
        hg = (gate * hidden).astype(BF)
        di = (gate * back * slope).astype(BF)
        mix_s[b] += nn(hg, wout[...])
        dn_s[b] += nt(di, win[...])
        part_in, part_out = nn(xt[b], di), nn(gt[b], hg)
        gin = part_in if gin is None else gin + part_in
        gout = part_out if gout is None else gout + part_out
    if final:
        gin_s[...] = (gin + gin_in[0]).astype(BF)
        gout_s[...] = (gout + gout_in[0]).astype(BF)
        for dst, rows in ((keep, own), (send, oth)):
            dst[0, 0:256, :] = gin_s[rows, :]
            dst[0, 256:512, :] = gout_s[rows, :]
    else:
        gin_out[0] = gin
        gout_out[0] = gout

    @pl.when(e == pl.num_programs(0) - 1)
    def _():
        for b, dn, mx in ((0, dn0, mix0), (1, dn1, mix1)):
            chosen = sel[jnp.bitwise_xor(t, base + b)]
            dp = dprob[b] * chosen
            dl = router[b] * (dp - jnp.sum(router[b] * dp, -1, keepdims=True))
            dl = jnp.where(lane < EXPERTS, dl, 0.0).astype(BF)
            dn[...] = (dn_s[b] + nn(dl, small[...])).astype(BF)
            mx[...] = mix_s[b].astype(BF)
            part = tn(dl, xs[b][...])
            if b == 0:
                wrg[...] = part
            else:
                wrg[...] += part


def moe(final, idx, xs, gs, sel, small, weights, carried):
    whole = lambda shape: pl.BlockSpec(shape, lambda e: (0,) * len(shape))
    expert = lambda shape: pl.BlockSpec((1,) + shape, lambda e: (e, 0, 0))
    row = whole((ROWS, D))
    in_specs = [smem(), row, row, row, row, whole((4, ROWS, 8)), whole((8, D))]
    in_specs += [expert((256, FFT))] * 2 + [expert((FFT, 256))] * 2
    outs, out_specs = [], []
    if final:
        in_specs += [expert((D, FFT))] * 2
        outs += [sds((EXPERTS, D, FFT), BF)] * 2
    else:
        outs += [sds((EXPERTS, D, FFT), F32)] * 2
    out_specs += [expert((D, FFT))] * 2
    outs += [sds((ROWS, D), BF)] * 4 + [sds((8, D), F32)]
    out_specs += [row] * 4 + [whole((8, D))]
    scratch = [
        pltpu.VMEM((D, FFT), BF),
        pltpu.VMEM((FFT, D), BF),
        pltpu.VMEM((2, D, ROWS), BF),
        pltpu.VMEM((2, D, ROWS), BF),
        pltpu.VMEM((2, ROWS, 8), F32),
        pltpu.VMEM((2, ROWS, 8), F32),
        pltpu.VMEM((2, ROWS, 8), F32),
        pltpu.VMEM((2, ROWS, D), F32),
        pltpu.VMEM((2, ROWS, D), F32),
        pltpu.VMEM((D, FFT), BF),
        pltpu.VMEM((D, FFT), BF),
    ]
    return pl.pallas_call(
        functools.partial(moe_kernel, final),
        grid=(EXPERTS,),
        out_shape=outs,
        in_specs=in_specs,
        out_specs=out_specs,
        scratch_shapes=scratch,
        compiler_params=params(("arbitrary",)),
    )(idx, *xs, *gs, sel, small, *weights, *carried)


def finish_kernel(idx, total, win_grad, wout_grad):
    win_grad[0] = total[0, 0:256, :].astype(F32)
    wout_grad[0] = total[0, 256:512, :].astype(F32).T


def finish(idx, total):
    expert = lambda shape: pl.BlockSpec((1,) + shape, lambda e: (e, 0, 0))
    return pl.pallas_call(
        finish_kernel,
        grid=(EXPERTS,),
        out_shape=[sds((EXPERTS, 256, FFT), F32), sds((EXPERTS, FFT, 256), F32)],
        in_specs=[smem(), expert((512, FFT))],
        out_specs=[expert((256, FFT)), expert((FFT, 256))],
        compiler_params=params(("arbitrary",)),
    )(idx, total)


def unpack_kernel(idx, own, sib, qkv_grad, o_grad):
    c = idx[1]
    for src, ca in ((own, c), (sib, 1 - c)):
        rows = pl.ds(pl.multiple_of(ca * 128, 128), 128)
        for i in range(3):
            qkv_grad[i, rows, :] = src[i * 128 : (i + 1) * 128, :].astype(F32)
        head = pl.ds(pl.multiple_of(ca * 64, 64), 64)
        o_grad[head, 0:128] = src[384:448, :].astype(F32)
        o_grad[head, 128:256] = src[448:512, :].astype(F32)


def flip(x, axis, bit):
    n = lax.axis_size(axis)
    return lax.ppermute(x, axis, [(i, i ^ bit) for i in range(n)])


def core(x):
    return flip(x, "tensor", 1)


def across(x):
    return flip(x, "tensor", 2)


def other(x):
    return flip(x, "fsdp", 1)


def plus(*parts):
    return functools.reduce(jnp.add, [p.astype(F32) for p in parts])


def packs_of_whole(qkv, out):
    packs = []
    for j in range(4):
        for cr in range(2):
            pair = []
            for fr in range(2):
                at = fr * 256 + cr * 128
                head = out[j * 128 + cr * 64 : j * 128 + cr * 64 + 64, fr * 256 : fr * 256 + 256]
                pair.append(
                    jnp.concatenate(
                        [qkv[i, at : at + 128, j * 128 : (j + 1) * 128] for i in range(3)]
                        + [head[:, :128], head[:, 128:]]
                    )
                )
            packs.append(jnp.stack(pair))
    return packs


def whole_of_packs(packs):
    qkv, out = jnp.zeros((3, D, D), F32), jnp.zeros((D, D), F32)
    for j in range(4):
        for cr in range(2):
            for fr in range(2):
                pack = packs[2 * j + cr][fr].astype(F32)
                at, hd = fr * 256 + cr * 128, j * 128 + cr * 64
                qkv = qkv.at[:, at : at + 128, j * 128 : (j + 1) * 128].set(pack[:384].reshape(3, 128, 128))
                out = out.at[hd : hd + 64, fr * 256 : fr * 256 + 128].set(pack[384:448])
                out = out.at[hd : hd + 64, fr * 256 + 128 : fr * 256 + 256].set(pack[448:512])
    return qkv, out


def local(
    tokens, gain_one, shift_one, w_qkv, w_attn_out, gain_two, shift_two, w_router, w_in, w_out, routes, cotangent
):
    nf, nh = lax.axis_size("fsdp"), lax.axis_size("heads")
    near = nf == 2 and nh == 4
    f, h, t = lax.axis_index("fsdp"), lax.axis_index("heads"), lax.axis_index("tensor")
    zero = jnp.zeros((), jnp.int32)
    idx = jnp.stack([f if near else zero, t % 2 if near else zero, t, h]).astype(jnp.int32)
    small_own = jnp.concatenate([w_router.T, jnp.stack([gain_one, shift_one, gain_two, shift_two])])

    if near:
        (pack,) = call(pack_kernel, [sds((512, 128), BF)], (idx, w_qkv, w_attn_out))
        pack = jnp.stack([pack, other(pack)])
        small_oth = other(small_own)
        small = jnp.where(
            f == 0, jnp.concatenate([small_own, small_oth], 1), jnp.concatenate([small_oth, small_own], 1)
        )
        packs = []
        for j in range(4):
            mine = flip(pack, "heads", j) if j else pack
            packs += [mine, core(mine)]
        weights = (w_in, other(w_in), w_out, other(w_out))
    else:
        small = lax.all_gather(small_own, "fsdp", axis=1, tiled=True)
        qkv_all = lax.all_gather(lax.all_gather(w_qkv, "fsdp", axis=1, tiled=True), "heads", axis=2, tiled=True)
        out_all = lax.all_gather(lax.all_gather(w_attn_out, "fsdp", axis=1, tiled=True), "heads", axis=0, tiled=True)
        packs = packs_of_whole(qkv_all, out_all)
        in_all = lax.all_gather(w_in, "fsdp", axis=1, tiled=True)
        o_all = lax.all_gather(w_out, "fsdp", axis=2, tiled=True)
        weights = (in_all[:, :256], in_all[:, 256:], o_all[:, :, :256], o_all[:, :, 256:])

    tok, cot0 = call(pad_kernel, [sds((ROWS, D), BF)] * 2, (idx, tokens, cotangent))
    cot1, cot2 = core(cot0), across(cot0)
    cot3 = core(cot2)
    sel = jnp.sum((routes[:, :, None] == jnp.arange(8, dtype=jnp.int32)).astype(F32), 1)
    sel = jnp.pad(sel.reshape(4, 2, SEQ, 8), ((0, 0), (0, 0), (0, PAD - SEQ), (0, 0))).reshape(4, ROWS, 8)

    n1, n2_0, resid, qkv, mix, wq, wo = call(
        attn_fwd_kernel,
        [
            sds((ROWS, D), BF),
            sds((ROWS, D), BF),
            sds((ROWS, D), F32),
            sds((4, ROWS, 384), BF),
            sds((4, ROWS, 128), BF),
            sds((4, D, 384), BF),
            sds((4, 128, D), BF),
        ],
        (idx, tok, small, *packs),
    )
    n2_1, n2_2 = core(n2_0), across(n2_0)
    n2_3 = core(n2_2)

    gin, gout, m0, m1, d0, d1, wr_a = moe(False, idx, (n2_0, n2_1), (cot0, cot1), sel, small, weights, ())
    keep, send, m2, m3, d2, d3, wr_b = moe(True, idx, (n2_2, n2_3), (cot2, cot3), sel, small, weights, (gin, gout))

    d_near, m_near = core(d1), core(m1)
    d_far = across(plus(d2, core(d3)).astype(BF))
    m_far = across(plus(m2, core(m3)).astype(BF))

    outs = call(
        attn_bwd_kernel,
        [sds((2, 512, 128), BF)] * 8 + [sds((SEQ * 2, D), BF), sds((8, D), F32)],
        (idx, d0, d_near, d_far, resid, cot0, tok, small, n1, qkv, mix, wq, wo, wr_a + wr_b),
        [
            pltpu.VMEM((ROWS, 384), BF),
            pltpu.VMEM((D, 384), BF),
            pltpu.VMEM((128, D), BF),
            pltpu.VMEM((ROWS, D), F32),
        ],
    )
    packs, input_grad, sgrad = outs[:8], outs[8], outs[9]
    (output,) = call(out_kernel, [sds((SEQ * 2, D), BF)], (idx, resid, m0, m_near, m_far))

    if near:
        totals = []
        for e in range(EXPERTS):
            part = plus(keep[e], other(send[e])).astype(BF)
            part = plus(part, lax.ppermute(part, "heads", [(0, 1), (3, 2)])).astype(BF)
            part = plus(part, lax.ppermute(part, "heads", [(1, 2), (2, 1)])).astype(BF)
            part = jnp.where((h == 0) | (h == 3), lax.ppermute(part, "heads", [(1, 0), (2, 3)]), part)
            totals.append(part)
        win_grad, wout_grad = finish(idx, jnp.stack(totals))

        halves = [plus(packs[2 * j], core(packs[2 * j + 1])).astype(BF) for j in range(4)]
        sgrad = sgrad + core(sgrad)
        half = plus(halves[0], *[flip(halves[j], "heads", j) for j in range(1, 4)]).astype(BF)
        pieces = [sgrad] + [flip(sgrad, "heads", j) for j in range(1, 4)]
        sgrad = (pieces[0] + pieces[1]) + (pieces[2] + pieces[3])
        half = plus(half[0], other(half[1])).astype(BF)
        sgrad = sgrad + other(sgrad)
        half = plus(half, across(half)).astype(BF)
        sgrad = sgrad + across(sgrad)
        qkv_grad, o_grad = call(
            unpack_kernel, [sds((3, 256, 128), F32), sds((128, 256), F32)], (idx, half, core(half))
        )
        sgrad = lax.dynamic_slice_in_dim(sgrad, f * 256, 256, 1)
    else:
        gin = jnp.concatenate([keep[:, :256], send[:, :256]], 1)
        gout = jnp.concatenate([keep[:, 256:], send[:, 256:]], 1).transpose(0, 2, 1)
        win_grad = lax.psum_scatter(gin, "fsdp", scatter_dimension=1, tiled=True)
        wout_grad = lax.psum_scatter(gout, "fsdp", scatter_dimension=2, tiled=True)
        win_grad = lax.psum(win_grad, "heads").astype(F32)
        wout_grad = lax.psum(wout_grad, "heads").astype(F32)
        qkv_grad, o_grad = whole_of_packs(packs)
        both = ("fsdp", "heads", "tensor")
        qkv_grad = lax.psum_scatter(qkv_grad, "fsdp", scatter_dimension=1, tiled=True)
        qkv_grad = lax.psum_scatter(qkv_grad, "heads", scatter_dimension=2, tiled=True)
        qkv_grad = lax.psum(qkv_grad, "tensor")
        o_grad = lax.psum_scatter(o_grad, "fsdp", scatter_dimension=1, tiled=True)
        o_grad = lax.psum_scatter(o_grad, "heads", scatter_dimension=0, tiled=True)
        o_grad = lax.psum(o_grad, "tensor")
        sgrad = lax.psum(sgrad, both)
        sgrad = lax.dynamic_slice_in_dim(sgrad, f * gain_one.shape[0], gain_one.shape[0], 1)

    return (
        output,
        input_grad,
        sgrad[4],
        sgrad[5],
        qkv_grad,
        o_grad,
        sgrad[6],
        sgrad[7],
        sgrad[0:4].T,
        win_grad,
        wout_grad,
    )


def solution(mesh):
    placed = (
        P(("fsdp", "heads", "tensor"), None),
        P("fsdp"),
        P("fsdp"),
        P(None, "fsdp", "heads"),
        P("heads", "fsdp"),
        P("fsdp"),
        P("fsdp"),
        P("fsdp", None),
        P(None, "fsdp", "tensor"),
        P(None, "tensor", "fsdp"),
        P(("fsdp", "heads"), None),
        P(("fsdp", "heads", "tensor"), None),
    )
    return jax.shard_map(
        local,
        mesh=mesh,
        in_specs=placed,
        out_specs=(
            P(("fsdp", "heads", "tensor"), None),
            P(("fsdp", "heads", "tensor"), None),
            P("fsdp"),
            P("fsdp"),
            P(None, "fsdp", "heads"),
            P("heads", "fsdp"),
            P("fsdp"),
            P("fsdp"),
            P("fsdp", None),
            P(None, "fsdp", "tensor"),
            P(None, "tensor", "fsdp"),
        ),
        check_vma=False,
    )
```

```python
import functools

import jax
import jax.numpy as jnp
from jax import lax
from jax.experimental import pallas as pl
from jax.experimental.pallas import tpu as pltpu
from jax.sharding import PartitionSpec as P

HD = 64
SEQ = 197
PAD = 208
ROWS = 2 * PAD
D = 512
FFT = 512
EXPERTS = 4
BF = jnp.bfloat16
F32 = jnp.float32
PACK = 528
GELU_C = 0.7978845608028654


def nn(a, b):
    return lax.dot_general(a, b, (((1,), (0,)), ((), ())), preferred_element_type=F32)


def nt(a, b):
    return lax.dot_general(a, b, (((1,), (1,)), ((), ())), preferred_element_type=F32)


def tn(a, b):
    return lax.dot_general(a, b, (((0,), (0,)), ((), ())), preferred_element_type=F32)


def params(sem=None, mib=24):
    return pltpu.CompilerParams(vmem_limit_bytes=mib * 1024 * 1024, dimension_semantics=sem)


def smem():
    return pl.BlockSpec(memory_space=pltpu.SMEM)


def vmem():
    return pl.BlockSpec(memory_space=pltpu.VMEM)


def sds(shape, dtype):
    return jax.ShapeDtypeStruct(shape, dtype)


def skip(kernel, n_args, n_after):
    def run(*refs):
        kernel(*refs[:n_args], *refs[n_args + n_after :])

    return run


def call(kernel, outs, args, scratch=(), after=(), mib=24):
    return pl.pallas_call(
        skip(kernel, len(args), len(after)),
        out_shape=outs,
        in_specs=[smem()] + [vmem()] * (len(args) - 1) + [pl.BlockSpec(memory_space=pl.ANY)] * len(after),
        out_specs=[vmem()] * len(outs),
        scratch_shapes=list(scratch),
        compiler_params=params(mib=mib),
    )(*args, *after)


def pack_kernel(idx, wqkv, wo, wr, g1, s1, g2, s2, out):
    c = idx[1]
    rows = pl.ds(pl.multiple_of(c * 128, 128), 128)
    for i in range(3):
        out[i * 128 : (i + 1) * 128, :] = wqkv[i, rows, :]
    head = pl.ds(pl.multiple_of(c * 64, 64), 64)
    out[384:448, :] = wo[head, 0:128]
    out[448:512, :] = wo[head, 128:256]
    small = [wr[...].astype(F32).T] + [r[...].reshape(1, 256).astype(F32) for r in (g1, s1, g2, s2)]
    small = jnp.concatenate(small, axis=0).astype(BF)
    out[512:520, :] = small[:, 0:128]
    out[520:528, :] = small[:, 128:256]


def pair_kernel(idx, own, oth, out):
    out[0] = own[...]
    out[1] = oth[...]


def weights_kernel(idx, win, wout, out):
    for e in range(EXPERTS):
        out[e, 0:256, :] = win[e]
        out[e, 256:512, 0:256] = wout[e, 0:256, :]
        out[e, 256:512, 256:512] = wout[e, 256:512, :]


def spread(v):
    zero = jnp.zeros((PAD - SEQ, v.shape[1]), v.dtype)
    return jnp.concatenate([v[:SEQ], zero, v[SEQ:], zero], axis=0)


def close(v):
    return jnp.concatenate([v[:SEQ], v[PAD : PAD + SEQ]], axis=0)


def pad_kernel(idx, tok, cot, tok_out, cot_out):
    tok_out[...] = spread(tok[...].astype(F32)).astype(BF)
    cot_out[...] = spread(cot[...].astype(F32)).astype(BF)


def norm_parts(x):
    center = jnp.mean(x, -1, keepdims=True)
    centered = x - center
    rstd = lax.rsqrt(jnp.mean(centered * centered, -1, keepdims=True) + 1e-06)
    return centered * rstd, rstd


def norm_back(xhat, rstd, grad, gain):
    dxhat = grad * gain
    m1 = jnp.mean(dxhat, -1, keepdims=True)
    m2 = jnp.mean(dxhat * xhat, -1, keepdims=True)
    return rstd * (dxhat - m1 - xhat * m2)


def attn_fwd_kernel(first, idx, tok, *refs):
    packs, refs = refs[:4], refs[4:]
    if first:
        small, n1_ref, acc_ref, qkv_ref, mix_ref, wq_ref, wo_ref = refs
    else:
        small, n1_ref, acc_in, n2_ref, acc_ref, qkv_ref, mix_ref, wq_ref, wo_ref = refs
    f, c = idx[0], idx[1]
    if first:
        for fr in range(2):
            at = jnp.bitwise_xor(f, fr) * 256
            for i in range(2):
                cols = pl.ds(pl.multiple_of(at + i * 128, 128), 128)
                small[:, cols] = packs[0][fr, 512 + 8 * i : 520 + 8 * i, :]
        x = tok[...].astype(F32)
        xhat, _ = norm_parts(x)
        n1 = (xhat * small[4:5, :].astype(F32) + small[5:6, :].astype(F32)).astype(BF)
        n1_ref[...] = n1
        acc = [x[0:PAD], x[PAD:ROWS]]
    else:
        n1 = n1_ref[...]
        acc = [acc_in[0:PAD, :], acc_in[PAD:ROWS, :]]
    lane = lax.broadcasted_iota(jnp.int32, (PAD, 128), 1)
    key = lax.broadcasted_iota(jnp.int32, (PAD, PAD), 1)
    for j in range(2):
        for fr in range(2):
            fa = jnp.bitwise_xor(f, fr)
            for cr in range(2):
                ca = jnp.bitwise_xor(c, cr)
                src = packs[2 * j + cr]
                rows = pl.ds(pl.multiple_of(fa * 256 + ca * 128, 128), 128)
                for i in range(3):
                    wq_ref[j, rows, i * 128 : (i + 1) * 128] = src[fr, i * 128 : (i + 1) * 128, :]
                head = pl.ds(pl.multiple_of(ca * 64, 64), 64)
                for i in range(2):
                    cols = pl.ds(pl.multiple_of(fa * 256 + i * 128, 128), 128)
                    wo_ref[j, head, cols] = src[fr, 384 + 64 * i : 448 + 64 * i, :]
        qkv_ref[j] = nn(n1, wq_ref[j]).astype(BF)
        for im in range(2):
            r = slice(im * PAD, (im + 1) * PAD)
            q, k, v = (qkv_ref[j, r, i * 128 : (i + 1) * 128] for i in range(3))
            outs = []
            for head in range(2):
                s = nt(jnp.where(lane // HD == head, q, jnp.zeros_like(q)), k) * 0.125
                s = jnp.where(key < SEQ, s, -1e30)
                e = jnp.exp(s - jnp.max(s, -1, keepdims=True))
                p = e / jnp.sum(e, -1, keepdims=True)
                outs.append(nn(p.astype(BF), v))
            mix = jnp.where(lane < HD, outs[0], outs[1]).astype(BF)
            mix_ref[j, r, :] = mix
            acc[im] = acc[im] + nn(mix, wo_ref[j])
    for im in range(2):
        r = slice(im * PAD, (im + 1) * PAD)
        acc_ref[r, :] = acc[im]
        if not first:
            xhat, _ = norm_parts(acc[im])
            n2_ref[r, :] = (xhat * small[6:7, :].astype(F32) + small[7:8, :].astype(F32)).astype(BF)


def attn_bwd_kernel(
    idx, d0, d1, d2, resid, cot, tok, small, n1, qkv_a, qkv_b, mix_a, mix_b, wq_a, wq_b, wo_a, wo_b, wr_a, wr_b, *refs
):
    own, sib, igrad, dqkv_s, gq_s, go_s, dn1_s, sgrad = refs
    f, c = idx[0], idx[1]
    dn2 = d0[...].astype(F32) + d1[...].astype(F32) + d2[...].astype(F32)
    xhat, rstd = norm_parts(resid[...])
    sgrad[0:4, :] = (wr_a[...] + wr_b[...])[0:4]
    sgrad[6:7, :] = jnp.sum(dn2 * xhat, 0, keepdims=True)
    sgrad[7:8, :] = jnp.sum(dn2, 0, keepdims=True)
    dresid = cot[...].astype(F32) + norm_back(xhat, rstd, dn2, small[6:7, :].astype(F32))
    dattn = dresid.astype(BF)
    lane = lax.broadcasted_iota(jnp.int32, (PAD, 128), 1)
    key = lax.broadcasted_iota(jnp.int32, (PAD, PAD), 0)
    n1t = n1[...].T
    for j in range(4):
        qkv, mix, wq, wo = (pair[j // 2].at[j % 2] for pair in ((qkv_a, qkv_b), (mix_a, mix_b), (wq_a, wq_b), (wo_a, wo_b)))
        go_s[...] = tn(mix[...], dattn).astype(BF)
        dmix = nt(dattn, wo[...]).astype(BF)
        for im in range(2):
            r = slice(im * PAD, (im + 1) * PAD)
            q, k, v = (qkv[r, i * 128 : (i + 1) * 128] for i in range(3))
            dm = dmix[r]
            dq, dk, dv = [], [], []
            for head in range(2):
                keep = lane // HD == head
                s = nt(k, jnp.where(keep, q, jnp.zeros_like(q))) * 0.125
                s = jnp.where(key < SEQ, s, -1e30)
                e = jnp.exp(s - jnp.max(s, 0, keepdims=True))
                p = e / jnp.sum(e, 0, keepdims=True)
                dp = nt(v, jnp.where(keep, dm, jnp.zeros_like(dm)))
                ds = (p * (dp - jnp.sum(p * dp, 0, keepdims=True))).astype(BF)
                dq.append(tn(ds, k))
                dk.append(nn(ds, q))
                dv.append(nn(p.astype(BF), dm))
            first = lane < HD
            dqkv_s[r, 0:128] = (jnp.where(first, dq[0], dq[1]) * 0.125).astype(BF)
            dqkv_s[r, 128:256] = (jnp.where(first, dk[0], dk[1]) * 0.125).astype(BF)
            dqkv_s[r, 256:384] = jnp.where(first, dv[0], dv[1]).astype(BF)
        dqkv = dqkv_s[...]
        gq_s[...] = nn(n1t, dqkv).astype(BF)
        part = nt(dqkv, wq[...])
        if j == 0:
            dn1_s[...] = part
        else:
            dn1_s[...] += part
        for fr in range(2):
            fa = jnp.bitwise_xor(f, fr)
            for cr in range(2):
                ca = jnp.bitwise_xor(c, cr)
                dst = (own, sib)[cr]
                rows = pl.ds(pl.multiple_of(fa * 256 + ca * 128, 128), 128)
                for i in range(3):
                    dst[j, fr, i * 128 : (i + 1) * 128, :] = gq_s[rows, i * 128 : (i + 1) * 128]
                head = pl.ds(pl.multiple_of(ca * 64, 64), 64)
                for i in range(2):
                    cols = pl.ds(pl.multiple_of(fa * 256 + i * 128, 128), 128)
                    dst[j, fr, 384 + 64 * i : 448 + 64 * i, :] = go_s[head, cols]
    dn1 = dn1_s[...]
    xhat, rstd = norm_parts(tok[...].astype(F32))
    sgrad[4:5, :] = jnp.sum(dn1 * xhat, 0, keepdims=True)
    sgrad[5:6, :] = jnp.sum(dn1, 0, keepdims=True)
    for fr in range(2):
        for cr in range(2):
            at = jnp.bitwise_xor(f, fr) * 256 + jnp.bitwise_xor(c, cr) * 128
            rows = sgrad[:, pl.ds(pl.multiple_of(at, 128), 128)]
            rows = jnp.concatenate([rows, jnp.zeros_like(rows)], axis=0).astype(BF)
            for j in range(4):
                (own, sib)[cr][j, fr, 512:528, :] = rows
    grad = dresid + norm_back(xhat, rstd, dn1, small[4:5, :].astype(F32))
    igrad[...] = close(grad).astype(BF)


def out_kernel(idx, resid, m0, m1, m2, out):
    total = resid[...] + m0[...].astype(F32) + m1[...].astype(F32) + m2[...].astype(F32)
    out[...] = close(total).astype(BF)


def moe_kernel(start, end, final, base, e0, n, idx, x0, x1, g0, g1, routes, small, w_own, w_oth, *refs):
    take = lambda k: (refs[:k], refs[k:])
    if final:
        (gin_in, gout_in), refs = take(2)
    if not start:
        (mix_in, dn_in, dp_in), refs = take(3)
    if final:
        keeps, refs = take(n)
        sends, refs = take(n)
    else:
        (gin_out, gout_out), refs = take(2)
    if end:
        (mix0, mix1, dn0, dn1, wrg), refs = take(5)
    else:
        (mix_s, dn_s, dprob), refs = take(3)
    (win, wout, xt, gt, gates, router, chosen, gin_s, gout_s), refs = take(9)
    if end:
        mix_s, dn_s, dprob = refs
    step = pl.program_id(0)
    e = step + e0
    f, t = idx[0], idx[2]
    xs, gs = (x0, x1), (g0, g1)
    lane = lax.broadcasted_iota(jnp.int32, (ROWS, 8), 1)

    @pl.when(step == 0)
    def _():
        if start:
            dprob[...] = jnp.zeros_like(dprob)
            mix_s[...] = jnp.zeros_like(mix_s)
            dn_s[...] = jnp.zeros_like(dn_s)
        else:
            dprob[...] = dp_in[...]
            mix_s[...] = mix_in[...]
            dn_s[...] = dn_in[...]
        for b in range(2):
            xt[b] = xs[b][...].T
            gt[b] = gs[b][...].T
            logits = nt(xs[b][...], small[...])
            logits = jnp.where(lane < EXPERTS, logits, -1e30)
            ex = jnp.exp(logits - jnp.max(logits, -1, keepdims=True))
            prob = ex / jnp.sum(ex, -1, keepdims=True)
            router[b] = prob
            named = routes[jnp.bitwise_xor(t, base + b)]
            expert = lax.broadcasted_iota(jnp.int32, (8, ROWS), 0)
            hit = jnp.where((named[0:1] == expert) | (named[1:2] == expert), 1.0, 0.0).T
            chosen[b] = hit
            gates[b] = prob * hit

    own = pl.ds(pl.multiple_of(f * 256, 256), 256)
    oth = pl.ds(pl.multiple_of((1 - f) * 256, 256), 256)
    for w, half in ((w_own, own), (w_oth, oth)):
        win[half, :] = w[0, 0:256, :]
        wout[0:256, half] = w[0, 256:512, 0:256]
        wout[256:512, half] = w[0, 256:512, 256:512]
    gin = gout = None
    for b in range(2):
        inner = nn(xs[b][...], win[...])
        back = nt(gs[b][...], wout[...])
        gate = jnp.sum(jnp.where(lane == e, gates[b], 0.0), -1, keepdims=True)
        square = inner * inner
        th = jnp.tanh(GELU_C * inner * (1.0 + 0.044715 * square))
        half = 0.5 * (1.0 + th)
        hidden = inner * half
        slope = half + 0.5 * inner * (1.0 - th * th) * (GELU_C * (1.0 + (3 * 0.044715) * square))
        dprob[b] += jnp.where(lane == e, jnp.sum(hidden * back, -1, keepdims=True), 0.0)
        hg = (gate * hidden).astype(BF)
        di = (gate * back * slope).astype(BF)
        mix_s[b] += nn(hg, wout[...])
        dn_s[b] += nt(di, win[...])
        part_in, part_out = nn(xt[b], di), nn(gt[b], hg)
        gin = part_in if gin is None else gin + part_in
        gout = part_out if gout is None else gout + part_out
    if final:
        gin_s[...] = (gin + gin_in[0]).astype(BF)
        gout_s[...] = (gout + gout_in[0]).astype(BF)
        for i in range(n):

            @pl.when(step == i)
            def _():
                for dst, rows in ((keeps[i], own), (sends[i], oth)):
                    dst[0:256, :] = gin_s[rows, :]
                    dst[256:512, :] = gout_s[rows, :]
    else:
        gin_out[0] = gin
        gout_out[0] = gout
    if end:

        @pl.when(step == n - 1)
        def _():
            for b, dn, mx in ((0, dn0, mix0), (1, dn1, mix1)):
                dp = dprob[b] * chosen[b]
                dl = router[b] * (dp - jnp.sum(router[b] * dp, -1, keepdims=True))
                dl = jnp.where(lane < EXPERTS, dl, 0.0).astype(BF)
                dn[...] = (dn_s[b] + nn(dl, small[...])).astype(BF)
                mx[...] = mix_s[b].astype(BF)
                part = tn(dl, xs[b][...])
                if b == 0:
                    wrg[...] = part
                else:
                    wrg[...] += part


def moe(base, e0, n, idx, xs, gs, routes, small, weights, grads=(), sums=(), end=True, after=()):
    start, final = not sums, bool(grads)
    whole = lambda shape: pl.BlockSpec(shape, lambda e: (0,) * len(shape))
    expert = lambda at: pl.BlockSpec((1, 512, 512), lambda e: (e + at, 0, 0))
    row, both = whole((ROWS, D)), whole((2, ROWS, D))
    carry = [(2, ROWS, D), (2, ROWS, D), (2, ROWS, 8)]
    in_specs = [smem(), row, row, row, row, whole((4, 2, ROWS)), whole((8, D))] + [expert(e0)] * 2
    in_specs += [expert(e0)] * len(grads) + [whole(shape) for shape in carry[: len(sums)]]
    in_specs += [pl.BlockSpec(memory_space=pl.ANY)] * len(after)
    if final:
        outs, out_specs = [sds((512, 512), BF)] * (2 * n), [whole((512, 512))] * (2 * n)
    else:
        outs, out_specs = [sds((n, D, FFT), F32)] * 2, [expert(0)] * 2
    if end:
        outs += [sds((ROWS, D), BF)] * 4 + [sds((8, D), F32)]
        out_specs += [row] * 4 + [whole((8, D))]
    else:
        outs += [sds(shape, F32) for shape in carry]
        out_specs += [whole(shape) for shape in carry]
    scratch = [
        pltpu.VMEM((D, FFT), BF),
        pltpu.VMEM((FFT, D), BF),
        pltpu.VMEM((2, D, ROWS), BF),
        pltpu.VMEM((2, D, ROWS), BF),
        pltpu.VMEM((2, ROWS, 8), F32),
        pltpu.VMEM((2, ROWS, 8), F32),
        pltpu.VMEM((2, ROWS, 8), F32),
        pltpu.VMEM((D, FFT), BF),
        pltpu.VMEM((D, FFT), BF),
    ]
    if end:
        scratch += [pltpu.VMEM(shape, F32) for shape in carry]
    kernel = functools.partial(moe_kernel, start, end, final, base, e0, n)
    n_in = 9 + len(grads) + len(sums)
    return pl.pallas_call(
        skip(kernel, n_in, len(after)),
        grid=(n,),
        out_shape=outs,
        in_specs=in_specs,
        out_specs=out_specs,
        scratch_shapes=scratch,
        compiler_params=params(("arbitrary",), 44),
    )(idx, *xs, *gs, routes, small, *weights, *grads, *sums, *after)


def add_kernel(idx, a, b, out):
    out[...] = (a[...].astype(F32) + b[...].astype(F32)).astype(BF)


def add(idx, a, b, after=()):
    return call(add_kernel, [sds(a.shape, BF)], (idx, a, b), after=after)[0]


def finish_kernel(idx, mine, given, *refs):
    win_grad, wout_grad = refs[-2:]
    ends = (idx[3] == 0) | (idx[3] == 3)
    total = jnp.where(ends, given[...], mine[...]).astype(F32)
    win_grad[0] = total[0:256, :]
    wout_grad[0] = total[256:512, :].T


def finish(idx, e, mine, given, into=(), after=()):
    block = lambda shape: pl.BlockSpec((1,) + shape, lambda i: (e, 0, 0))
    anywhere = [pl.BlockSpec(memory_space=pl.ANY)]
    return pl.pallas_call(
        skip(finish_kernel, 3, len(into) + len(after)),
        grid=(1,),
        out_shape=[sds((EXPERTS, 256, FFT), F32), sds((EXPERTS, FFT, 256), F32)],
        in_specs=[smem(), vmem(), vmem()] + anywhere * (len(into) + len(after)),
        out_specs=[block((256, FFT)), block((FFT, 256))],
        input_output_aliases={3: 0, 4: 1} if into else {},
        compiler_params=params(),
    )(idx, mine, given, *into, *after)


def merge_kernel(idx, own, sib, *outs):
    for j in range(4):
        outs[j][...] = (own[j].astype(F32) + sib[j].astype(F32)).astype(BF)


def gather_kernel(idx, a, b, c, d, keep, send):
    total = ((a[...].astype(F32) + b[...].astype(F32)) + (c[...].astype(F32) + d[...].astype(F32))).astype(BF)
    keep[...] = total[0]
    send[...] = total[1]


def unpack_kernel(idx, own, sib, qkv_grad, o_grad, sgrad):
    c = idx[1]
    for src, ca in ((own, c), (sib, 1 - c)):
        rows = pl.ds(pl.multiple_of(ca * 128, 128), 128)
        for i in range(3):
            qkv_grad[i, rows, :] = src[i * 128 : (i + 1) * 128, :].astype(F32)
        head = pl.ds(pl.multiple_of(ca * 64, 64), 64)
        o_grad[head, 0:128] = src[384:448, :].astype(F32)
        o_grad[head, 128:256] = src[448:512, :].astype(F32)
        sgrad[:, rows] = src[512:520, :].astype(F32)


def flip(x, axis, bit):
    n = lax.axis_size(axis)
    return lax.ppermute(x, axis, [(i, i ^ bit) for i in range(n)])


def core(x):
    return flip(x, "tensor", 1)


def across(x):
    return flip(x, "tensor", 2)


def other(x):
    return flip(x, "fsdp", 1)


def packs_of_whole(qkv, out, small):
    packs = []
    for j in range(4):
        for cr in range(2):
            pair = []
            for fr in range(2):
                at = fr * 256 + cr * 128
                head = out[j * 128 + cr * 64 : j * 128 + cr * 64 + 64, fr * 256 : fr * 256 + 256]
                pair.append(
                    jnp.concatenate(
                        [qkv[i, at : at + 128, j * 128 : (j + 1) * 128] for i in range(3)]
                        + [head[:, :128], head[:, 128:]]
                        + [small[:, fr * 256 : fr * 256 + 128], small[:, fr * 256 + 128 : fr * 256 + 256]]
                    )
                )
            packs.append(jnp.stack(pair))
    return packs


def whole_of_packs(packs):
    qkv, out, small = jnp.zeros((3, D, D), F32), jnp.zeros((D, D), F32), jnp.zeros((8, D), F32)
    for j in range(4):
        for cr in range(2):
            for fr in range(2):
                pack = packs[cr][j, fr].astype(F32)
                at, hd = fr * 256 + cr * 128, j * 128 + cr * 64
                qkv = qkv.at[:, at : at + 128, j * 128 : (j + 1) * 128].set(pack[:384].reshape(3, 128, 128))
                out = out.at[hd : hd + 64, fr * 256 : fr * 256 + 128].set(pack[384:448])
                out = out.at[hd : hd + 64, fr * 256 + 128 : fr * 256 + 256].set(pack[448:512])
                small = small.at[:, at : at + 128].set(pack[512:520])
    return qkv, out, small


def local(
    tokens, gain_one, shift_one, w_qkv, w_attn_out, gain_two, shift_two, w_router, w_in, w_out, routes, cotangent
):
    nf, nh = lax.axis_size("fsdp"), lax.axis_size("heads")
    near = nf == 2 and nh == 4
    f, h, t = lax.axis_index("fsdp"), lax.axis_index("heads"), lax.axis_index("tensor")
    zero = jnp.zeros((), jnp.int32)
    idx = jnp.stack([f if near else zero, t % 2 if near else zero, t, h]).astype(jnp.int32)
    shapes = lambda *given: [sds(shape, dtype) for shape, dtype in given]

    if near:
        (pack,) = call(
            pack_kernel,
            [sds((PACK, 128), BF)],
            (idx, w_qkv, w_attn_out, w_router, gain_one, shift_one, gain_two, shift_two),
        )
        pack_far = other(pack)
        (w_own,) = call(weights_kernel, [sds((EXPERTS, 512, 512), BF)], (idx, w_in, w_out), after=(pack,))
        w_oth = other(w_own)
        tok, cot0 = call(pad_kernel, [sds((ROWS, D), BF)] * 2, (idx, tokens, cotangent), after=(w_own,))
        (pair,) = call(pair_kernel, [sds((2, PACK, 128), BF)], (idx, pack, pack_far), after=(tok,))
        packs = []
        for j in range(4):
            mine = flip(pair, "heads", j) if j else pair
            packs += [mine, core(mine)]
    else:
        small_own = jnp.concatenate([w_router.T, jnp.stack([gain_one, shift_one, gain_two, shift_two])])
        small = lax.all_gather(small_own, "fsdp", axis=1, tiled=True)
        qkv_all = lax.all_gather(lax.all_gather(w_qkv, "fsdp", axis=1, tiled=True), "heads", axis=2, tiled=True)
        out_all = lax.all_gather(lax.all_gather(w_attn_out, "fsdp", axis=1, tiled=True), "heads", axis=0, tiled=True)
        packs = packs_of_whole(qkv_all, out_all, small)
        in_all = lax.all_gather(w_in, "fsdp", axis=1, tiled=True)
        o_all = lax.all_gather(w_out, "fsdp", axis=2, tiled=True)
        (w_own,) = call(weights_kernel, [sds((EXPERTS, 512, 512), BF)], (idx, in_all[:, :256], o_all[:, :, :256]))
        (w_oth,) = call(weights_kernel, [sds((EXPERTS, 512, 512), BF)], (idx, in_all[:, 256:], o_all[:, :, 256:]))
        tok, cot0 = call(pad_kernel, [sds((ROWS, D), BF)] * 2, (idx, tokens, cotangent))

    named = jnp.pad(routes.T.reshape(2, 8, SEQ), ((0, 0), (0, 0), (0, PAD - SEQ)), constant_values=-1)
    named = named.reshape(2, 4, ROWS).transpose(1, 0, 2)

    kept = [((2, ROWS, 384), BF), ((2, ROWS, 128), BF), ((2, D, 384), BF), ((2, 128, D), BF)]
    small, n1, acc, qkv_a, mix_a, wq_a, wo_a = call(
        functools.partial(attn_fwd_kernel, True),
        shapes(((8, D), BF), ((ROWS, D), BF), ((ROWS, D), F32), *kept),
        (idx, tok, *packs[:4]),
    )
    cot1, cot2 = core(cot0), across(cot0)
    cot3 = core(cot2)
    n2_0, resid, qkv_b, mix_b, wq_b, wo_b = call(
        functools.partial(attn_fwd_kernel, False),
        shapes(((ROWS, D), BF), ((ROWS, D), F32), *kept),
        (idx, tok, *packs[4:], small, n1, acc),
    )
    n2_1, n2_2 = core(n2_0), across(n2_0)
    n2_3 = core(n2_2)

    shared = (named, small, (w_own, w_oth))
    gin, gout, m0, m1, d0, d1, wr_a = moe(0, 0, EXPERTS, idx, (n2_0, n2_1), (cot0, cot1), *shared)
    far = ((n2_2, n2_3), (cot2, cot3))
    keep0, send0, *sums = moe(2, 0, 1, idx, *far, *shared, grads=(gin, gout), end=False)
    outs = moe(2, 1, 3, idx, *far, *shared, grads=(gin, gout), sums=tuple(sums))
    keeps, sends = [keep0, *outs[0:3]], [send0, *outs[3:6]]
    m2, m3, d2, d3, wr_b = outs[6:]

    d_near = core(d1)
    d_sum = add(idx, d2, core(d3))
    d_far = across(d_sum)
    if near:
        got = [other(send) for send in sends]
        inward = lambda x: lax.ppermute(x, "heads", [(0, 1), (3, 2)])
        middle = lambda x: lax.ppermute(x, "heads", [(1, 2), (2, 1)])
        outward = lambda x: lax.ppermute(x, "heads", [(1, 0), (2, 3)])
        ones, twos, threes = [None] * 4, [None] * 4, [None] * 4
        ones[0] = add(idx, keeps[0], got[0], after=(d_sum,))
        m_near = core(m1)
        m_sum = add(idx, m2, core(m3), after=(ones[0],))
        m_far = across(m_sum)
        ones[1] = add(idx, keeps[1], got[1], after=(m_sum,))
        twos[0] = add(idx, ones[0], inward(ones[0]), after=(ones[1],))
        before = (twos[0],)
    else:
        m_near = core(m1)
        m_far = across(add(idx, m2, core(m3)))
        before = ()

    own, sib, input_grad = call(
        attn_bwd_kernel,
        shapes(((4, 2, PACK, 128), BF), ((4, 2, PACK, 128), BF), ((SEQ * 2, D), BF)),
        (idx, d0, d_near, d_far, resid, cot0, tok, small, n1)
        + (qkv_a, qkv_b, mix_a, mix_b, wq_a, wq_b, wo_a, wo_b, wr_a, wr_b),
        [
            pltpu.VMEM((ROWS, 384), BF),
            pltpu.VMEM((D, 384), BF),
            pltpu.VMEM((128, D), BF),
            pltpu.VMEM((ROWS, D), F32),
            pltpu.VMEM((8, D), F32),
        ],
        after=before,
        mib=32,
    )

    if near:
        sib = core(sib)
        ones[2] = add(idx, keeps[2], got[2], after=(input_grad,))
        twos[1] = add(idx, ones[1], inward(ones[1]), after=(ones[2],))
        halves = call(merge_kernel, [sds((2, PACK, 128), BF)] * 4, (idx, own, sib), after=(twos[1],))
        halves = [halves[0]] + [flip(halves[j], "heads", j) for j in range(1, 4)]
        threes[0] = add(idx, twos[0], middle(twos[0]), after=(halves[0],))
        ones[3] = add(idx, keeps[3], got[3], after=(threes[0],))
        (output,) = call(
            out_kernel, [sds((SEQ * 2, D), BF)], (idx, resid, m0, m_near, m_far), after=(ones[3],)
        )
        twos[2] = add(idx, ones[2], inward(ones[2]), after=(output,))
        threes[1] = add(idx, twos[1], middle(twos[1]), after=(twos[2],))
        grads = finish(idx, 0, threes[0], outward(threes[0]), after=(threes[1],))
        twos[3] = add(idx, ones[3], inward(ones[3]), after=(grads[0],))
        half, send = call(gather_kernel, [sds((PACK, 128), BF)] * 2, (idx, *halves), after=(twos[3],))
        threes[2] = add(idx, twos[2], middle(twos[2]), after=(half,))
        half = add(idx, half, other(send), after=(threes[2],))
        grads = finish(idx, 1, threes[1], outward(threes[1]), grads, after=(half,))
        half = add(idx, half, across(half), after=(grads[0],))
        threes[3] = add(idx, twos[3], middle(twos[3]), after=(half,))
        grads = finish(idx, 2, threes[2], outward(threes[2]), grads, after=(threes[3],))
        qkv_grad, o_grad, sgrad = call(
            unpack_kernel,
            shapes(((3, 256, 128), F32), ((128, 256), F32), ((8, 256), F32)),
            (idx, half, core(half)),
            after=(grads[0],),
        )
        win_grad, wout_grad = finish(idx, 3, threes[3], outward(threes[3]), grads, after=(sgrad,))
    else:
        (output,) = call(out_kernel, [sds((SEQ * 2, D), BF)], (idx, resid, m0, m_near, m_far))
        keep, send = jnp.stack(keeps), jnp.stack(sends)
        gin = jnp.concatenate([keep[:, :256], send[:, :256]], 1)
        gout = jnp.concatenate([keep[:, 256:], send[:, 256:]], 1).transpose(0, 2, 1)
        win_grad = lax.psum_scatter(gin, "fsdp", scatter_dimension=1, tiled=True)
        wout_grad = lax.psum_scatter(gout, "fsdp", scatter_dimension=2, tiled=True)
        win_grad = lax.psum(win_grad, "heads").astype(F32)
        wout_grad = lax.psum(wout_grad, "heads").astype(F32)
        qkv_grad, o_grad, sgrad = whole_of_packs((own, sib))
        qkv_grad = lax.psum_scatter(qkv_grad, "fsdp", scatter_dimension=1, tiled=True)
        qkv_grad = lax.psum_scatter(qkv_grad, "heads", scatter_dimension=2, tiled=True)
        qkv_grad = lax.psum(qkv_grad, "tensor")
        o_grad = lax.psum_scatter(o_grad, "fsdp", scatter_dimension=1, tiled=True)
        o_grad = lax.psum_scatter(o_grad, "heads", scatter_dimension=0, tiled=True)
        o_grad = lax.psum(o_grad, "tensor")
        sgrad = lax.psum(sgrad, ("fsdp", "heads", "tensor"))
        sgrad = lax.dynamic_slice_in_dim(sgrad, f * gain_one.shape[0], gain_one.shape[0], 1)

    return (
        output,
        input_grad,
        sgrad[4],
        sgrad[5],
        qkv_grad,
        o_grad,
        sgrad[6],
        sgrad[7],
        sgrad[0:4].T,
        win_grad,
        wout_grad,
    )


def solution(mesh):
    placed = (
        P(("fsdp", "heads", "tensor"), None),
        P("fsdp"),
        P("fsdp"),
        P(None, "fsdp", "heads"),
        P("heads", "fsdp"),
        P("fsdp"),
        P("fsdp"),
        P("fsdp", None),
        P(None, "fsdp", "tensor"),
        P(None, "tensor", "fsdp"),
        P(("fsdp", "heads"), None),
        P(("fsdp", "heads", "tensor"), None),
    )
    return jax.shard_map(
        local,
        mesh=mesh,
        in_specs=placed,
        out_specs=(
            P(("fsdp", "heads", "tensor"), None),
            P(("fsdp", "heads", "tensor"), None),
            P("fsdp"),
            P("fsdp"),
            P(None, "fsdp", "heads"),
            P("heads", "fsdp"),
            P("fsdp"),
            P("fsdp"),
            P("fsdp", None),
            P(None, "fsdp", "tensor"),
            P(None, "tensor", "fsdp"),
        ),
        check_vma=False,
    )
```

```python
import functools

import jax
import jax.numpy as jnp
from jax import lax
from jax.experimental import pallas as pl
from jax.experimental.pallas import tpu as pltpu
from jax.sharding import PartitionSpec as P

HD = 64
SEQ = 197
PAD = 208
ROWS = 2 * PAD
D = 512
FFT = 512
EXPERTS = 4
BF = jnp.bfloat16
F32 = jnp.float32
PACK = 528
GELU_C = 0.7978845608028654


def nn(a, b):
    return lax.dot_general(a, b, (((1,), (0,)), ((), ())), preferred_element_type=F32)


def nt(a, b):
    return lax.dot_general(a, b, (((1,), (1,)), ((), ())), preferred_element_type=F32)


def tn(a, b):
    return lax.dot_general(a, b, (((0,), (0,)), ((), ())), preferred_element_type=F32)


def params(sem=None, mib=24):
    return pltpu.CompilerParams(vmem_limit_bytes=mib * 1024 * 1024, dimension_semantics=sem)


def smem():
    return pl.BlockSpec(memory_space=pltpu.SMEM)


def vmem():
    return pl.BlockSpec(memory_space=pltpu.VMEM)


def sds(shape, dtype):
    return jax.ShapeDtypeStruct(shape, dtype)


def held(*shape, dtype=BF):
    return pltpu.VMEM(shape, dtype)


def skip(kernel, n_args, n_after):
    def run(*refs):
        kernel(*refs[:n_args], *refs[n_args + n_after :])

    return run


def call(kernel, outs, args, scratch=(), after=(), mib=16, fetch=False):
    spec = (lambda x: pl.BlockSpec(x.shape, lambda i: (0,) * len(x.shape))) if fetch else (lambda x: vmem())
    return pl.pallas_call(
        skip(kernel, len(args), len(after)),
        grid=(1,) if fetch else (),
        out_shape=outs,
        in_specs=[smem()] + [spec(x) for x in args[1:]] + [pl.BlockSpec(memory_space=pl.ANY)] * len(after),
        out_specs=[spec(x) for x in outs],
        scratch_shapes=list(scratch),
        compiler_params=params(mib=mib),
    )(*args, *after)


def pack_kernel(idx, wqkv, wo, wr, g1, s1, g2, s2, out):
    c = idx[1]
    rows = pl.ds(pl.multiple_of(c * 128, 128), 128)
    for i in range(3):
        out[i * 128 : (i + 1) * 128, :] = wqkv[i, rows, :]
    head = pl.ds(pl.multiple_of(c * 64, 64), 64)
    out[384:448, :] = wo[head, 0:128]
    out[448:512, :] = wo[head, 128:256]
    small = [wr[...].astype(F32).T] + [r[...].reshape(1, 256).astype(F32) for r in (g1, s1, g2, s2)]
    small = jnp.concatenate(small, axis=0).astype(BF)
    out[512:520, :] = small[:, 0:128]
    out[520:528, :] = small[:, 128:256]


def pair_kernel(idx, own, oth, out):
    out[0] = own[...]
    out[1] = oth[...]


def weights_kernel(idx, win, wout, out):
    out[0:256, :] = win[0]
    out[256:512, 0:256] = wout[0, 0:256, :]
    out[256:512, 256:512] = wout[0, 256:512, :]


def packed_weights(idx, e, w_in, w_out, after=()):
    return pl.pallas_call(
        skip(weights_kernel, 3, len(after)),
        grid=(1,),
        out_shape=held(512, 512),
        in_specs=[smem(), pl.BlockSpec((1, 256, 512), lambda i: (e, 0, 0)), pl.BlockSpec((1, 512, 256), lambda i: (e, 0, 0))]
        + [pl.BlockSpec(memory_space=pl.ANY)] * len(after),
        out_specs=vmem(),
        compiler_params=params(mib=8),
    )(idx, w_in, w_out, *after)


def spread(v):
    zero = jnp.zeros((PAD - SEQ, v.shape[1]), v.dtype)
    return jnp.concatenate([v[:SEQ], zero, v[SEQ:], zero], axis=0)


def close(v):
    return jnp.concatenate([v[:SEQ], v[PAD : PAD + SEQ]], axis=0)


def pad_kernel(idx, rows, out):
    out[...] = spread(rows[...].astype(F32)).astype(BF)


def norm_parts(x):
    center = jnp.mean(x, -1, keepdims=True)
    centered = x - center
    rstd = lax.rsqrt(jnp.mean(centered * centered, -1, keepdims=True) + 1e-06)
    return centered * rstd, rstd


def norm_back(xhat, rstd, grad, gain):
    dxhat = grad * gain
    m1 = jnp.mean(dxhat, -1, keepdims=True)
    m2 = jnp.mean(dxhat * xhat, -1, keepdims=True)
    return rstd * (dxhat - m1 - xhat * m2)


def attn_fwd_kernel(first, idx, tok, *refs):
    packs, refs = (refs[0:2], refs[2:4]), refs[4:]
    if first:
        small, n1_ref, acc_ref, qkv_ref, mix_ref, wq_ref, wo_ref = refs
    else:
        small, n1_ref, acc_in, n2_ref, acc_ref, qkv_ref, mix_ref, wq_ref, wo_ref = refs
    f, c = idx[0], idx[1]
    if first:
        for fr in range(2):
            at = jnp.bitwise_xor(f, fr) * 256
            for i in range(2):
                cols = pl.ds(pl.multiple_of(at + i * 128, 128), 128)
                small[:, cols] = packs[0][fr][0, 512 + 8 * i : 520 + 8 * i, :]
        x = tok[...].astype(F32)
        xhat, _ = norm_parts(x)
        n1 = (xhat * small[4:5, :].astype(F32) + small[5:6, :].astype(F32)).astype(BF)
        n1_ref[...] = n1
        acc = [x[0:PAD], x[PAD:ROWS]]
    else:
        n1 = n1_ref[...]
        acc = [acc_in[0:PAD, :], acc_in[PAD:ROWS, :]]
    lane = lax.broadcasted_iota(jnp.int32, (PAD, 128), 1)
    key = lax.broadcasted_iota(jnp.int32, (PAD, PAD), 1)
    for j in range(2):
        for fr in range(2):
            fa = jnp.bitwise_xor(f, fr)
            for cr in range(2):
                ca = jnp.bitwise_xor(c, cr)
                src = packs[cr][fr]
                rows = pl.ds(pl.multiple_of(fa * 256 + ca * 128, 128), 128)
                for i in range(3):
                    wq_ref[j, rows, i * 128 : (i + 1) * 128] = src[j, i * 128 : (i + 1) * 128, :]
                head = pl.ds(pl.multiple_of(ca * 64, 64), 64)
                for i in range(2):
                    cols = pl.ds(pl.multiple_of(fa * 256 + i * 128, 128), 128)
                    wo_ref[j, head, cols] = src[j, 384 + 64 * i : 448 + 64 * i, :]
        qkv_ref[j] = nn(n1, wq_ref[j]).astype(BF)
        for im in range(2):
            r = slice(im * PAD, (im + 1) * PAD)
            q, k, v = (qkv_ref[j, r, i * 128 : (i + 1) * 128] for i in range(3))
            outs = []
            for head in range(2):
                s = nt(jnp.where(lane // HD == head, q, jnp.zeros_like(q)), k) * 0.125
                s = jnp.where(key < SEQ, s, -1e30)
                e = jnp.exp(s - jnp.max(s, -1, keepdims=True))
                p = e / jnp.sum(e, -1, keepdims=True)
                outs.append(nn(p.astype(BF), v))
            mix = jnp.where(lane < HD, outs[0], outs[1]).astype(BF)
            mix_ref[j, r, :] = mix
            acc[im] = acc[im] + nn(mix, wo_ref[j])
    for im in range(2):
        r = slice(im * PAD, (im + 1) * PAD)
        acc_ref[r, :] = acc[im]
        if not first:
            xhat, _ = norm_parts(acc[im])
            n2_ref[r, :] = (xhat * small[6:7, :].astype(F32) + small[7:8, :].astype(F32)).astype(BF)


def attn_bwd_kernel(first, idx, *refs):
    take = lambda k: (refs[:k], refs[k:])
    if first:
        (d0, d1, d2, resid, cot, wr_a, wr_b, small), refs = take(8)
    else:
        (dresid_in, sgrad_in, dn1_in, tok, small), refs = take(5)
    (n1, qkvs, mixes, wqs, wos, own, sib), refs = take(7)
    if first:
        dresid_out, sgrad, dn1_out, dqkv_s, gq_s, go_s = refs
    else:
        igrad, dqkv_s, gq_s, go_s, sgrad = refs
    f, c = idx[0], idx[1]
    if first:
        dn2 = d0[...].astype(F32) + d1[...].astype(F32) + d2[...].astype(F32)
        xhat, rstd = norm_parts(resid[...])
        sgrad[0:4, :] = (wr_a[...] + wr_b[...])[0:4]
        sgrad[4:6, :] = jnp.zeros((2, D), F32)
        sgrad[6:7, :] = jnp.sum(dn2 * xhat, 0, keepdims=True)
        sgrad[7:8, :] = jnp.sum(dn2, 0, keepdims=True)
        dresid = cot[...].astype(F32) + norm_back(xhat, rstd, dn2, small[6:7, :].astype(F32))
        dresid_out[...] = dresid
    else:
        dresid = dresid_in[...]
    dattn = dresid.astype(BF)
    lane = lax.broadcasted_iota(jnp.int32, (PAD, 128), 1)
    key = lax.broadcasted_iota(jnp.int32, (PAD, PAD), 0)
    n1t = n1[...].T
    dn1 = None if first else dn1_in[...]
    for j in range(2):
        qkv, mix, wq, wo = (ref.at[j] for ref in (qkvs, mixes, wqs, wos))
        go_s[...] = tn(mix[...], dattn).astype(BF)
        dmix = nt(dattn, wo[...]).astype(BF)
        for im in range(2):
            r = slice(im * PAD, (im + 1) * PAD)
            q, k, v = (qkv[r, i * 128 : (i + 1) * 128] for i in range(3))
            dm = dmix[r]
            dq, dk, dv = [], [], []
            for head in range(2):
                keep = lane // HD == head
                s = nt(k, jnp.where(keep, q, jnp.zeros_like(q))) * 0.125
                s = jnp.where(key < SEQ, s, -1e30)
                e = jnp.exp(s - jnp.max(s, 0, keepdims=True))
                p = e / jnp.sum(e, 0, keepdims=True)
                dp = nt(v, jnp.where(keep, dm, jnp.zeros_like(dm)))
                ds = (p * (dp - jnp.sum(p * dp, 0, keepdims=True))).astype(BF)
                dq.append(tn(ds, k))
                dk.append(nn(ds, q))
                dv.append(nn(p.astype(BF), dm))
            near = lane < HD
            dqkv_s[r, 0:128] = (jnp.where(near, dq[0], dq[1]) * 0.125).astype(BF)
            dqkv_s[r, 128:256] = (jnp.where(near, dk[0], dk[1]) * 0.125).astype(BF)
            dqkv_s[r, 256:384] = jnp.where(near, dv[0], dv[1]).astype(BF)
        dqkv = dqkv_s[...]
        gq_s[...] = nn(n1t, dqkv).astype(BF)
        part = nt(dqkv, wq[...])
        dn1 = part if dn1 is None else dn1 + part
        for fr in range(2):
            fa = jnp.bitwise_xor(f, fr)
            for cr in range(2):
                ca = jnp.bitwise_xor(c, cr)
                dst = (own, sib)[cr]
                rows = pl.ds(pl.multiple_of(fa * 256 + ca * 128, 128), 128)
                for i in range(3):
                    dst[j, fr, i * 128 : (i + 1) * 128, :] = gq_s[rows, i * 128 : (i + 1) * 128]
                head = pl.ds(pl.multiple_of(ca * 64, 64), 64)
                for i in range(2):
                    cols = pl.ds(pl.multiple_of(fa * 256 + i * 128, 128), 128)
                    dst[j, fr, 384 + 64 * i : 448 + 64 * i, :] = go_s[head, cols]
    if first:
        dn1_out[...] = dn1
        for ref in (own, sib):
            for j in range(2):
                for fr in range(2):
                    ref[j, fr, 512:528, :] = jnp.zeros((16, 128), BF)
        return
    xhat, rstd = norm_parts(tok[...].astype(F32))
    sgrad[...] = sgrad_in[...]
    sgrad[4:5, :] = jnp.sum(dn1 * xhat, 0, keepdims=True)
    sgrad[5:6, :] = jnp.sum(dn1, 0, keepdims=True)
    for fr in range(2):
        for cr in range(2):
            at = jnp.bitwise_xor(f, fr) * 256 + jnp.bitwise_xor(c, cr) * 128
            rows = sgrad[:, pl.ds(pl.multiple_of(at, 128), 128)]
            rows = jnp.concatenate([rows, jnp.zeros_like(rows)], axis=0).astype(BF)
            for j in range(2):
                (own, sib)[cr][j, fr, 512:528, :] = rows
    grad = dresid + norm_back(xhat, rstd, dn1, small[4:5, :].astype(F32))
    igrad[...] = close(grad).astype(BF)


def out_kernel(idx, resid, m0, m1, m2, out):
    total = resid[...] + m0[...].astype(F32) + m1[...].astype(F32) + m2[...].astype(F32)
    out[...] = close(total).astype(BF)


def moe_kernel(start, end, fresh, e, base, idx, x0, x1, g0, g1, w_own, w_oth, *refs):
    take = lambda k: (refs[:k], refs[k:])
    if start:
        (routes, small), refs = take(2)
    else:
        (xt, gt, gating, mix_in, dn_in, dp_in), refs = take(6)
    if end:
        (small,), refs = take(1)
    if not fresh:
        (gin_in, gout_in), refs = take(2)
    if start:
        (xt, gt, gating), refs = take(3)
    if end:
        (dn0, dn1, mix0, mix1, wrg), refs = take(5)
    else:
        (mix, dn, dprob), refs = take(3)
    (out_a, out_b), (win, wout, hg_s, di_s) = refs[:2], refs[2:]
    f, t = idx[0], idx[2]
    xs, gs = (x0, x1), (g0, g1)
    lane = lax.broadcasted_iota(jnp.int32, (ROWS, 8), 1)
    if start:
        for b in range(2):
            xt[b] = xs[b][...].T
            gt[b] = gs[b][...].T
            logits = jnp.where(lane < EXPERTS, nt(xs[b][...], small[...]), -1e30)
            ex = jnp.exp(logits - jnp.max(logits, -1, keepdims=True))
            named = routes[jnp.bitwise_xor(t, base + b)]
            expert = lax.broadcasted_iota(jnp.int32, (8, ROWS), 0)
            gating[b, :, 0:8] = ex / jnp.sum(ex, -1, keepdims=True)
            gating[b, :, 8:16] = jnp.where((named[0:1] == expert) | (named[1:2] == expert), 1.0, 0.0).T
    own = pl.ds(pl.multiple_of(f * 256, 256), 256)
    oth = pl.ds(pl.multiple_of((1 - f) * 256, 256), 256)
    for w, half in ((w_own, own), (w_oth, oth)):
        win[half, :] = w[0:256, :]
        wout[0:256, half] = w[256:512, 0:256]
        wout[256:512, half] = w[256:512, 256:512]
    for b in range(2):
        inner = nn(xs[b][...], win[...])
        back = nt(gs[b][...], wout[...])
        gate = gating[b, :, e : e + 1] * gating[b, :, 8 + e : 9 + e]
        square = inner * inner
        th = jnp.tanh(inner * (square * (GELU_C * 0.044715) + GELU_C))
        half = th * 0.5 + 0.5
        hidden = inner * half
        slope = half * ((1.0 - half) * (inner * (square * (6 * GELU_C * 0.044715) + 2 * GELU_C)) + 1.0)
        dp = jnp.where(lane == e, jnp.sum(hidden * back, -1, keepdims=True), 0.0)
        hg = (gate * hidden).astype(BF)
        di = ((gate * back) * slope).astype(BF)
        hg_s[b] = hg
        di_s[b] = di
        mx, dx = nn(hg, wout[...]), nt(di, win[...])
        if not start:
            dp, mx, dx = dp + dp_in[b], mx + mix_in[b], dx + dn_in[b]
        if end:
            router = gating[b, :, 0:8]
            dp = dp * gating[b, :, 8:16]
            dl = router * (dp - jnp.sum(router * dp, -1, keepdims=True))
            dl = jnp.where(lane < EXPERTS, dl, 0.0).astype(BF)
            (dn0, dn1)[b][...] = (dx + nn(dl, small[...])).astype(BF)
            (mix0, mix1)[b][...] = mx.astype(BF)
            part = tn(dl, xs[b][...])
            wrg[...] = part if b == 0 else wrg[...] + part
        else:
            mix[b], dn[b], dprob[b] = mx, dx, dp
    if fresh:
        out_a[...] = nn(xt[0], di_s[0]) + nn(xt[1], di_s[1])
        out_b[...] = nn(gt[0], hg_s[0]) + nn(gt[1], hg_s[1])
    else:
        for dst, rows in ((out_a, own), (out_b, oth)):
            gin = gin_in[rows, :] + nn(xt[0, rows, :], di_s[0]) + nn(xt[1, rows, :], di_s[1])
            gout = gout_in[rows, :] + nn(gt[0, rows, :], hg_s[0]) + nn(gt[1, rows, :], hg_s[1])
            dst[0:256, :] = gin.astype(BF)
            dst[256:512, :] = gout.astype(BF)


def moe(e, base, idx, rows, weights, state, shared, grads=(), end=False, after=()):
    start, fresh = not state, not grads
    routes, small = shared
    args = (idx, *rows, *weights) + ((routes, small) if start else state) + ((small,) if end else ()) + grads
    outs = []
    if start:
        outs += [held(2, D, ROWS), held(2, D, ROWS), held(2, ROWS, 16, dtype=F32)]
    if end:
        outs += [held(ROWS, D)] * 4 + [held(8, D, dtype=F32)]
    else:
        outs += [held(2, ROWS, D, dtype=F32)] * 2 + [held(2, ROWS, 8, dtype=F32)]
    outs += [held(D, FFT, dtype=F32) if fresh else held(512, 512)] * 2
    scratch = [pltpu.VMEM((D, FFT), BF), pltpu.VMEM((FFT, D), BF)] + [pltpu.VMEM((2, ROWS, D), BF)] * 2
    got = call(functools.partial(moe_kernel, start, end, fresh, e, base), outs, args, scratch, after, 16)
    made, grads = got[:-2], got[-2:]
    if not end:
        made = tuple(made) if start else tuple(state[:3]) + tuple(made)
    return made, tuple(grads)


def add_kernel(idx, a, b, out):
    out[...] = (a[...].astype(F32) + b[...].astype(F32)).astype(BF)


def add(idx, a, b, after=()):
    return call(add_kernel, [held(*a.shape)], (idx, a, b), after=after, mib=8)[0]


def finish_kernel(idx, mine, given, *refs):
    win_grad, wout_grad = refs[-2:]
    ends = (idx[3] == 0) | (idx[3] == 3)
    total = jnp.where(ends, given[...], mine[...]).astype(F32)
    win_grad[0] = total[0:256, :]
    wout_grad[0] = total[256:512, :].T


def finish(idx, e, mine, given, into=(), after=()):
    block = lambda shape: pl.BlockSpec((1,) + shape, lambda i: (e, 0, 0))
    anywhere = [pl.BlockSpec(memory_space=pl.ANY)]
    return pl.pallas_call(
        skip(finish_kernel, 3, len(into) + len(after)),
        grid=(1,),
        out_shape=[sds((EXPERTS, 256, FFT), F32), sds((EXPERTS, FFT, 256), F32)],
        in_specs=[smem(), vmem(), vmem()] + anywhere * (len(into) + len(after)),
        out_specs=[block((256, FFT)), block((FFT, 256))],
        input_output_aliases={3: 0, 4: 1} if into else {},
        compiler_params=params(),
    )(idx, mine, given, *into, *after)


def merge_kernel(idx, own, sib, *outs):
    for j in range(2):
        outs[j][...] = (own[j].astype(F32) + sib[j].astype(F32)).astype(BF)


def cross_kernel(idx, near, near_got, far, far_got, pair, over):
    total = (near[...].astype(F32) + near_got[...].astype(F32)).astype(BF)
    pair[...] = total
    over[...] = (far[...].astype(F32) + far_got[...].astype(F32)).astype(BF)
    over[:, 512:528, :] = total[:, 512:528, :]


def halves_kernel(idx, pair, got, keep, send):
    total = (pair[...].astype(F32) + got[...].astype(F32)).astype(BF)
    keep[...] = total[0]
    send[...] = total[1]


def unpack_kernel(idx, own, sib, qkv_grad, o_grad, sgrad):
    c = idx[1]
    for src, ca in ((own, c), (sib, 1 - c)):
        rows = pl.ds(pl.multiple_of(ca * 128, 128), 128)
        for i in range(3):
            qkv_grad[i, rows, :] = src[i * 128 : (i + 1) * 128, :].astype(F32)
        head = pl.ds(pl.multiple_of(ca * 64, 64), 64)
        o_grad[head, 0:128] = src[384:448, :].astype(F32)
        o_grad[head, 128:256] = src[448:512, :].astype(F32)
        sgrad[:, rows] = src[512:520, :].astype(F32)


def flip(x, axis, bit):
    n = lax.axis_size(axis)
    return lax.ppermute(x, axis, [(i, i ^ bit) for i in range(n)])


def core(x):
    return flip(x, "tensor", 1)


def across(x):
    return flip(x, "tensor", 2)


def other(x):
    return flip(x, "fsdp", 1)


def packs_of_whole(qkv, out, small):
    def pack(j, fr, cr):
        at = fr * 256 + cr * 128
        head = out[j * 128 + cr * 64 : j * 128 + cr * 64 + 64, fr * 256 : fr * 256 + 256]
        return jnp.concatenate(
            [qkv[i, at : at + 128, j * 128 : (j + 1) * 128] for i in range(3)]
            + [head[:, :128], head[:, 128:]]
            + [small[:, fr * 256 : fr * 256 + 128], small[:, fr * 256 + 128 : fr * 256 + 256]]
        )

    return [
        [jnp.stack([pack(2 * p + j, fr, cr) for j in range(2)]) for cr in range(2) for fr in range(2)] for p in range(2)
    ]


def whole_of_packs(packs):
    qkv, out, small = jnp.zeros((3, D, D), F32), jnp.zeros((D, D), F32), jnp.zeros((8, D), F32)
    for j in range(4):
        for cr in range(2):
            for fr in range(2):
                pack = packs[j // 2][cr][j % 2, fr].astype(F32)
                at, hd = fr * 256 + cr * 128, j * 128 + cr * 64
                qkv = qkv.at[:, at : at + 128, j * 128 : (j + 1) * 128].set(pack[:384].reshape(3, 128, 128))
                out = out.at[hd : hd + 64, fr * 256 : fr * 256 + 128].set(pack[384:448])
                out = out.at[hd : hd + 64, fr * 256 + 128 : fr * 256 + 256].set(pack[448:512])
                if j == 0:
                    small = small.at[:, at : at + 128].set(pack[512:520])
    return qkv, out, small


def local(
    tokens, gain_one, shift_one, w_qkv, w_attn_out, gain_two, shift_two, w_router, w_in, w_out, routes, cotangent
):
    nf, nh = lax.axis_size("fsdp"), lax.axis_size("heads")
    near = nf == 2 and nh == 4
    f, h, t = lax.axis_index("fsdp"), lax.axis_index("heads"), lax.axis_index("tensor")
    zero = jnp.zeros((), jnp.int32)
    idx = jnp.stack([f if near else zero, t % 2 if near else zero, t, h]).astype(jnp.int32)

    w_own, w_oth = [None] * 4, [None] * 4
    rows = sds((ROWS, D), BF)
    if near:
        (pack,) = call(
            pack_kernel,
            [sds((PACK, 128), BF)],
            (idx, w_qkv, w_attn_out, w_router, gain_one, shift_one, gain_two, shift_two),
            fetch=True,
        )
        slots = [pack] + [flip(pack, "heads", j) for j in range(1, 4)]
        w_own[0] = packed_weights(idx, 0, w_in, w_out, after=(pack,))
        w_oth[0] = other(w_own[0])
        (tok,) = call(pad_kernel, [rows], (idx, tokens), after=(w_own[0],), fetch=True)
        (pair_a,) = call(pair_kernel, [held(2, PACK, 128)], (idx, slots[0], slots[1]), after=(tok,))
        (pair_b,) = call(pair_kernel, [held(2, PACK, 128)], (idx, slots[2], slots[3]), after=(pair_a,))
        (cot0,) = call(pad_kernel, [rows], (idx, cotangent), after=(pair_b,), fetch=True)
        w_own[1] = packed_weights(idx, 1, w_in, w_out, after=(cot0,))
        w_oth[1] = other(w_own[1])
        packs = []
        for pair in (pair_a, pair_b):
            pair_far = other(pair)
            packs.append([pair, pair_far, core(pair), core(pair_far)])
        before = (w_own[1], w_oth[0])
    else:
        small_own = jnp.concatenate([w_router.T, jnp.stack([gain_one, shift_one, gain_two, shift_two])])
        small = lax.all_gather(small_own, "fsdp", axis=1, tiled=True)
        qkv_all = lax.all_gather(lax.all_gather(w_qkv, "fsdp", axis=1, tiled=True), "heads", axis=2, tiled=True)
        out_all = lax.all_gather(lax.all_gather(w_attn_out, "fsdp", axis=1, tiled=True), "heads", axis=0, tiled=True)
        packs = packs_of_whole(qkv_all, out_all, small)
        in_all = lax.all_gather(w_in, "fsdp", axis=1, tiled=True)
        o_all = lax.all_gather(w_out, "fsdp", axis=2, tiled=True)
        for e in range(EXPERTS):
            w_own[e] = packed_weights(idx, e, in_all[:, :256], o_all[:, :, :256])
            w_oth[e] = packed_weights(idx, e, in_all[:, 256:], o_all[:, :, 256:])
        (tok,) = call(pad_kernel, [rows], (idx, tokens), fetch=True)
        (cot0,) = call(pad_kernel, [rows], (idx, cotangent), fetch=True)
        before = ()

    named = jnp.pad(routes.T.reshape(2, 8, SEQ), ((0, 0), (0, 0), (0, PAD - SEQ)), constant_values=-1)
    named = named.reshape(2, 4, ROWS).transpose(1, 0, 2)

    kept = [held(2, ROWS, 384), held(2, ROWS, 128), held(2, D, 384), held(2, 128, D)]
    small, n1, acc, qkv_a, mix_a, wq_a, wo_a = call(
        functools.partial(attn_fwd_kernel, True),
        [held(8, D), held(ROWS, D), held(ROWS, D, dtype=F32), *kept],
        (idx, tok, *packs[0]),
        after=before,
    )
    if near:
        w_own[2] = packed_weights(idx, 2, w_in, w_out, after=(n1,))
        w_oth[2] = other(w_own[2])
        before = (w_own[2],)
    cot1, cot2 = core(cot0), across(cot0)
    cot3 = core(cot2)
    n2_0, resid, qkv_b, mix_b, wq_b, wo_b = call(
        functools.partial(attn_fwd_kernel, False),
        [held(ROWS, D), held(ROWS, D, dtype=F32), *kept],
        (idx, tok, *packs[1], small, n1, acc),
        after=before,
    )
    n2_1, n2_2 = core(n2_0), across(n2_0)
    n2_3 = core(n2_2)
    if near:
        w_own[3] = packed_weights(idx, 3, w_in, w_out, after=(n2_0,))
        w_oth[3] = other(w_own[3])
        before = (w_own[3], w_oth[1])

    shared = (named, small)
    rows_a, rows_b = (n2_0, n2_1, cot0, cot1), (n2_2, n2_3, cot2, cot3)
    weights = [(w_own[e], w_oth[e]) for e in range(EXPERTS)]
    state_a, grads0 = moe(0, 0, idx, rows_a, weights[0], (), shared, after=before)
    state_a, grads1 = moe(1, 0, idx, rows_a, weights[1], state_a, shared, after=grads0)
    state_b, (keep0, send0) = moe(0, 2, idx, rows_b, weights[0], (), shared, grads0, after=grads1[:1])
    state_b, (keep1, send1) = moe(1, 2, idx, rows_b, weights[1], state_b, shared, grads1)
    state_a, grads2 = moe(2, 0, idx, rows_a, weights[2], state_a, shared, after=(keep1,))
    state_b, (keep2, send2) = moe(2, 2, idx, rows_b, weights[2], state_b, shared, grads2)
    (d2, d3, m2, m3, wr_b), grads3 = moe(3, 2, idx, rows_b, weights[3], state_b, shared, end=True)
    (d0, d1, m0, m1, wr_a), (keep3, send3) = moe(3, 0, idx, rows_a, weights[3], state_a, shared, grads3, end=True)
    keeps, sends = (keep0, keep1, keep2, keep3), (send0, send1, send2, send3)

    d_near = core(d1)
    d_sum = add(idx, d2, core(d3), after=(keep3,))
    d_far = across(d_sum)
    m_near = core(m1)
    m_sum = add(idx, m2, core(m3), after=(d_sum,))
    m_far = across(m_sum)
    ones, twos, threes = [None] * 4, [None] * 4, [None] * 4
    inward = lambda x: lax.ppermute(x, "heads", [(0, 1), (3, 2)])
    middle = lambda x: lax.ppermute(x, "heads", [(1, 2), (2, 1)])
    outward = lambda x: lax.ppermute(x, "heads", [(1, 0), (2, 3)])
    before = ()
    if near:
        got = [other(send) for send in sends]
        ones[0] = add(idx, keeps[0], got[0], after=(m_sum,))
        ones[1] = add(idx, keeps[1], got[1], after=(ones[0],))
        twos[0] = add(idx, ones[0], inward(ones[0]), after=(ones[1],))
        before = (twos[0],)

    scratch = [pltpu.VMEM((ROWS, 384), BF), pltpu.VMEM((D, 384), BF), pltpu.VMEM((128, D), BF)]
    both = [held(2, 2, PACK, 128)] * 2
    own_b, sib_b, dresid, sgrad, dn1 = call(
        functools.partial(attn_bwd_kernel, True),
        both + [held(ROWS, D, dtype=F32), held(8, D, dtype=F32), held(ROWS, D, dtype=F32)],
        (idx, d0, d_near, d_far, resid, cot0, wr_a, wr_b, small, n1, qkv_b, mix_b, wq_b, wo_b),
        scratch,
        after=before,
    )
    if near:
        ones[2] = add(idx, keeps[2], got[2], after=(dn1,))
        twos[1] = add(idx, ones[1], inward(ones[1]), after=(ones[2],))
        before = (twos[1],)
    own_a, sib_a, input_grad = call(
        functools.partial(attn_bwd_kernel, False),
        both + [sds((SEQ * 2, D), BF)],
        (idx, dresid, sgrad, dn1, tok, small, n1, qkv_a, mix_a, wq_a, wo_a),
        scratch + [pltpu.VMEM((8, D), F32)],
        after=before,
    )

    if near:
        held_pack = held(2, PACK, 128)
        slot2, slot3 = call(merge_kernel, [held_pack] * 2, (idx, own_b, core(sib_b)), after=(own_a,))
        got3 = flip(slot3, "heads", 1)
        ones[3] = add(idx, keeps[3], got[3], after=(slot2,))
        slot0, slot1 = call(merge_kernel, [held_pack] * 2, (idx, own_a, core(sib_a)), after=(ones[3],))
        got1 = flip(slot1, "heads", 1)
        threes[0] = add(idx, twos[0], middle(twos[0]), after=(slot0,))
        twos[2] = add(idx, ones[2], inward(ones[2]), after=(threes[0],))
        pair, over = call(cross_kernel, [held_pack] * 2, (idx, slot0, got1, slot2, got3), after=(twos[2],))
        over = flip(over, "heads", 2)
        threes[1] = add(idx, twos[1], middle(twos[1]), after=(pair,))
        twos[3] = add(idx, ones[3], inward(ones[3]), after=(threes[1],))
        (output,) = call(out_kernel, [sds((SEQ * 2, D), BF)], (idx, resid, m0, m_near, m_far), after=(twos[3],))
        grads = finish(idx, 0, threes[0], outward(threes[0]), after=(output,))
        threes[2] = add(idx, twos[2], middle(twos[2]), after=(grads[0],))
        half, send = call(halves_kernel, [held(PACK, 128)] * 2, (idx, pair, over), after=(threes[2],))
        grads = finish(idx, 1, threes[1], outward(threes[1]), grads, after=(half,))
        half = add(idx, half, other(send), after=(grads[0],))
        threes[3] = add(idx, twos[3], middle(twos[3]), after=(half,))
        half = add(idx, half, across(half), after=(threes[3],))
        grads = finish(idx, 2, threes[2], outward(threes[2]), grads, after=(half,))
        qkv_grad, o_grad, sgrad = call(
            unpack_kernel,
            [sds((3, 256, 128), F32), sds((128, 256), F32), sds((8, 256), F32)],
            (idx, half, core(half)),
            after=(grads[0],),
        )
        win_grad, wout_grad = finish(idx, 3, threes[3], outward(threes[3]), grads, after=(sgrad,))
    else:
        (output,) = call(out_kernel, [sds((SEQ * 2, D), BF)], (idx, resid, m0, m_near, m_far))
        keep, send = jnp.stack(keeps), jnp.stack(sends)
        gin = jnp.concatenate([keep[:, :256], send[:, :256]], 1)
        gout = jnp.concatenate([keep[:, 256:], send[:, 256:]], 1).transpose(0, 2, 1)
        win_grad = lax.psum_scatter(gin, "fsdp", scatter_dimension=1, tiled=True)
        wout_grad = lax.psum_scatter(gout, "fsdp", scatter_dimension=2, tiled=True)
        win_grad = lax.psum(win_grad, "heads").astype(F32)
        wout_grad = lax.psum(wout_grad, "heads").astype(F32)
        qkv_grad, o_grad, sgrad = whole_of_packs(((own_a, sib_a), (own_b, sib_b)))
        qkv_grad = lax.psum_scatter(qkv_grad, "fsdp", scatter_dimension=1, tiled=True)
        qkv_grad = lax.psum_scatter(qkv_grad, "heads", scatter_dimension=2, tiled=True)
        qkv_grad = lax.psum(qkv_grad, "tensor")
        o_grad = lax.psum_scatter(o_grad, "fsdp", scatter_dimension=1, tiled=True)
        o_grad = lax.psum_scatter(o_grad, "heads", scatter_dimension=0, tiled=True)
        o_grad = lax.psum(o_grad, "tensor")
        sgrad = lax.psum(sgrad, ("fsdp", "heads", "tensor"))
        sgrad = lax.dynamic_slice_in_dim(sgrad, f * gain_one.shape[0], gain_one.shape[0], 1)

    return (
        output,
        input_grad,
        sgrad[4],
        sgrad[5],
        qkv_grad,
        o_grad,
        sgrad[6],
        sgrad[7],
        sgrad[0:4].T,
        win_grad,
        wout_grad,
    )


def solution(mesh):
    placed = (
        P(("fsdp", "heads", "tensor"), None),
        P("fsdp"),
        P("fsdp"),
        P(None, "fsdp", "heads"),
        P("heads", "fsdp"),
        P("fsdp"),
        P("fsdp"),
        P("fsdp", None),
        P(None, "fsdp", "tensor"),
        P(None, "tensor", "fsdp"),
        P(("fsdp", "heads"), None),
        P(("fsdp", "heads", "tensor"), None),
    )
    return jax.shard_map(
        local,
        mesh=mesh,
        in_specs=placed,
        out_specs=(
            P(("fsdp", "heads", "tensor"), None),
            P(("fsdp", "heads", "tensor"), None),
            P("fsdp"),
            P("fsdp"),
            P(None, "fsdp", "heads"),
            P("heads", "fsdp"),
            P("fsdp"),
            P("fsdp"),
            P("fsdp", None),
            P(None, "fsdp", "tensor"),
            P(None, "tensor", "fsdp"),
        ),
        check_vma=False,
    )
```

```python
import functools

import jax
import jax.numpy as jnp
from jax import lax
from jax.experimental import pallas as pl
from jax.experimental.pallas import tpu as pltpu
from jax.sharding import PartitionSpec as P

HD = 64
SEQ = 197
PAD = 208
ROWS = 2 * PAD
D = 512
FFT = 512
EXPERTS = 4
BF = jnp.bfloat16
F32 = jnp.float32
PACK = 528
GELU_C = 0.7978845608028654


def nn(a, b):
    return lax.dot_general(a, b, (((1,), (0,)), ((), ())), preferred_element_type=F32)


def nt(a, b):
    return lax.dot_general(a, b, (((1,), (1,)), ((), ())), preferred_element_type=F32)


def tn(a, b):
    return lax.dot_general(a, b, (((0,), (0,)), ((), ())), preferred_element_type=F32)


def params(sem=None, mib=24):
    return pltpu.CompilerParams(vmem_limit_bytes=mib * 1024 * 1024, dimension_semantics=sem)


class Place:
    def __init__(self, apart):
        self.apart = apart

    def f(self):
        return 0 if self.apart else lax.axis_index("fsdp")

    def c(self):
        return 0 if self.apart else lax.axis_index("tensor") & 1

    def t(self):
        return lax.axis_index("tensor")

    def h(self):
        return lax.axis_index("heads")


def vmem():
    return pl.BlockSpec(memory_space=pltpu.VMEM)


def sds(shape, dtype):
    return jax.ShapeDtypeStruct(shape, dtype)


def held(*shape, dtype=BF):
    return pltpu.VMEM(shape, dtype)


def skip(kernel, n_args, n_after):
    def run(*refs):
        kernel(*refs[:n_args], *refs[n_args + n_after :])

    return run


def call(kernel, outs, args, scratch=(), after=(), mib=16, fetch=False):
    spec = (lambda x: pl.BlockSpec(x.shape, lambda i: (0,) * len(x.shape))) if fetch else (lambda x: vmem())
    space = pltpu.HBM if fetch else pltpu.VMEM
    return pl.pallas_call(
        skip(kernel, len(args), len(after)),
        grid=(1,) if fetch else (),
        out_shape=outs,
        in_specs=[spec(x) for x in args] + [pl.BlockSpec(memory_space=pl.ANY)] * len(after),
        out_specs=[spec(x) for x in outs],
        scratch_shapes=list(scratch),
        compiler_params=params(mib=mib),
    )(*[pltpu.with_memory_space_constraint(x, space) for x in args], *after)


def pack_kernel(at, wqkv, wo, wr, g1, s1, g2, s2, out):
    c = at.c()
    rows = pl.ds(pl.multiple_of(c * 128, 128), 128)
    for i in range(3):
        out[i * 128 : (i + 1) * 128, :] = wqkv[i, rows, :]
    head = pl.ds(pl.multiple_of(c * 64, 64), 64)
    out[384:448, :] = wo[head, 0:128]
    out[448:512, :] = wo[head, 128:256]
    small = [wr[...].astype(F32)] + [r[...].reshape(1, 256).astype(F32) for r in (g1, s1, g2, s2)]
    small = jnp.concatenate(small, axis=0).astype(BF)
    out[512:520, :] = small[:, 0:128]
    out[520:528, :] = small[:, 128:256]


def copy_kernel(src, out):
    out[...] = src[...]


def gate(x, after):
    return call(copy_kernel, [held(*x.shape)], (x,), after=after, mib=8)[0]


def pair_kernel(own, oth, out):
    out[0] = own[...]
    out[1] = oth[...]


def weights_kernel(win, wout, out):
    out[0:256, :] = win[0]
    out[256:512, 0:256] = wout[0, 0:256, :]
    out[256:512, 256:512] = wout[0, 256:512, :]


def packed_weights(e, w_in, w_out, after=()):
    hbm = lambda x: pltpu.with_memory_space_constraint(x, pltpu.HBM)
    return pl.pallas_call(
        skip(weights_kernel, 2, len(after)),
        grid=(1,),
        out_shape=held(512, 512),
        in_specs=[pl.BlockSpec((1, 256, 512), lambda i: (e, 0, 0)), pl.BlockSpec((1, 512, 256), lambda i: (e, 0, 0))]
        + [pl.BlockSpec(memory_space=pl.ANY)] * len(after),
        out_specs=vmem(),
        compiler_params=params(mib=8),
    )(hbm(w_in), hbm(w_out), *after)


def spread(v):
    zero = jnp.zeros((PAD - SEQ, v.shape[1]), v.dtype)
    return jnp.concatenate([v[:SEQ], zero, v[SEQ:], zero], axis=0)


def close(v):
    return jnp.concatenate([v[:SEQ], v[PAD : PAD + SEQ]], axis=0)


def pad_kernel(rows, out):
    out[...] = spread(rows[...].astype(F32)).astype(BF)


def norm_parts(x):
    center = jnp.mean(x, -1, keepdims=True)
    centered = x - center
    rstd = lax.rsqrt(jnp.mean(centered * centered, -1, keepdims=True) + 1e-06)
    return centered * rstd, rstd


def norm_back(xhat, rstd, grad, gain):
    dxhat = grad * gain
    m1 = jnp.mean(dxhat, -1, keepdims=True)
    m2 = jnp.mean(dxhat * xhat, -1, keepdims=True)
    return rstd * (dxhat - m1 - xhat * m2)


def attn_fwd_kernel(first, at, tok, *refs):
    packs, refs = (refs[0:2], refs[2:4]), refs[4:]
    if first:
        (small, n1_ref, acc_ref), refs = refs[:3], refs[3:]
    else:
        (small, n1_ref, acc_in, n2_ref, acc_ref), refs = refs[:5], refs[5:]
    kept, (qkv_ref, mix_ref, wq_ref, wo_ref), sems = refs[:4], refs[4:8], refs[8]
    copies = []

    def keep(which, j):
        src, dst = (qkv_ref, mix_ref, wq_ref, wo_ref)[which].at[j], kept[which].at[j]
        copies.append(pltpu.make_async_copy(src, dst, sems.at[which, j]))
        copies[-1].start()

    f, c = at.f(), at.c()
    if first:
        for fr in range(2):
            left = (f ^ fr) * 256
            for i in range(2):
                cols = pl.ds(pl.multiple_of(left + i * 128, 128), 128)
                small[:, cols] = packs[0][fr][0, 512 + 8 * i : 520 + 8 * i, :]
        x = tok[...].astype(F32)
        xhat, _ = norm_parts(x)
        n1 = (xhat * small[4:5, :].astype(F32) + small[5:6, :].astype(F32)).astype(BF)
        n1_ref[...] = n1
        acc = [x[0:PAD], x[PAD:ROWS]]
    else:
        n1 = n1_ref[...]
        acc = [acc_in[0:PAD, :], acc_in[PAD:ROWS, :]]
    lane = lax.broadcasted_iota(jnp.int32, (PAD, 128), 1)
    key = lax.broadcasted_iota(jnp.int32, (PAD, PAD), 1)
    for j in range(2):
        for fr in range(2):
            fa = f ^ fr
            for cr in range(2):
                ca = c ^ cr
                src = packs[cr][fr]
                rows = pl.ds(pl.multiple_of(fa * 256 + ca * 128, 128), 128)
                for i in range(3):
                    wq_ref[j, rows, i * 128 : (i + 1) * 128] = src[j, i * 128 : (i + 1) * 128, :]
                head = pl.ds(pl.multiple_of(ca * 64, 64), 64)
                for i in range(2):
                    cols = pl.ds(pl.multiple_of(fa * 256 + i * 128, 128), 128)
                    wo_ref[j, head, cols] = src[j, 384 + 64 * i : 448 + 64 * i, :]
        keep(2, j)
        keep(3, j)
        qkv_ref[j] = nn(n1, wq_ref[j]).astype(BF)
        keep(0, j)
        for im in range(2):
            r = slice(im * PAD, (im + 1) * PAD)
            q, k, v = (qkv_ref[j, r, i * 128 : (i + 1) * 128] for i in range(3))
            outs = []
            for head in range(2):
                s = nt(jnp.where(lane // HD == head, q, jnp.zeros_like(q)), k) * 0.125
                s = jnp.where(key < SEQ, s, -1e30)
                e = jnp.exp(s - jnp.max(s, -1, keepdims=True))
                p = e / jnp.sum(e, -1, keepdims=True)
                outs.append(nn(p.astype(BF), v))
            mix = jnp.where(lane < HD, outs[0], outs[1]).astype(BF)
            mix_ref[j, r, :] = mix
            acc[im] = acc[im] + nn(mix, wo_ref[j])
        keep(1, j)
    for im in range(2):
        r = slice(im * PAD, (im + 1) * PAD)
        acc_ref[r, :] = acc[im]
        if not first:
            xhat, _ = norm_parts(acc[im])
            n2_ref[r, :] = (xhat * small[6:7, :].astype(F32) + small[7:8, :].astype(F32)).astype(BF)
    for copy in copies:
        copy.wait()


def attn_bwd_kernel(first, at, *refs):
    take = lambda k: (refs[:k], refs[k:])
    if first:
        (d0, d1, d2, resid, cot, wr_a, wr_b, small), refs = take(8)
    else:
        (dresid_in, sgrad_in, dn1_in, tok, small), refs = take(5)
    (n1, qkvs, mixes, wqs, wos, own, *sibs), refs = take(8)
    if first:
        dresid_out, sgrad, dn1_out, dqkv_s, gq_s, go_s = refs
    else:
        igrad, dqkv_s, gq_s, go_s, sgrad = refs
    f, c = at.f(), at.c()
    if first:
        dn2 = d0[...].astype(F32) + d1[...].astype(F32) + d2[...].astype(F32)
        xhat, rstd = norm_parts(resid[...])
        sgrad[0:4, :] = (wr_a[...] + wr_b[...])[0:4]
        sgrad[4:6, :] = jnp.zeros((2, D), F32)
        sgrad[6:7, :] = jnp.sum(dn2 * xhat, 0, keepdims=True)
        sgrad[7:8, :] = jnp.sum(dn2, 0, keepdims=True)
        dresid = cot[...].astype(F32) + norm_back(xhat, rstd, dn2, small[6:7, :].astype(F32))
        dresid_out[...] = dresid
    else:
        dresid = dresid_in[...]
    dattn = dresid.astype(BF)
    lane = lax.broadcasted_iota(jnp.int32, (PAD, 128), 1)
    key = lax.broadcasted_iota(jnp.int32, (PAD, PAD), 0)
    n1t = n1[...].T
    dn1 = None if first else dn1_in[...]
    for j in range(2):
        qkv, mix, wq, wo = (ref.at[j] for ref in (qkvs, mixes, wqs, wos))
        go_s[...] = tn(mix[...], dattn).astype(BF)
        dmix = nt(dattn, wo[...]).astype(BF)
        for im in range(2):
            r = slice(im * PAD, (im + 1) * PAD)
            q, k, v = (qkv[r, i * 128 : (i + 1) * 128] for i in range(3))
            dm = dmix[r]
            dq, dk, dv = [], [], []
            for head in range(2):
                keep = lane // HD == head
                s = nt(k, jnp.where(keep, q, jnp.zeros_like(q))) * 0.125
                s = jnp.where(key < SEQ, s, -1e30)
                e = jnp.exp(s - jnp.max(s, 0, keepdims=True))
                p = e / jnp.sum(e, 0, keepdims=True)
                dp = nt(v, jnp.where(keep, dm, jnp.zeros_like(dm)))
                ds = (p * (dp - jnp.sum(p * dp, 0, keepdims=True))).astype(BF)
                dq.append(tn(ds, k))
                dk.append(nn(ds, q))
                dv.append(nn(p.astype(BF), dm))
            near = lane < HD
            dqkv_s[r, 0:128] = (jnp.where(near, dq[0], dq[1]) * 0.125).astype(BF)
            dqkv_s[r, 128:256] = (jnp.where(near, dk[0], dk[1]) * 0.125).astype(BF)
            dqkv_s[r, 256:384] = jnp.where(near, dv[0], dv[1]).astype(BF)
        dqkv = dqkv_s[...]
        gq_s[...] = nn(n1t, dqkv).astype(BF)
        part = nt(dqkv, wq[...])
        dn1 = part if dn1 is None else dn1 + part
        for fr in range(2):
            fa = f ^ fr
            for cr in range(2):
                ca = c ^ cr
                dst = (own.at[j], sibs[j])[cr]
                rows = pl.ds(pl.multiple_of(fa * 256 + ca * 128, 128), 128)
                for i in range(3):
                    dst[fr, i * 128 : (i + 1) * 128, :] = gq_s[rows, i * 128 : (i + 1) * 128]
                head = pl.ds(pl.multiple_of(ca * 64, 64), 64)
                for i in range(2):
                    cols = pl.ds(pl.multiple_of(fa * 256 + i * 128, 128), 128)
                    dst[fr, 384 + 64 * i : 448 + 64 * i, :] = go_s[head, cols]
    if first:
        dn1_out[...] = dn1
        for j in range(2):
            for fr in range(2):
                own[j, fr, 512:528, :] = jnp.zeros((16, 128), BF)
                sibs[j][fr, 512:528, :] = jnp.zeros((16, 128), BF)
        return
    xhat, rstd = norm_parts(tok[...].astype(F32))
    sgrad[...] = sgrad_in[...]
    sgrad[4:5, :] = jnp.sum(dn1 * xhat, 0, keepdims=True)
    sgrad[5:6, :] = jnp.sum(dn1, 0, keepdims=True)
    for fr in range(2):
        for cr in range(2):
            left = (f ^ fr) * 256 + (c ^ cr) * 128
            rows = sgrad[:, pl.ds(pl.multiple_of(left, 128), 128)]
            rows = jnp.concatenate([rows, jnp.zeros_like(rows)], axis=0).astype(BF)
            for j in range(2):
                (own.at[j], sibs[j])[cr][fr, 512:528, :] = rows
    grad = dresid + norm_back(xhat, rstd, dn1, small[4:5, :].astype(F32))
    igrad[...] = close(grad).astype(BF)


def out_kernel(resid, m0, m1, m2, out):
    total = resid[...] + m0[...].astype(F32) + m1[...].astype(F32) + m2[...].astype(F32)
    out[...] = close(total).astype(BF)


def assemble_kernel(at, own, oth, win, wout):
    f = at.f()
    for w, half in ((own, f), (oth, 1 - f)):
        half = pl.ds(pl.multiple_of(half * 256, 256), 256)
        win[half, :] = w[0:256, :]
        wout[0:256, half] = w[256:512, 0:256]
        wout[256:512, half] = w[256:512, 256:512]


def assemble(at, own, oth, after=()):
    return call(functools.partial(assemble_kernel, at), [held(512, 512)] * 2, (own, oth), after=after, mib=8)


def moe_kernel(start, end, fresh, e, base, at, x0, x1, g0, g1, win, wout, *refs):
    take = lambda k: (refs[:k], refs[k:])
    if start:
        (routes, small), refs = take(2)
    else:
        (xt, gt, gating, mix_in, dn_in, dp_in), refs = take(6)
    if end:
        (small,), refs = take(1)
    if not fresh:
        (gin_in, gout_in), refs = take(2)
    if start:
        (xt, gt, gating), refs = take(3)
    if end:
        (dn0, dn1, mix0, mix1, wrg), refs = take(5)
    else:
        (mix, dn, dprob), refs = take(3)
    out_a, out_b, hg_s, di_s = refs
    f = at.f()
    xs, gs = (x0, x1), (g0, g1)
    lane = lax.broadcasted_iota(jnp.int32, (ROWS, 8), 1)
    if start:
        for b in range(2):
            xt[b] = xs[b][...].T
            gt[b] = gs[b][...].T
            logits = jnp.where(lane < EXPERTS, nt(xs[b][...], small[...]), -1e30)
            ex = jnp.exp(logits - jnp.max(logits, -1, keepdims=True))
            named = routes[at.t() ^ (base + b)]
            expert = lax.broadcasted_iota(jnp.int32, (8, ROWS), 0)
            gating[b, :, 0:8] = ex / jnp.sum(ex, -1, keepdims=True)
            gating[b, :, 8:16] = jnp.where((named[0:1] == expert) | (named[1:2] == expert), 1.0, 0.0).T
    own = pl.ds(pl.multiple_of(f * 256, 256), 256)
    oth = pl.ds(pl.multiple_of((1 - f) * 256, 256), 256)
    for b in range(2):
        inner = nn(xs[b][...], win[...])
        back = nt(gs[b][...], wout[...])
        gate = gating[b, :, e : e + 1] * gating[b, :, 8 + e : 9 + e]
        square = inner * inner
        th = jnp.tanh(inner * (square * (GELU_C * 0.044715) + GELU_C))
        half = th * 0.5 + 0.5
        hidden = inner * half
        slope = half * ((1.0 - half) * (inner * (square * (6 * GELU_C * 0.044715) + 2 * GELU_C)) + 1.0)
        dp = jnp.where(lane == e, jnp.sum(hidden * back, -1, keepdims=True), 0.0)
        hg = (gate * hidden).astype(BF)
        di = ((gate * back) * slope).astype(BF)
        hg_s[b] = hg
        di_s[b] = di
        mx, dx = nn(hg, wout[...]), nt(di, win[...])
        if not start:
            dp, mx, dx = dp + dp_in[b], mx + mix_in[b], dx + dn_in[b]
        if end:
            router = gating[b, :, 0:8]
            dp = dp * gating[b, :, 8:16]
            dl = router * (dp - jnp.sum(router * dp, -1, keepdims=True))
            dl = jnp.where(lane < EXPERTS, dl, 0.0).astype(BF)
            (dn0, dn1)[b][...] = (dx + nn(dl, small[...])).astype(BF)
            (mix0, mix1)[b][...] = mx.astype(BF)
            part = tn(dl, xs[b][...])
            wrg[...] = part if b == 0 else wrg[...] + part
        else:
            mix[b], dn[b], dprob[b] = mx, dx, dp
    if fresh:
        out_a[...] = nn(xt[0], di_s[0]) + nn(xt[1], di_s[1])
        out_b[...] = nn(gt[0], hg_s[0]) + nn(gt[1], hg_s[1])
    else:
        for dst, rows in ((out_a, own), (out_b, oth)):
            gin = gin_in[rows, :] + nn(xt[0, rows, :], di_s[0]) + nn(xt[1, rows, :], di_s[1])
            gout = gout_in[rows, :] + nn(gt[0, rows, :], hg_s[0]) + nn(gt[1, rows, :], hg_s[1])
            dst[0:256, :] = gin.astype(BF)
            dst[256:512, :] = gout.astype(BF)


def moe(e, base, at, rows, weights, state, shared, grads=(), end=False, after=()):
    start, fresh = not state, not grads
    routes, small = shared
    args = (*rows, *weights) + ((routes, small) if start else state) + ((small,) if end else ()) + grads
    outs = []
    if start:
        outs += [held(2, D, ROWS), held(2, D, ROWS), held(2, ROWS, 16, dtype=F32)]
    if end:
        outs += [held(ROWS, D)] * 4 + [held(8, D, dtype=F32)]
    else:
        outs += [held(2, ROWS, D, dtype=F32)] * 2 + [held(2, ROWS, 8, dtype=F32)]
    outs += [held(D, FFT, dtype=F32) if fresh else held(512, 512)] * 2
    scratch = [pltpu.VMEM((2, ROWS, D), BF)] * 2
    got = call(functools.partial(moe_kernel, start, end, fresh, e, base, at), outs, args, scratch, after, 16)
    made, grads = got[:-2], got[-2:]
    if not end:
        made = tuple(made) if start else tuple(state[:3]) + tuple(made)
    return made, tuple(grads)


def add_kernel(a, b, out):
    out[...] = (a[...].astype(F32) + b[...].astype(F32)).astype(BF)


def add(a, b, after=()):
    return call(add_kernel, [held(*a.shape)], (a, b), after=after, mib=8)[0]


def finish_kernel(at, mine, given, *refs):
    win_grad, wout_grad, done = refs[-3:]
    done[...] = jnp.zeros_like(done)
    h = at.h()
    total = jnp.where((h == 0) | (h == 3), given[...], mine[...]).astype(F32)
    win_grad[0] = total[0:256, :]
    wout_grad[0] = total[256:512, :].T


def finish(at, e, mine, given, into=(), after=()):
    block = lambda shape: pl.BlockSpec((1,) + shape, lambda i: (e, 0, 0))
    anywhere = [pl.BlockSpec(memory_space=pl.ANY)]
    pin = lambda x: pltpu.with_memory_space_constraint(x, pltpu.VMEM)
    return pl.pallas_call(
        skip(functools.partial(finish_kernel, at), 2, len(into) + len(after)),
        grid=(1,),
        out_shape=[pltpu.HBM((EXPERTS, 256, FFT), F32), pltpu.HBM((EXPERTS, FFT, 256), F32), held(8, 128, dtype=F32)],
        in_specs=[vmem(), vmem()] + anywhere * (len(into) + len(after)),
        out_specs=[block((256, FFT)), block((FFT, 256)), vmem()],
        input_output_aliases={2: 0, 3: 1} if into else {},
        compiler_params=params(mib=12),
    )(pin(mine), pin(given), *[pltpu.with_memory_space_constraint(x, pltpu.HBM) for x in into], *after)


def halves_kernel(own, sib0, sib1, keep, send):
    for j in range(2):
        sib = (sib0, sib1)[j]
        keep[j] = (own[j, 0].astype(F32) + sib[0].astype(F32)).astype(BF)
        send[j] = (own[j, 1].astype(F32) + sib[1].astype(F32)).astype(BF)


def slots_kernel(keep, got, first, second):
    first[...] = (keep[0].astype(F32) + got[0].astype(F32)).astype(BF)
    second[...] = (keep[1].astype(F32) + got[1].astype(F32)).astype(BF)


def cross_kernel(near, near_got, far, far_got, pair, over):
    total = (near[...].astype(F32) + near_got[...].astype(F32)).astype(BF)
    pair[...] = total
    over[0:512, :] = (far[0:512, :].astype(F32) + far_got[0:512, :].astype(F32)).astype(BF)
    over[512:528, :] = total[512:528]


def unpack_kernel(at, own, sib, qkv_grad, o_grad, wr_grad, g1, s1, g2, s2):
    c = at.c()
    for src, ca in ((own, c), (sib, 1 - c)):
        rows = pl.ds(pl.multiple_of(ca * 128, 128), 128)
        for i in range(3):
            qkv_grad[i, rows, :] = src[i * 128 : (i + 1) * 128, :].astype(F32)
        head = pl.ds(pl.multiple_of(ca * 64, 64), 64)
        o_grad[head, 0:128] = src[384:448, :].astype(F32)
        o_grad[head, 128:256] = src[448:512, :].astype(F32)
        small = src[512:528, :].astype(F32)
        wr_grad[:, rows] = small[0:4]
        for i, ref in enumerate((g1, s1, g2, s2)):
            ref[:, rows] = small[4 + i : 5 + i]


def flip(x, axis, bit):
    n = lax.axis_size(axis)
    return lax.ppermute(x, axis, [(i, i ^ bit) for i in range(n)])


def core(x):
    return flip(x, "tensor", 1)


def across(x):
    return flip(x, "tensor", 2)


def other(x):
    return flip(x, "fsdp", 1)


def packs_of_whole(qkv, out, small):
    def pack(j, fr, cr):
        at = fr * 256 + cr * 128
        head = out[j * 128 + cr * 64 : j * 128 + cr * 64 + 64, fr * 256 : fr * 256 + 256]
        return jnp.concatenate(
            [qkv[i, at : at + 128, j * 128 : (j + 1) * 128] for i in range(3)]
            + [head[:, :128], head[:, 128:]]
            + [small[:, fr * 256 : fr * 256 + 128], small[:, fr * 256 + 128 : fr * 256 + 256]]
        )

    return [
        [jnp.stack([pack(2 * p + j, fr, cr) for j in range(2)]) for cr in range(2) for fr in range(2)] for p in range(2)
    ]


def whole_of_packs(packs):
    qkv, out, small = jnp.zeros((3, D, D), F32), jnp.zeros((D, D), F32), jnp.zeros((8, D), F32)
    for j in range(4):
        for cr in range(2):
            for fr in range(2):
                pack = packs[j // 2][cr][j % 2, fr].astype(F32)
                at, hd = fr * 256 + cr * 128, j * 128 + cr * 64
                qkv = qkv.at[:, at : at + 128, j * 128 : (j + 1) * 128].set(pack[:384].reshape(3, 128, 128))
                out = out.at[hd : hd + 64, fr * 256 : fr * 256 + 128].set(pack[384:448])
                out = out.at[hd : hd + 64, fr * 256 + 128 : fr * 256 + 256].set(pack[448:512])
                if j == 0:
                    small = small.at[:, at : at + 128].set(pack[512:520])
    return qkv, out, small


def forward(kernel, outs, kept, args, scratch, after):
    return pl.pallas_call(
        skip(kernel, len(args), len(after)),
        out_shape=outs + kept,
        in_specs=[vmem()] * len(args) + [pl.BlockSpec(memory_space=pl.ANY)] * len(after),
        out_specs=[vmem()] * len(outs) + [pl.BlockSpec(memory_space=pl.ANY)] * len(kept),
        scratch_shapes=scratch,
        compiler_params=params(mib=20),
    )(*[pltpu.with_memory_space_constraint(x, pltpu.VMEM) for x in args], *after)


def local(
    tokens, gain_one, shift_one, w_qkv, w_attn_out, gain_two, shift_two, w_router, w_in, w_out, routes, cotangent
):
    nf, nh = lax.axis_size("fsdp"), lax.axis_size("heads")
    near = nf == 2 and nh == 4
    f = lax.axis_index("fsdp")
    at = Place(not near)

    w_own, w_oth = [None] * 4, [None] * 4
    rows = sds((ROWS, D), BF)
    if near:
        (pack,) = call(
            functools.partial(pack_kernel, at),
            [sds((PACK, 128), BF)],
            (w_qkv, w_attn_out, w_router.T, gain_one, shift_one, gain_two, shift_two),
            fetch=True,
        )
        slots = [pack] + [flip(pack, "heads", j) for j in range(1, 4)]
        w_own[0] = packed_weights(0, w_in, w_out, after=(pack,))
        w_oth[0] = other(w_own[0])
        (tok,) = call(pad_kernel, [rows], (tokens,), after=(w_own[0],), fetch=True)
        pair = lambda a, b, after: call(pair_kernel, [held(2, PACK, 128)], (a, b), after=after, mib=8)[0]
        pair_b = pair(slots[2], slots[3], (tok, w_oth[0]))
        pair_a = pair(slots[0], slots[1], (pair_b,))
        far_a = pair(other(slots[0]), other(slots[1]), (pair_a,))
        far_b = other(pair_b)
        w_own[1] = packed_weights(1, w_in, w_out, after=(far_a,))
        w_oth[1] = other(w_own[1])
        sib_a = pair(core(slots[0]), core(slots[1]), (w_own[1],))
        packs = [[pair_a, far_a, sib_a, core(far_a)]]
        before = (w_own[1],)
    else:
        small_own = jnp.concatenate([w_router.T, jnp.stack([gain_one, shift_one, gain_two, shift_two])])
        small = lax.all_gather(small_own, "fsdp", axis=1, tiled=True)
        qkv_all = lax.all_gather(lax.all_gather(w_qkv, "fsdp", axis=1, tiled=True), "heads", axis=2, tiled=True)
        out_all = lax.all_gather(lax.all_gather(w_attn_out, "fsdp", axis=1, tiled=True), "heads", axis=0, tiled=True)
        packs = packs_of_whole(qkv_all, out_all, small)
        in_all = lax.all_gather(w_in, "fsdp", axis=1, tiled=True)
        o_all = lax.all_gather(w_out, "fsdp", axis=2, tiled=True)
        for e in range(EXPERTS):
            w_own[e] = packed_weights(e, in_all[:, :256], o_all[:, :, :256])
            w_oth[e] = packed_weights(e, in_all[:, 256:], o_all[:, :, 256:])
        (tok,) = call(pad_kernel, [rows], (tokens,), fetch=True)
        before = ()

    named = jnp.pad(routes.T.reshape(2, 8, SEQ), ((0, 0), (0, 0), (0, PAD - SEQ)), constant_values=-1)
    named = named.reshape(2, 4, ROWS).transpose(1, 0, 2)

    kept = [pltpu.HBM(shape, BF) for shape in ((2, ROWS, 384), (2, ROWS, 128), (2, D, 384), (2, 128, D))]
    scratch = [pltpu.VMEM(x.shape, BF) for x in kept] + [pltpu.SemaphoreType.DMA((4, 2))]
    small, n1, acc, qkv_a, mix_a, wq_a, wo_a = forward(
        functools.partial(attn_fwd_kernel, True, at),
        [held(8, D), held(ROWS, D), held(ROWS, D, dtype=F32)],
        kept,
        (tok, *packs[0]),
        scratch,
        before,
    )
    (cot0,) = call(pad_kernel, [rows], (cotangent,), after=(n1,), fetch=True)
    cot1, cot2 = core(cot0), across(cot0)
    before = ()
    if near:
        w_own[2] = packed_weights(2, w_in, w_out, after=(cot0,))
        w_oth[2] = other(w_own[2])
        far_b = gate(far_b, (w_own[2],))
        packs.append([pair_b, far_b, core(pair_b), core(far_b)])
    n2_0, resid, qkv_b, mix_b, wq_b, wo_b = forward(
        functools.partial(attn_fwd_kernel, False, at),
        [held(ROWS, D), held(ROWS, D, dtype=F32)],
        kept,
        (tok, *packs[1], small, n1, acc),
        scratch,
        before,
    )
    n2_1, n2_2 = core(n2_0), across(n2_0)

    shared = (named, small)
    rows_a = (n2_0, n2_1, cot0, cot1)
    before = (n2_0,)
    if near:
        w_own[3] = packed_weights(3, w_in, w_out, after=before)
        w_oth[3] = other(w_own[3])
        before = (w_own[3],)
    weights = [assemble(at, w_own[0], w_oth[0], before)]
    weights.append(assemble(at, w_own[1], w_oth[1], weights[0]))
    state_a, grads0 = moe(0, 0, at, rows_a, weights[0], (), shared, after=weights[1])
    state_a, grads1 = moe(1, 0, at, rows_a, weights[1], state_a, shared)
    cot2 = gate(cot2, grads1[:1])
    n2_2 = gate(n2_2, (cot2,))
    rows_b = (n2_2, core(n2_2), cot2, core(cot2))
    weights.append(assemble(at, w_own[2], w_oth[2], (n2_2,)))
    state_b, (keep0, send0) = moe(0, 2, at, rows_b, weights[0], (), shared, grads0, after=weights[2])
    state_b, (keep1, send1) = moe(1, 2, at, rows_b, weights[1], state_b, shared, grads1)
    state_a, grads2 = moe(2, 0, at, rows_a, weights[2], state_a, shared, after=(keep1,))
    weights.append(assemble(at, w_own[3], w_oth[3], grads2[:1]))
    state_b, (keep2, send2) = moe(2, 2, at, rows_b, weights[2], state_b, shared, grads2, after=weights[3])
    (d2, d3, m2, m3, wr_b), grads3 = moe(3, 2, at, rows_b, weights[3], state_b, shared, end=True)
    ones, twos, threes, before = [None] * 4, [None] * 4, [None] * 4, grads3[:1]
    if near:
        got0 = other(send0)
        ones[0] = add(keep0, got0, after=before)
        before = (ones[0],)
    (d0, d1, m0, m1, wr_a), (keep3, send3) = moe(3, 0, at, rows_a, weights[3], state_a, shared, grads3, True, before)
    keeps, sends = (keep0, keep1, keep2, keep3), (send0, send1, send2, send3)

    d_near = core(d1)
    d_sum = add(d2, core(d3), after=(keep3,))
    d_far = across(d_sum)
    inward = lambda x: lax.ppermute(x, "heads", [(0, 1), (3, 2)])
    middle = lambda x: lax.ppermute(x, "heads", [(1, 2), (2, 1)])
    outward = lambda x: lax.ppermute(x, "heads", [(1, 0), (2, 3)])
    before = ()
    if near:
        got = [got0] + [other(send) for send in sends[1:]]
        ones[1] = add(keeps[1], got[1], after=(d_sum,))
        twos[0] = add(ones[0], inward(ones[0]), after=(ones[1],))
        before = (twos[0],)

    scratch = [pltpu.VMEM((ROWS, 384), BF), pltpu.VMEM((D, 384), BF), pltpu.VMEM((128, D), BF)]
    both = [held(2, 2, PACK, 128)] + [held(2, PACK, 128)] * 2
    own_b, sib_2, sib_3, dresid, sgrad, dn1 = call(
        functools.partial(attn_bwd_kernel, True, at),
        both + [held(ROWS, D, dtype=F32), held(8, D, dtype=F32), held(ROWS, D, dtype=F32)],
        (d0, d_near, d_far, resid, cot0, wr_a, wr_b, small, n1, qkv_b, mix_b, wq_b, wo_b),
        scratch,
        after=before,
    )
    if near:
        ones[2] = add(keeps[2], got[2], after=(dn1,))
        twos[1] = add(ones[1], inward(ones[1]), after=(ones[2],))
        keep_b, send_b = call(halves_kernel, [held(2, PACK, 128)] * 2, (own_b, core(sib_2), core(sib_3)), after=(twos[1],))
        threes[0] = add(twos[0], middle(twos[0]), after=(keep_b,))
        ones[3] = add(keeps[3], got[3], after=(threes[0],))
        before = (ones[3],)
    own_a, sib_0, sib_1, input_grad = call(
        functools.partial(attn_bwd_kernel, False, at),
        both + [sds((SEQ * 2, D), BF)],
        (dresid, sgrad, dn1, tok, small, n1, qkv_a, mix_a, wq_a, wo_a),
        scratch + [pltpu.VMEM((8, D), F32)],
        after=before,
    )

    if near:
        one_pack = held(PACK, 128)
        slot2, slot3 = call(slots_kernel, [one_pack] * 2, (keep_b, other(send_b)), after=(own_a,))
        twos[2] = add(ones[2], inward(ones[2]), after=(slot2,))
        threes[1] = add(twos[1], middle(twos[1]), after=(twos[2],))
        keep_a, send_a = call(halves_kernel, [held(2, PACK, 128)] * 2, (own_a, core(sib_0), core(sib_1)), after=(threes[1],))
        *grads, done = finish(at, 0, threes[0], outward(threes[0]), after=(keep_a,))
        twos[3] = add(ones[3], inward(ones[3]), after=(done,))
        slot0, slot1 = call(slots_kernel, [one_pack] * 2, (keep_a, other(send_a)), after=(twos[3],))
        threes[2] = add(twos[2], middle(twos[2]), after=(slot0,))
        *grads, done = finish(at, 1, threes[1], outward(threes[1]), grads, after=(threes[2],))
        pair, over = call(
            cross_kernel,
            [one_pack] * 2,
            (slot0, flip(slot1, "heads", 1), slot2, flip(slot3, "heads", 1)),
            after=(done,),
        )
        threes[3] = add(twos[3], middle(twos[3]), after=(pair,))
        m_near = core(m1)
        m_sum = add(m2, core(m3), after=(threes[3],))
        m_far = across(m_sum)
        half = add(pair, flip(over, "heads", 2), after=(m_sum,))
        *grads, done = finish(at, 2, threes[2], outward(threes[2]), grads, after=(half,))
        half = add(half, across(half), after=(done,))
        vector = sds((1, 256), F32)
        qkv_grad, o_grad, wr_grad, *vectors = call(
            functools.partial(unpack_kernel, at),
            [sds((3, 256, 128), F32), sds((128, 256), F32), sds((4, 256), F32)] + [vector] * 4,
            (half, core(half)),
        )
        (output,) = call(out_kernel, [sds((SEQ * 2, D), BF)], (resid, m0, m_near, m_far), after=(half,))
        win_grad, wout_grad, _ = finish(at, 3, threes[3], outward(threes[3]), grads, after=(half,))
        vectors = [v.reshape(256) for v in vectors]
    else:
        m_near = core(m1)
        m_far = across(add(m2, core(m3)))
        (output,) = call(out_kernel, [sds((SEQ * 2, D), BF)], (resid, m0, m_near, m_far))
        keep, send = jnp.stack(keeps), jnp.stack(sends)
        gin = jnp.concatenate([keep[:, :256], send[:, :256]], 1)
        gout = jnp.concatenate([keep[:, 256:], send[:, 256:]], 1).transpose(0, 2, 1)
        win_grad = lax.psum_scatter(gin, "fsdp", scatter_dimension=1, tiled=True)
        wout_grad = lax.psum_scatter(gout, "fsdp", scatter_dimension=2, tiled=True)
        win_grad = lax.psum(win_grad, "heads").astype(F32)
        wout_grad = lax.psum(wout_grad, "heads").astype(F32)
        qkv_grad, o_grad, sgrad = whole_of_packs(((own_a, jnp.stack([sib_0, sib_1])), (own_b, jnp.stack([sib_2, sib_3]))))
        qkv_grad = lax.psum_scatter(qkv_grad, "fsdp", scatter_dimension=1, tiled=True)
        qkv_grad = lax.psum_scatter(qkv_grad, "heads", scatter_dimension=2, tiled=True)
        qkv_grad = lax.psum(qkv_grad, "tensor")
        o_grad = lax.psum_scatter(o_grad, "fsdp", scatter_dimension=1, tiled=True)
        o_grad = lax.psum_scatter(o_grad, "heads", scatter_dimension=0, tiled=True)
        o_grad = lax.psum(o_grad, "tensor")
        sgrad = lax.psum(sgrad, ("fsdp", "heads", "tensor"))
        sgrad = lax.dynamic_slice_in_dim(sgrad, f * gain_one.shape[0], gain_one.shape[0], 1)
        wr_grad, vectors = sgrad[0:4], [sgrad[4 + i] for i in range(4)]

    return (
        output,
        input_grad,
        vectors[0],
        vectors[1],
        qkv_grad,
        o_grad,
        vectors[2],
        vectors[3],
        wr_grad.T,
        win_grad,
        wout_grad,
    )


def solution(mesh):
    placed = (
        P(("fsdp", "heads", "tensor"), None),
        P("fsdp"),
        P("fsdp"),
        P(None, "fsdp", "heads"),
        P("heads", "fsdp"),
        P("fsdp"),
        P("fsdp"),
        P("fsdp", None),
        P(None, "fsdp", "tensor"),
        P(None, "tensor", "fsdp"),
        P(("fsdp", "heads"), None),
        P(("fsdp", "heads", "tensor"), None),
    )
    return jax.shard_map(
        local,
        mesh=mesh,
        in_specs=placed,
        out_specs=(
            P(("fsdp", "heads", "tensor"), None),
            P(("fsdp", "heads", "tensor"), None),
            P("fsdp"),
            P("fsdp"),
            P(None, "fsdp", "heads"),
            P("heads", "fsdp"),
            P("fsdp"),
            P("fsdp"),
            P("fsdp", None),
            P(None, "fsdp", "tensor"),
            P(None, "tensor", "fsdp"),
        ),
        check_vma=False,
    )
```

```python
import functools

import jax
import jax.numpy as jnp
from jax import lax
from jax.experimental import pallas as pl
from jax.experimental.pallas import tpu as pltpu
from jax.sharding import PartitionSpec as P

HD = 64
SEQ = 197
PAD = 208
ROWS = 2 * PAD
D = 512
FFT = 512
EXPERTS = 4
BF = jnp.bfloat16
F32 = jnp.float32
PACK = 528
GELU_C = 0.7978845608028654


def nn(a, b):
    return lax.dot_general(a, b, (((1,), (0,)), ((), ())), preferred_element_type=F32)


def nt(a, b):
    return lax.dot_general(a, b, (((1,), (1,)), ((), ())), preferred_element_type=F32)


def tn(a, b):
    return lax.dot_general(a, b, (((0,), (0,)), ((), ())), preferred_element_type=F32)


def params(sem=None, mib=24):
    return pltpu.CompilerParams(vmem_limit_bytes=mib * 1024 * 1024, dimension_semantics=sem)


class Place:
    def __init__(self, apart):
        self.apart = apart

    def f(self):
        return 0 if self.apart else lax.axis_index("fsdp")

    def c(self):
        return 0 if self.apart else lax.axis_index("tensor") & 1

    def t(self):
        return lax.axis_index("tensor")

    def h(self):
        return lax.axis_index("heads")


def vmem():
    return pl.BlockSpec(memory_space=pltpu.VMEM)


def sds(shape, dtype):
    return jax.ShapeDtypeStruct(shape, dtype)


def held(*shape, dtype=BF):
    return pltpu.VMEM(shape, dtype)


def skip(kernel, n_args, n_after):
    def run(*refs):
        kernel(*refs[:n_args], *refs[n_args + n_after :])

    return run


def takes(us):
    return pl.CostEstimate(flops=int(us * 230000000), transcendentals=0, bytes_accessed=0)


def call(kernel, outs, args, scratch=(), after=(), mib=16, fetch=False, us=0.2):
    spec = (lambda x: pl.BlockSpec(x.shape, lambda i: (0,) * len(x.shape))) if fetch else (lambda x: vmem())
    space = pltpu.HBM if fetch else pltpu.VMEM
    return pl.pallas_call(
        skip(kernel, len(args), len(after)),
        grid=(1,) if fetch else (),
        out_shape=outs,
        in_specs=[spec(x) for x in args] + [pl.BlockSpec(memory_space=pl.ANY)] * len(after),
        out_specs=[spec(x) for x in outs],
        scratch_shapes=list(scratch),
        cost_estimate=takes(us),
        compiler_params=params(mib=mib),
    )(*[pltpu.with_memory_space_constraint(x, space) for x in args], *after)


def pack_kernel(at, wqkv, wo, wr, g1, s1, g2, s2, out):
    c = at.c()
    rows = pl.ds(pl.multiple_of(c * 128, 128), 128)
    for i in range(3):
        out[i * 128 : (i + 1) * 128, :] = wqkv[i, rows, :]
    head = pl.ds(pl.multiple_of(c * 64, 64), 64)
    out[384:448, :] = wo[head, 0:128]
    out[448:512, :] = wo[head, 128:256]
    small = [wr[...].astype(F32)] + [r[...].reshape(1, 256).astype(F32) for r in (g1, s1, g2, s2)]
    small = jnp.concatenate(small, axis=0).astype(BF)
    out[512:520, :] = small[:, 0:128]
    out[520:528, :] = small[:, 128:256]


def copy_kernel(src, out):
    out[...] = src[...]


def gate(x, after, us=0.2):
    return call(copy_kernel, [held(*x.shape)], (x,), after=after, mib=8, us=us)[0]


def pair_kernel(own, oth, out):
    out[0] = own[...]
    out[1] = oth[...]


def weights_kernel(win, wout, out):
    for e in range(out.shape[0]):
        out[e, 0:256, :] = win[e]
        out[e, 256:512, 0:256] = wout[e, 0:256, :]
        out[e, 256:512, 256:512] = wout[e, 256:512, :]


def packed_weights(first, n, w_in, w_out, after=(), us=1.2):
    hbm = lambda x: pltpu.with_memory_space_constraint(x, pltpu.HBM)
    return pl.pallas_call(
        skip(weights_kernel, 2, len(after)),
        grid=(1,),
        out_shape=held(n, 512, 512),
        in_specs=[
            pl.BlockSpec((n, 256, 512), lambda i: (first // n, 0, 0)),
            pl.BlockSpec((n, 512, 256), lambda i: (first // n, 0, 0)),
        ]
        + [pl.BlockSpec(memory_space=pl.ANY)] * len(after),
        out_specs=vmem(),
        cost_estimate=takes(us),
        compiler_params=params(mib=8),
    )(hbm(w_in), hbm(w_out), *after)


def spread(v):
    zero = jnp.zeros((PAD - SEQ, v.shape[1]), v.dtype)
    return jnp.concatenate([v[:SEQ], zero, v[SEQ:], zero], axis=0)


def close(v):
    return jnp.concatenate([v[:SEQ], v[PAD : PAD + SEQ]], axis=0)


def pad_kernel(rows, out):
    out[...] = spread(rows[...].astype(F32)).astype(BF)


def norm_parts(x):
    center = jnp.mean(x, -1, keepdims=True)
    centered = x - center
    rstd = lax.rsqrt(jnp.mean(centered * centered, -1, keepdims=True) + 1e-06)
    return centered * rstd, rstd


def norm_back(xhat, rstd, grad, gain):
    dxhat = grad * gain
    m1 = jnp.mean(dxhat, -1, keepdims=True)
    m2 = jnp.mean(dxhat * xhat, -1, keepdims=True)
    return rstd * (dxhat - m1 - xhat * m2)


def attn_fwd_kernel(first, at, tok, *refs):
    packs, refs = (refs[0:2], refs[2:4]), refs[4:]
    if first:
        (small, n1_ref, acc_ref), refs = refs[:3], refs[3:]
    else:
        (small, n1_ref, acc_in, n2_ref, acc_ref), refs = refs[:5], refs[5:]
    kept, (qkv_ref, mix_ref, wq_ref, wo_ref), sems = refs[:4], refs[4:8], refs[8]
    copies = []

    def keep(which, j):
        src, dst = (qkv_ref, mix_ref, wq_ref, wo_ref)[which].at[j], kept[which].at[j]
        copies.append(pltpu.make_async_copy(src, dst, sems.at[which, j]))
        copies[-1].start()

    f, c = at.f(), at.c()
    if first:
        for fr in range(2):
            left = (f ^ fr) * 256
            for i in range(2):
                cols = pl.ds(pl.multiple_of(left + i * 128, 128), 128)
                small[:, cols] = packs[0][fr][0, 512 + 8 * i : 520 + 8 * i, :]
        x = tok[...].astype(F32)
        xhat, _ = norm_parts(x)
        n1 = (xhat * small[4:5, :].astype(F32) + small[5:6, :].astype(F32)).astype(BF)
        n1_ref[...] = n1
        acc = [x[0:PAD], x[PAD:ROWS]]
    else:
        n1 = n1_ref[...]
        acc = [acc_in[0:PAD, :], acc_in[PAD:ROWS, :]]
    lane = lax.broadcasted_iota(jnp.int32, (PAD, 128), 1)
    key = lax.broadcasted_iota(jnp.int32, (PAD, PAD), 1)
    for j in range(2):
        for fr in range(2):
            fa = f ^ fr
            for cr in range(2):
                ca = c ^ cr
                src = packs[cr][fr]
                rows = pl.ds(pl.multiple_of(fa * 256 + ca * 128, 128), 128)
                for i in range(3):
                    wq_ref[j, rows, i * 128 : (i + 1) * 128] = src[j, i * 128 : (i + 1) * 128, :]
                head = pl.ds(pl.multiple_of(ca * 64, 64), 64)
                for i in range(2):
                    cols = pl.ds(pl.multiple_of(fa * 256 + i * 128, 128), 128)
                    wo_ref[j, head, cols] = src[j, 384 + 64 * i : 448 + 64 * i, :]
        keep(2, j)
        keep(3, j)
        qkv_ref[j] = nn(n1, wq_ref[j]).astype(BF)
        keep(0, j)
        for im in range(2):
            r = slice(im * PAD, (im + 1) * PAD)
            q, k, v = (qkv_ref[j, r, i * 128 : (i + 1) * 128] for i in range(3))
            outs = []
            for head in range(2):
                s = nt(jnp.where(lane // HD == head, q, jnp.zeros_like(q)), k) * 0.125
                s = jnp.where(key < SEQ, s, -1e30)
                e = jnp.exp(s - jnp.max(s, -1, keepdims=True))
                p = e / jnp.sum(e, -1, keepdims=True)
                outs.append(nn(p.astype(BF), v))
            mix = jnp.where(lane < HD, outs[0], outs[1]).astype(BF)
            mix_ref[j, r, :] = mix
            acc[im] = acc[im] + nn(mix, wo_ref[j])
        keep(1, j)
    for im in range(2):
        r = slice(im * PAD, (im + 1) * PAD)
        acc_ref[r, :] = acc[im]
        if not first:
            xhat, _ = norm_parts(acc[im])
            n2_ref[r, :] = (xhat * small[6:7, :].astype(F32) + small[7:8, :].astype(F32)).astype(BF)
    for copy in copies:
        copy.wait()


def attn_bwd_kernel(first, at, *refs):
    take = lambda k: (refs[:k], refs[k:])
    if first:
        (d0, d1a, d1b, d2, resid, cot, wr_a, wr_b, small), refs = take(9)
    else:
        (dresid_in, sgrad_in, dn1_in, tok, small), refs = take(5)
    (n1, qkvs, mixes, wqs, wos, own, *sibs), refs = take(8)
    if first:
        dresid_out, sgrad, dn1_out, dqkv_s, gq_s, go_s = refs
    else:
        igrad, dqkv_s, gq_s, go_s, sgrad = refs
    f, c = at.f(), at.c()
    if first:
        dn2 = d0[...].astype(F32) + d2[...].astype(F32)
        dn2 = dn2 + jnp.concatenate([d1a[...], d1b[...]], axis=0).astype(F32)
        xhat, rstd = norm_parts(resid[...])
        sgrad[0:4, :] = (wr_a[...] + wr_b[...])[0:4]
        sgrad[4:6, :] = jnp.zeros((2, D), F32)
        sgrad[6:7, :] = jnp.sum(dn2 * xhat, 0, keepdims=True)
        sgrad[7:8, :] = jnp.sum(dn2, 0, keepdims=True)
        dresid = cot[...].astype(F32) + norm_back(xhat, rstd, dn2, small[6:7, :].astype(F32))
        dresid_out[...] = dresid
    else:
        dresid = dresid_in[...]
    dattn = dresid.astype(BF)
    lane = lax.broadcasted_iota(jnp.int32, (PAD, 128), 1)
    key = lax.broadcasted_iota(jnp.int32, (PAD, PAD), 0)
    n1t = n1[...].T
    dn1 = None if first else dn1_in[...]
    for j in range(2):
        qkv, mix, wq, wo = (ref.at[j] for ref in (qkvs, mixes, wqs, wos))
        go_s[...] = tn(mix[...], dattn).astype(BF)
        dmix = nt(dattn, wo[...]).astype(BF)
        for im in range(2):
            r = slice(im * PAD, (im + 1) * PAD)
            q, k, v = (qkv[r, i * 128 : (i + 1) * 128] for i in range(3))
            dm = dmix[r]
            dq, dk, dv = [], [], []
            for head in range(2):
                keep = lane // HD == head
                s = nt(k, jnp.where(keep, q, jnp.zeros_like(q))) * 0.125
                s = jnp.where(key < SEQ, s, -1e30)
                e = jnp.exp(s - jnp.max(s, 0, keepdims=True))
                p = e / jnp.sum(e, 0, keepdims=True)
                dp = nt(v, jnp.where(keep, dm, jnp.zeros_like(dm)))
                ds = (p * (dp - jnp.sum(p * dp, 0, keepdims=True))).astype(BF)
                dq.append(tn(ds, k))
                dk.append(nn(ds, q))
                dv.append(nn(p.astype(BF), dm))
            near = lane < HD
            dqkv_s[r, 0:128] = (jnp.where(near, dq[0], dq[1]) * 0.125).astype(BF)
            dqkv_s[r, 128:256] = (jnp.where(near, dk[0], dk[1]) * 0.125).astype(BF)
            dqkv_s[r, 256:384] = jnp.where(near, dv[0], dv[1]).astype(BF)
        dqkv = dqkv_s[...]
        gq_s[...] = nn(n1t, dqkv).astype(BF)
        part = nt(dqkv, wq[...])
        dn1 = part if dn1 is None else dn1 + part
        for fr in range(2):
            fa = f ^ fr
            for cr in range(2):
                ca = c ^ cr
                dst = (own.at[j], sibs[j])[cr]
                rows = pl.ds(pl.multiple_of(fa * 256 + ca * 128, 128), 128)
                for i in range(3):
                    dst[fr, i * 128 : (i + 1) * 128, :] = gq_s[rows, i * 128 : (i + 1) * 128]
                head = pl.ds(pl.multiple_of(ca * 64, 64), 64)
                for i in range(2):
                    cols = pl.ds(pl.multiple_of(fa * 256 + i * 128, 128), 128)
                    dst[fr, 384 + 64 * i : 448 + 64 * i, :] = go_s[head, cols]
    if first:
        dn1_out[...] = dn1
        for j in range(2):
            for fr in range(2):
                own[j, fr, 512:528, :] = jnp.zeros((16, 128), BF)
                sibs[j][fr, 512:528, :] = jnp.zeros((16, 128), BF)
        return
    xhat, rstd = norm_parts(tok[...].astype(F32))
    sgrad[...] = sgrad_in[...]
    sgrad[4:5, :] = jnp.sum(dn1 * xhat, 0, keepdims=True)
    sgrad[5:6, :] = jnp.sum(dn1, 0, keepdims=True)
    for fr in range(2):
        for cr in range(2):
            left = (f ^ fr) * 256 + (c ^ cr) * 128
            rows = sgrad[:, pl.ds(pl.multiple_of(left, 128), 128)]
            rows = jnp.concatenate([rows, jnp.zeros_like(rows)], axis=0).astype(BF)
            for j in range(2):
                (own.at[j], sibs[j])[cr][fr, 512:528, :] = rows
    grad = dresid + norm_back(xhat, rstd, dn1, small[4:5, :].astype(F32))
    igrad[...] = close(grad).astype(BF)


def out_kernel(resid, m0, m1, m2, out):
    total = resid[...] + m0[...].astype(F32) + m1[...].astype(F32) + m2[...].astype(F32)
    out[...] = close(total).astype(BF)


def assemble_kernel(at, e, own, oth, win, wout):
    f = at.f()
    for w, half in ((own, f), (oth, 1 - f)):
        half = pl.ds(pl.multiple_of(half * 256, 256), 256)
        win[half, :] = w[e, 0:256, :]
        wout[0:256, half] = w[e, 256:512, 0:256]
        wout[256:512, half] = w[e, 256:512, 256:512]


def assemble(at, e, own, oth, after=(), us=0.3):
    part, place = ((0, 0), (1, 0), (2, 0), (2, 1))[e]
    kernel = functools.partial(assemble_kernel, at, place)
    return call(kernel, [held(512, 512)] * 2, (own[part], oth[part]), after=after, mib=8, us=us)


def moe_kernel(start, end, fresh, e, base, at, x0, x1, g0, g1, win, wout, *refs):
    take = lambda k: (refs[:k], refs[k:])
    if start:
        (routes, small), refs = take(2)
    else:
        (xt, gt, gating, mix_in, dn_in, dp_in), refs = take(6)
    if end:
        (small,), refs = take(1)
    if not fresh:
        (gin_in, gout_in), refs = take(2)
    if start:
        (xt, gt, gating), refs = take(3)
    if end:
        (dn0, dn1a, dn1b, mix0, mix1, wrg), refs = take(6)
    else:
        (mix, dn, dprob), refs = take(3)
    out_a, out_b, hg_s, di_s = refs
    f = at.f()
    xs, gs = (x0, x1), (g0, g1)
    lane = lax.broadcasted_iota(jnp.int32, (ROWS, 8), 1)
    if start:
        for b in range(2):
            xt[b] = xs[b][...].T
            gt[b] = gs[b][...].T
            logits = jnp.where(lane < EXPERTS, nt(xs[b][...], small[...]), -1e30)
            ex = jnp.exp(logits - jnp.max(logits, -1, keepdims=True))
            named = routes[at.t() ^ (base + b)]
            expert = lax.broadcasted_iota(jnp.int32, (8, ROWS), 0)
            gating[b, :, 0:8] = ex / jnp.sum(ex, -1, keepdims=True)
            gating[b, :, 8:16] = jnp.where((named[0:1] == expert) | (named[1:2] == expert), 1.0, 0.0).T
    own = pl.ds(pl.multiple_of(f * 256, 256), 256)
    oth = pl.ds(pl.multiple_of((1 - f) * 256, 256), 256)
    for b in range(2):
        inner = nn(xs[b][...], win[...])
        back = nt(gs[b][...], wout[...])
        gate = gating[b, :, e : e + 1] * gating[b, :, 8 + e : 9 + e]
        square = inner * inner
        th = jnp.tanh(inner * (square * (GELU_C * 0.044715) + GELU_C))
        half = th * 0.5 + 0.5
        hidden = inner * half
        slope = half * ((1.0 - half) * (inner * (square * (6 * GELU_C * 0.044715) + 2 * GELU_C)) + 1.0)
        dp = jnp.where(lane == e, jnp.sum(hidden * back, -1, keepdims=True), 0.0)
        hg = (gate * hidden).astype(BF)
        di = ((gate * back) * slope).astype(BF)
        hg_s[b] = hg
        di_s[b] = di
        mx, dx = nn(hg, wout[...]), nt(di, win[...])
        if not start:
            dp, mx, dx = dp + dp_in[b], mx + mix_in[b], dx + dn_in[b]
        if end:
            router = gating[b, :, 0:8]
            dp = dp * gating[b, :, 8:16]
            dl = router * (dp - jnp.sum(router * dp, -1, keepdims=True))
            dl = jnp.where(lane < EXPERTS, dl, 0.0).astype(BF)
            dx = (dx + nn(dl, small[...])).astype(BF)
            if b == 0:
                dn0[...] = dx
            else:
                dn1a[...], dn1b[...] = dx[0:PAD], dx[PAD:ROWS]
            (mix0, mix1)[b][...] = mx.astype(BF)
            part = tn(dl, xs[b][...])
            wrg[...] = part if b == 0 else wrg[...] + part
        else:
            mix[b], dn[b], dprob[b] = mx, dx, dp
    if fresh:
        out_a[...] = nn(xt[0], di_s[0]) + nn(xt[1], di_s[1])
        out_b[...] = nn(gt[0], hg_s[0]) + nn(gt[1], hg_s[1])
    else:
        for dst, rows in ((out_a, own), (out_b, oth)):
            gin = gin_in[rows, :] + nn(xt[0, rows, :], di_s[0]) + nn(xt[1, rows, :], di_s[1])
            gout = gout_in[rows, :] + nn(gt[0, rows, :], hg_s[0]) + nn(gt[1, rows, :], hg_s[1])
            dst[0:256, :] = gin.astype(BF)
            dst[256:512, :] = gout.astype(BF)


def moe(e, base, at, rows, weights, state, shared, grads=(), end=False, after=(), us=3.8):
    start, fresh = not state, not grads
    routes, small = shared
    args = (*rows, *weights) + ((routes, small) if start else state) + ((small,) if end else ()) + grads
    outs = []
    if start:
        outs += [held(2, D, ROWS), held(2, D, ROWS), held(2, ROWS, 16, dtype=F32)]
    if end:
        outs += [held(ROWS, D), held(PAD, D), held(PAD, D), held(ROWS, D), held(ROWS, D), held(8, D, dtype=F32)]
    else:
        outs += [held(2, ROWS, D, dtype=F32)] * 2 + [held(2, ROWS, 8, dtype=F32)]
    outs += [held(D, FFT, dtype=F32) if fresh else held(512, 512)] * 2
    scratch = [pltpu.VMEM((2, ROWS, D), BF)] * 2
    got = call(functools.partial(moe_kernel, start, end, fresh, e, base, at), outs, args, scratch, after, 16, us=us)
    made, grads = got[:-2], got[-2:]
    if not end:
        made = tuple(made) if start else tuple(state[:3]) + tuple(made)
    return made, tuple(grads)


def rows_kernel(whole, upper, lower, out):
    out[0:PAD, :] = (whole[0:PAD, :].astype(F32) + upper[...].astype(F32)).astype(BF)
    out[PAD:ROWS, :] = (whole[PAD:ROWS, :].astype(F32) + lower[...].astype(F32)).astype(BF)


def add_kernel(a, b, out):
    out[...] = (a[...].astype(F32) + b[...].astype(F32)).astype(BF)


def add(a, b, after=(), us=0.2):
    return call(add_kernel, [held(*a.shape)], (a, b), after=after, mib=8, us=us)[0]


def mixed_kernel(at, ends, middle, out):
    h = at.h()
    out[...] = jnp.where((h == 0) | (h == 3), ends[...], middle[...])


def mixed(at, ends, middle, after=(), us=0.2):
    return call(functools.partial(mixed_kernel, at), [held(512, 512)], (ends, middle), after=after, mib=8, us=us)[0]


def finish_kernel(at, mine, given, *refs):
    win_grad, wout_grad, done = refs[-3:]
    done[...] = jnp.zeros_like(done)
    h = at.h()
    total = jnp.where((h == 0) | (h == 3), given[...], mine[...]).astype(F32)
    win_grad[0] = total[0:256, :]
    wout_grad[0] = total[256:512, :].T


def finish(at, e, mine, given, into=(), after=(), us=1.2):
    block = lambda shape: pl.BlockSpec((1,) + shape, lambda i: (e, 0, 0))
    anywhere = [pl.BlockSpec(memory_space=pl.ANY)]
    pin = lambda x: pltpu.with_memory_space_constraint(x, pltpu.VMEM)
    return pl.pallas_call(
        skip(functools.partial(finish_kernel, at), 2, len(into) + len(after)),
        grid=(1,),
        out_shape=[pltpu.HBM((EXPERTS, 256, FFT), F32), pltpu.HBM((EXPERTS, FFT, 256), F32), held(8, 128, dtype=F32)],
        in_specs=[vmem(), vmem()] + anywhere * (len(into) + len(after)),
        out_specs=[block((256, FFT)), block((FFT, 256)), vmem()],
        input_output_aliases={2: 0, 3: 1} if into else {},
        cost_estimate=takes(us),
        compiler_params=params(mib=12),
    )(pin(mine), pin(given), *[pltpu.with_memory_space_constraint(x, pltpu.HBM) for x in into], *after)


def halves_kernel(own, sib0, sib1, keep, send):
    for j in range(2):
        sib = (sib0, sib1)[j]
        keep[j] = (own[j, 0].astype(F32) + sib[0].astype(F32)).astype(BF)
        send[j] = (own[j, 1].astype(F32) + sib[1].astype(F32)).astype(BF)


def slots_kernel(keep, got, first, second):
    first[...] = (keep[0].astype(F32) + got[0].astype(F32)).astype(BF)
    second[...] = (keep[1].astype(F32) + got[1].astype(F32)).astype(BF)


def both_slots_kernel(keep, got, slot3, first, given):
    slots_kernel(keep, got, first, given.at[0])
    given[1] = slot3[...]


def cross_kernel(mine, far, got, pair, over):
    total = (mine[...].astype(F32) + got[0].astype(F32)).astype(BF)
    pair[...] = total
    over[0:512, :] = (far[0:512, :].astype(F32) + got[1, 0:512, :].astype(F32)).astype(BF)
    over[512:528, :] = total[512:528]


def unpack_kernel(at, own, sib, qkv_grad, o_grad, wr_grad, g1, s1, g2, s2):
    c = at.c()
    for src, ca in ((own, c), (sib, 1 - c)):
        rows = pl.ds(pl.multiple_of(ca * 128, 128), 128)
        for i in range(3):
            qkv_grad[i, rows, :] = src[i * 128 : (i + 1) * 128, :].astype(F32)
        head = pl.ds(pl.multiple_of(ca * 64, 64), 64)
        o_grad[head, 0:128] = src[384:448, :].astype(F32)
        o_grad[head, 128:256] = src[448:512, :].astype(F32)
        small = src[512:528, :].astype(F32)
        wr_grad[:, rows] = small[0:4]
        for i, ref in enumerate((g1, s1, g2, s2)):
            ref[:, rows] = small[4 + i : 5 + i]


def flip(x, axis, bit):
    n = lax.axis_size(axis)
    return lax.ppermute(x, axis, [(i, i ^ bit) for i in range(n)])


def core(x):
    return flip(x, "tensor", 1)


def across(x):
    return flip(x, "tensor", 2)


def other(x):
    return flip(x, "fsdp", 1)


def packs_of_whole(qkv, out, small):
    def pack(j, fr, cr):
        at = fr * 256 + cr * 128
        head = out[j * 128 + cr * 64 : j * 128 + cr * 64 + 64, fr * 256 : fr * 256 + 256]
        return jnp.concatenate(
            [qkv[i, at : at + 128, j * 128 : (j + 1) * 128] for i in range(3)]
            + [head[:, :128], head[:, 128:]]
            + [small[:, fr * 256 : fr * 256 + 128], small[:, fr * 256 + 128 : fr * 256 + 256]]
        )

    return [
        [jnp.stack([pack(2 * p + j, fr, cr) for j in range(2)]) for cr in range(2) for fr in range(2)] for p in range(2)
    ]


def whole_of_packs(packs):
    qkv, out, small = jnp.zeros((3, D, D), F32), jnp.zeros((D, D), F32), jnp.zeros((8, D), F32)
    for j in range(4):
        for cr in range(2):
            for fr in range(2):
                pack = packs[j // 2][cr][j % 2, fr].astype(F32)
                at, hd = fr * 256 + cr * 128, j * 128 + cr * 64
                qkv = qkv.at[:, at : at + 128, j * 128 : (j + 1) * 128].set(pack[:384].reshape(3, 128, 128))
                out = out.at[hd : hd + 64, fr * 256 : fr * 256 + 128].set(pack[384:448])
                out = out.at[hd : hd + 64, fr * 256 + 128 : fr * 256 + 256].set(pack[448:512])
                if j == 0:
                    small = small.at[:, at : at + 128].set(pack[512:520])
    return qkv, out, small


def forward(kernel, outs, kept, args, scratch, after, us=4.0):
    return pl.pallas_call(
        skip(kernel, len(args), len(after)),
        out_shape=outs + kept,
        in_specs=[vmem()] * len(args) + [pl.BlockSpec(memory_space=pl.ANY)] * len(after),
        out_specs=[vmem()] * len(outs) + [pl.BlockSpec(memory_space=pl.ANY)] * len(kept),
        scratch_shapes=scratch,
        cost_estimate=takes(us),
        compiler_params=params(mib=20),
    )(*[pltpu.with_memory_space_constraint(x, pltpu.VMEM) for x in args], *after)


def local(
    tokens, gain_one, shift_one, w_qkv, w_attn_out, gain_two, shift_two, w_router, w_in, w_out, routes, cotangent
):
    nf, nh = lax.axis_size("fsdp"), lax.axis_size("heads")
    near = nf == 2 and nh == 4
    f = lax.axis_index("fsdp")
    at = Place(not near)

    w_own, w_oth = [None] * 3, [None] * 3
    rows = sds((ROWS, D), BF)
    if near:
        (pack,) = call(
            functools.partial(pack_kernel, at),
            [sds((PACK, 128), BF)],
            (w_qkv, w_attn_out, w_router.T, gain_one, shift_one, gain_two, shift_two),
            fetch=True,
            us=1.1,
        )
        slots = [pack] + [flip(pack, "heads", j) for j in range(1, 4)]
        w_own[0] = packed_weights(0, 1, w_in, w_out, after=(pack,), us=10)
        w_oth[0] = other(w_own[0])
        (tok,) = call(pad_kernel, [rows], (tokens,), after=(w_own[0],), fetch=True, us=6)
        pair = lambda a, b, after, us=0.2: call(pair_kernel, [held(2, PACK, 128)], (a, b), after=after, mib=8, us=us)[0]
        before = (tok,)
        w_own[1] = packed_weights(1, 1, w_in, w_out, after=(tok,))
        w_oth[1] = other(w_own[1])
        pair_b = pair(slots[2], slots[3], (w_own[1],))
        w_own[2] = packed_weights(2, 2, w_in, w_out, after=(pair_b,), us=1.5)
        w_oth[2] = other(w_own[2])
        (cot0,) = call(pad_kernel, [rows], (cotangent,), after=(w_own[2],), fetch=True, us=1.1)
        far = [other(slots[0]), other(slots[1])]
        far = [gate(far[0], (cot0, w_oth[0])), gate(far[1], (cot0,))]
        far_b = other(pair_b)
        pair_a = pair(slots[0], slots[1], (far[0],))
        far_a = pair(far[0], far[1], (pair_a,), 1.5)
        sib_a = pair(core(slots[0]), core(slots[1]), (far_a,))
        sib_far = pair(core(far[0]), core(far[1]), (sib_a,))
        packs = [[pair_a, far_a, sib_a, sib_far]]
        before = ()
    else:
        small_own = jnp.concatenate([w_router.T, jnp.stack([gain_one, shift_one, gain_two, shift_two])])
        small = lax.all_gather(small_own, "fsdp", axis=1, tiled=True)
        qkv_all = lax.all_gather(lax.all_gather(w_qkv, "fsdp", axis=1, tiled=True), "heads", axis=2, tiled=True)
        out_all = lax.all_gather(lax.all_gather(w_attn_out, "fsdp", axis=1, tiled=True), "heads", axis=0, tiled=True)
        packs = packs_of_whole(qkv_all, out_all, small)
        in_all = lax.all_gather(w_in, "fsdp", axis=1, tiled=True)
        o_all = lax.all_gather(w_out, "fsdp", axis=2, tiled=True)
        for i, (first, n) in enumerate(((0, 1), (1, 1), (2, 2))):
            w_own[i] = packed_weights(first, n, in_all[:, :256], o_all[:, :, :256])
            w_oth[i] = packed_weights(first, n, in_all[:, 256:], o_all[:, :, 256:])
        (tok,) = call(pad_kernel, [rows], (tokens,), fetch=True)
        (cot0,) = call(pad_kernel, [rows], (cotangent,), fetch=True)
        before = ()

    named = jnp.pad(routes.T.reshape(2, 8, SEQ), ((0, 0), (0, 0), (0, PAD - SEQ)), constant_values=-1)
    named = named.reshape(2, 4, ROWS).transpose(1, 0, 2)

    kept = [pltpu.HBM(shape, BF) for shape in ((2, ROWS, 384), (2, ROWS, 128), (2, D, 384), (2, 128, D))]
    scratch = [pltpu.VMEM(x.shape, BF) for x in kept] + [pltpu.SemaphoreType.DMA((4, 2))]
    small, n1, acc, qkv_a, mix_a, wq_a, wo_a = forward(
        functools.partial(attn_fwd_kernel, True, at),
        [held(8, D), held(ROWS, D), held(ROWS, D, dtype=F32)],
        kept,
        (tok, *packs[0]),
        scratch,
        before,
    )
    cot1, cot2 = core(cot0), across(cot0)
    before = (cot1,)
    if near:
        far_b = gate(far_b, (n1,), 2.2)
        before = (cot1,)
        packs.append([pair_b, far_b, core(pair_b), core(far_b)])
    n2_0, resid, qkv_b, mix_b, wq_b, wo_b = forward(
        functools.partial(attn_fwd_kernel, False, at),
        [held(ROWS, D), held(ROWS, D, dtype=F32)],
        kept,
        (tok, *packs[1], small, n1, acc),
        scratch,
        before,
        5.5,
    )
    n2_1, n2_2 = core(n2_0), across(n2_0)

    shared = (named, small)
    rows_a = (n2_0, n2_1, cot0, cot1)
    cot2 = gate(cot2, (n2_0,))
    weights = [assemble(at, 0, w_own, w_oth, (cot2,), 2)]
    state_a, grads0 = moe(0, 0, at, rows_a, weights[0], (), shared)
    weights.append(assemble(at, 1, w_own, w_oth, grads0[:1]))
    state_a, grads1 = moe(1, 0, at, rows_a, weights[1], state_a, shared, us=4)
    n2_2 = gate(n2_2, grads1[:1], 0.8)
    rows_b = (n2_2, core(n2_2), cot2, core(cot2))
    state_b, (keep0, send0) = moe(0, 2, at, rows_b, weights[0], (), shared, grads0)
    state_b, (keep1, send1) = moe(1, 2, at, rows_b, weights[1], state_b, shared, grads1)
    weights.append(assemble(at, 2, w_own, w_oth, (keep1,)))
    state_a, grads2 = moe(2, 0, at, rows_a, weights[2], state_a, shared)
    weights.append(assemble(at, 3, w_own, w_oth, grads2[:1], 1.0))
    state_b, (keep2, send2) = moe(2, 2, at, rows_b, weights[2], state_b, shared, grads2, after=weights[3])
    ones, twos, threes, before = [None] * 4, [None] * 4, [None] * 4, ()
    if near:
        got0 = other(send0)
        ones[0] = add(keep0, got0, after=(keep2,), us=2)
        before = (ones[0],)
    (d2, *d3, m2, m3, wr_b), grads3 = moe(
        3, 2, at, rows_b, weights[3], state_b, shared, end=True, after=before, us=5
    )
    (d_sum,) = call(rows_kernel, [held(ROWS, D)], (d2, core(d3[0]), core(d3[1])), after=grads3[:1], us=1.2)
    d_far = across(d_sum)
    before = (d_sum,)
    if near:
        got1 = other(send1)
        ones[1] = add(keep1, got1, after=before, us=1.5)
        before = (ones[1],)
    (d0, *d1, m0, m1, wr_a), (keep3, send3) = moe(
        3, 0, at, rows_a, weights[3], state_a, shared, grads3, True, before, us=5
    )
    keeps, sends = (keep0, keep1, keep2, keep3), (send0, send1, send2, send3)
    d_near = [core(d) for d in d1]
    inward = lambda x: lax.ppermute(x, "heads", [(0, 1), (3, 2)])
    middle = lambda x: lax.ppermute(x, "heads", [(1, 2), (2, 1)])
    outward = lambda x: lax.ppermute(x, "heads", [(1, 0), (2, 3)])
    before = ()
    if near:
        got = [got0, got1] + [other(send) for send in sends[2:]]
        twos[0] = add(ones[0], inward(ones[0]), after=(keep3,), us=4.3)
        before = (twos[0],)

    scratch = [pltpu.VMEM((ROWS, 384), BF), pltpu.VMEM((D, 384), BF), pltpu.VMEM((128, D), BF)]
    both = [held(2, 2, PACK, 128)] + [held(2, PACK, 128)] * 2
    own_b, sib_2, sib_3, dresid, sgrad, dn1 = call(
        functools.partial(attn_bwd_kernel, True, at),
        both + [held(ROWS, D, dtype=F32), held(8, D, dtype=F32), held(ROWS, D, dtype=F32)],
        (d0, *d_near, d_far, resid, cot0, wr_a, wr_b, small, n1, qkv_b, mix_b, wq_b, wo_b),
        scratch,
        after=before,
        us=6.2,
    )
    if near:
        ones[2] = add(keeps[2], got[2], after=(dn1,), us=1.5)
        keep_b, send_b = call(
            halves_kernel, [held(2, PACK, 128)] * 2, (own_b, core(sib_2), core(sib_3)), after=(ones[2],), us=1.5
        )
        twos[1] = add(ones[1], inward(ones[1]), after=(keep_b,), us=1)
        threes[0] = add(twos[0], middle(twos[0]), after=(twos[1],), us=0.3)
        both_ways = mixed(at, ones[2], threes[0], us=1.5)
        neighbour0 = flip(both_ways, "heads", 1)
        ones[3] = add(keeps[3], got[3], after=(both_ways,), us=0.3)
        before = (ones[3],)
    own_a, sib_0, sib_1, input_grad = call(
        functools.partial(attn_bwd_kernel, False, at),
        both + [sds((SEQ * 2, D), BF)],
        (dresid, sgrad, dn1, tok, small, n1, qkv_a, mix_a, wq_a, wo_a),
        scratch + [pltpu.VMEM((8, D), F32)],
        after=before,
        us=8.2,
    )

    if near:
        one_pack = held(PACK, 128)
        slot2, slot3 = call(slots_kernel, [one_pack] * 2, (keep_b, other(send_b)), after=(own_a,))
        keep_a, send_a = call(
            halves_kernel, [held(2, PACK, 128)] * 2, (own_a, core(sib_0), core(sib_1)), after=(slot3,), us=1.5
        )
        threes[1] = add(twos[1], middle(twos[1]), after=(keep_a,), us=0.3)
        both_ways = mixed(at, ones[3], threes[1], us=2)
        neighbour1 = flip(both_ways, "heads", 1)
        twos[2] = add(ones[2], neighbour0, after=(both_ways,), us=2)
        *grads, done = finish(at, 0, threes[0], neighbour0, after=(twos[2],), us=2)
        slot0, given = call(
            both_slots_kernel, [one_pack, held(2, PACK, 128)], (keep_a, other(send_a), slot3), after=(done,), us=4
        )
        twos[3] = add(ones[3], neighbour1, after=(given,), us=0.3)
        *grads, done = finish(at, 1, threes[1], neighbour1, grads, after=(twos[3],), us=1.2)
        threes[2] = add(twos[2], middle(twos[2]), after=(done,), us=3)
        pair, over = call(
            cross_kernel, [one_pack] * 2, (slot0, slot2, flip(given, "heads", 1)), after=(threes[2],), us=1.5
        )
        threes[3] = add(twos[3], middle(twos[3]), after=(pair,), us=2)
        m_near = core(m1)
        m_sum = add(m2, core(m3), after=(threes[3],), us=5)
        m_far = across(m_sum)
        half = add(pair, flip(over, "heads", 2), after=(m_sum,))
        *grads, done = finish(at, 2, threes[2], outward(threes[2]), grads, after=(half,), us=6)
        half = add(half, across(half), after=(done,), us=2)
        vector = sds((1, 256), F32)
        qkv_grad, o_grad, wr_grad, *vectors = call(
            functools.partial(unpack_kernel, at),
            [sds((3, 256, 128), F32), sds((128, 256), F32), sds((4, 256), F32)] + [vector] * 4,
            (half, core(half)),
        )
        (output,) = call(out_kernel, [sds((SEQ * 2, D), BF)], (resid, m0, m_near, m_far), after=(half,))
        win_grad, wout_grad, _ = finish(at, 3, threes[3], outward(threes[3]), grads, after=(half,))
        vectors = [v.reshape(256) for v in vectors]
    else:
        m_near = core(m1)
        m_far = across(add(m2, core(m3)))
        (output,) = call(out_kernel, [sds((SEQ * 2, D), BF)], (resid, m0, m_near, m_far))
        keep, send = jnp.stack(keeps), jnp.stack(sends)
        gin = jnp.concatenate([keep[:, :256], send[:, :256]], 1)
        gout = jnp.concatenate([keep[:, 256:], send[:, 256:]], 1).transpose(0, 2, 1)
        win_grad = lax.psum_scatter(gin, "fsdp", scatter_dimension=1, tiled=True)
        wout_grad = lax.psum_scatter(gout, "fsdp", scatter_dimension=2, tiled=True)
        win_grad = lax.psum(win_grad, "heads").astype(F32)
        wout_grad = lax.psum(wout_grad, "heads").astype(F32)
        qkv_grad, o_grad, sgrad = whole_of_packs(((own_a, jnp.stack([sib_0, sib_1])), (own_b, jnp.stack([sib_2, sib_3]))))
        qkv_grad = lax.psum_scatter(qkv_grad, "fsdp", scatter_dimension=1, tiled=True)
        qkv_grad = lax.psum_scatter(qkv_grad, "heads", scatter_dimension=2, tiled=True)
        qkv_grad = lax.psum(qkv_grad, "tensor")
        o_grad = lax.psum_scatter(o_grad, "fsdp", scatter_dimension=1, tiled=True)
        o_grad = lax.psum_scatter(o_grad, "heads", scatter_dimension=0, tiled=True)
        o_grad = lax.psum(o_grad, "tensor")
        sgrad = lax.psum(sgrad, ("fsdp", "heads", "tensor"))
        sgrad = lax.dynamic_slice_in_dim(sgrad, f * gain_one.shape[0], gain_one.shape[0], 1)
        wr_grad, vectors = sgrad[0:4], [sgrad[4 + i] for i in range(4)]

    return (
        output,
        input_grad,
        vectors[0],
        vectors[1],
        qkv_grad,
        o_grad,
        vectors[2],
        vectors[3],
        wr_grad.T,
        win_grad,
        wout_grad,
    )


def solution(mesh):
    placed = (
        P(("fsdp", "heads", "tensor"), None),
        P("fsdp"),
        P("fsdp"),
        P(None, "fsdp", "heads"),
        P("heads", "fsdp"),
        P("fsdp"),
        P("fsdp"),
        P("fsdp", None),
        P(None, "fsdp", "tensor"),
        P(None, "tensor", "fsdp"),
        P(("fsdp", "heads"), None),
        P(("fsdp", "heads", "tensor"), None),
    )
    return jax.shard_map(
        local,
        mesh=mesh,
        in_specs=placed,
        out_specs=(
            P(("fsdp", "heads", "tensor"), None),
            P(("fsdp", "heads", "tensor"), None),
            P("fsdp"),
            P("fsdp"),
            P(None, "fsdp", "heads"),
            P("heads", "fsdp"),
            P("fsdp"),
            P("fsdp"),
            P("fsdp", None),
            P(None, "fsdp", "tensor"),
            P(None, "tensor", "fsdp"),
        ),
        check_vma=False,
    )
```

```python
import functools

import jax
import jax.numpy as jnp
from jax import lax
from jax.experimental import pallas as pl
from jax.experimental.pallas import tpu as pltpu
from jax.sharding import PartitionSpec as P

HD = 64
SEQ = 197
PAD = 208
ROWS = 2 * PAD
D = 512
FFT = 512
EXPERTS = 4
BF = jnp.bfloat16
F32 = jnp.float32
PACK = 528
GELU_C = 0.7978845608028654


def nn(a, b):
    return lax.dot_general(a, b, (((1,), (0,)), ((), ())), preferred_element_type=F32)


def nt(a, b):
    return lax.dot_general(a, b, (((1,), (1,)), ((), ())), preferred_element_type=F32)


def tn(a, b):
    return lax.dot_general(a, b, (((0,), (0,)), ((), ())), preferred_element_type=F32)


def params(sem=None, mib=24):
    return pltpu.CompilerParams(vmem_limit_bytes=mib * 1024 * 1024, dimension_semantics=sem)


class Place:
    def __init__(self, apart):
        self.apart = apart

    def f(self):
        return 0 if self.apart else lax.axis_index("fsdp")

    def c(self):
        return 0 if self.apart else lax.axis_index("tensor") & 1

    def t(self):
        return lax.axis_index("tensor")

    def h(self):
        return lax.axis_index("heads")


def vmem():
    return pl.BlockSpec(memory_space=pltpu.VMEM)


def sds(shape, dtype):
    return jax.ShapeDtypeStruct(shape, dtype)


def held(*shape, dtype=BF):
    return pltpu.VMEM(shape, dtype)


def skip(kernel, n_args, n_after):
    def run(*refs):
        kernel(*refs[:n_args], *refs[n_args + n_after :])

    return run


def takes(us):
    return pl.CostEstimate(flops=int(us * 230000000), transcendentals=0, bytes_accessed=0)


def call(kernel, outs, args, scratch=(), after=(), mib=16, fetch=False, us=0.2):
    spec = (lambda x: pl.BlockSpec(x.shape, lambda i: (0,) * len(x.shape))) if fetch else (lambda x: vmem())
    space = pltpu.HBM if fetch else pltpu.VMEM
    return pl.pallas_call(
        skip(kernel, len(args), len(after)),
        grid=(1,) if fetch else (),
        out_shape=outs,
        in_specs=[spec(x) for x in args] + [pl.BlockSpec(memory_space=pl.ANY)] * len(after),
        out_specs=[spec(x) for x in outs],
        scratch_shapes=list(scratch),
        cost_estimate=takes(us),
        compiler_params=params(mib=mib),
    )(*[pltpu.with_memory_space_constraint(x, space) for x in args], *after)


def pack_kernel(at, wqkv, wo, wr, g1, s1, g2, s2, out):
    c = at.c()
    rows = pl.ds(pl.multiple_of(c * 128, 128), 128)
    for i in range(3):
        out[i * 128 : (i + 1) * 128, :] = wqkv[i, rows, :]
    head = pl.ds(pl.multiple_of(c * 64, 64), 64)
    out[384:448, :] = wo[head, 0:128]
    out[448:512, :] = wo[head, 128:256]
    small = [wr[...].astype(F32)] + [r[...].reshape(1, 256).astype(F32) for r in (g1, s1, g2, s2)]
    small = jnp.concatenate(small, axis=0).astype(BF)
    out[512:520, :] = small[:, 0:128]
    out[520:528, :] = small[:, 128:256]


def copy_kernel(src, out):
    out[...] = src[...]


def gate(x, after, us=0.2):
    return call(copy_kernel, [held(*x.shape)], (x,), after=after, mib=8, us=us)[0]


def pair_kernel(own, oth, out):
    out[0] = own[...]
    out[1] = oth[...]


def weights_kernel(win, wout, out):
    for e in range(out.shape[0]):
        out[e, 0:256, :] = win[e]
        out[e, 256:512, 0:256] = wout[e, 0:256, :]
        out[e, 256:512, 256:512] = wout[e, 256:512, :]


def packed_weights(first, n, w_in, w_out, after=(), us=1.2):
    hbm = lambda x: pltpu.with_memory_space_constraint(x, pltpu.HBM)
    return pl.pallas_call(
        skip(weights_kernel, 2, len(after)),
        grid=(1,),
        out_shape=held(n, 512, 512),
        in_specs=[
            pl.BlockSpec((n, 256, 512), lambda i: (first // n, 0, 0)),
            pl.BlockSpec((n, 512, 256), lambda i: (first // n, 0, 0)),
        ]
        + [pl.BlockSpec(memory_space=pl.ANY)] * len(after),
        out_specs=vmem(),
        cost_estimate=takes(us),
        compiler_params=params(mib=8),
    )(hbm(w_in), hbm(w_out), *after)


def spread(v):
    zero = jnp.zeros((PAD - SEQ, v.shape[1]), v.dtype)
    return jnp.concatenate([v[:SEQ], zero, v[SEQ:], zero], axis=0)


def close(v):
    return jnp.concatenate([v[:SEQ], v[PAD : PAD + SEQ]], axis=0)


def pad_kernel(rows, out):
    out[...] = spread(rows[...].astype(F32)).astype(BF)


def norm_parts(x):
    center = jnp.mean(x, -1, keepdims=True)
    centered = x - center
    rstd = lax.rsqrt(jnp.mean(centered * centered, -1, keepdims=True) + 1e-06)
    return centered * rstd, rstd


def norm_back(xhat, rstd, grad, gain):
    dxhat = grad * gain
    m1 = jnp.mean(dxhat, -1, keepdims=True)
    m2 = jnp.mean(dxhat * xhat, -1, keepdims=True)
    return rstd * (dxhat - m1 - xhat * m2)


def attn_fwd_kernel(first, at, tok, *refs):
    packs, refs = (refs[0:2], refs[2:4]), refs[4:]
    if first:
        (small, n1_ref, acc_ref), refs = refs[:3], refs[3:]
    else:
        (small, n1_ref, acc_in, n2_ref, acc_ref), refs = refs[:5], refs[5:]
    kept, (qkv_ref, mix_ref, wq_ref, wo_ref), sems = refs[:4], refs[4:8], refs[8]

    def keep(which, j):
        src, dst = (qkv_ref, mix_ref, wq_ref, wo_ref)[which].at[j], kept[which].at[j]
        return pltpu.make_async_copy(src, dst, sems.at[which, j])

    f, c = at.f(), at.c()
    if first:
        for fr in range(2):
            left = (f ^ fr) * 256
            for i in range(2):
                cols = pl.ds(pl.multiple_of(left + i * 128, 128), 128)
                small[:, cols] = packs[0][fr][0, 512 + 8 * i : 520 + 8 * i, :]
        x = tok[...].astype(F32)
        xhat, _ = norm_parts(x)
        n1 = (xhat * small[4:5, :].astype(F32) + small[5:6, :].astype(F32)).astype(BF)
        n1_ref[...] = n1
        acc_ref[...] = x
    else:
        acc_ref[...] = acc_in[...]
    lane = lax.broadcasted_iota(jnp.int32, (PAD, 128), 1)
    key = lax.broadcasted_iota(jnp.int32, (PAD, PAD), 1)

    def slot(j, carry):
        for fr in range(2):
            fa = f ^ fr
            for cr in range(2):
                ca = c ^ cr
                src = packs[cr][fr]
                rows = pl.ds(pl.multiple_of(fa * 256 + ca * 128, 128), 128)
                for i in range(3):
                    wq_ref[j, rows, i * 128 : (i + 1) * 128] = src[j, i * 128 : (i + 1) * 128, :]
                head = pl.ds(pl.multiple_of(ca * 64, 64), 64)
                for i in range(2):
                    cols = pl.ds(pl.multiple_of(fa * 256 + i * 128, 128), 128)
                    wo_ref[j, head, cols] = src[j, 384 + 64 * i : 448 + 64 * i, :]
        keep(2, j).start()
        keep(3, j).start()
        qkv_ref[j] = nn(n1_ref[...], wq_ref[j]).astype(BF)
        keep(0, j).start()
        for im in range(2):
            r = slice(im * PAD, (im + 1) * PAD)
            q, k, v = (qkv_ref[j, r, i * 128 : (i + 1) * 128] for i in range(3))
            outs = []
            for head in range(2):
                s = nt(jnp.where(lane // HD == head, q, jnp.zeros_like(q)), k) * 0.125
                s = jnp.where(key < SEQ, s, -1e30)
                e = jnp.exp(s - jnp.max(s, -1, keepdims=True))
                p = e / jnp.sum(e, -1, keepdims=True)
                outs.append(nn(p.astype(BF), v))
            mix = jnp.where(lane < HD, outs[0], outs[1]).astype(BF)
            mix_ref[j, r, :] = mix
            acc_ref[r, :] += nn(mix, wo_ref[j])
        keep(1, j).start()
        return carry

    lax.fori_loop(0, 2, slot, 0)
    if not first:
        for im in range(2):
            r = slice(im * PAD, (im + 1) * PAD)
            xhat, _ = norm_parts(acc_ref[r, :])
            n2_ref[r, :] = (xhat * small[6:7, :].astype(F32) + small[7:8, :].astype(F32)).astype(BF)
    for which in range(4):
        for j in range(2):
            keep(which, j).wait()


def attn_bwd_kernel(first, at, *refs):
    take = lambda k: (refs[:k], refs[k:])
    if first:
        (d0, d1a, d1b, d2, resid, cot, wr_a, wr_b, small), refs = take(9)
    else:
        (dresid_in, sgrad_in, dn1_in, tok, small), refs = take(5)
    (n1, qkvs, mixes, wqs, wos, own, *sibs), refs = take(8)
    if first:
        dresid_out, sgrad, dn1_s, dqkv_s, gq_s, go_s, n1t_s, dattn_s = refs
    else:
        igrad, dqkv_s, gq_s, go_s, n1t_s, dattn_s, sgrad, dn1_s = refs
    f, c = at.f(), at.c()
    if first:
        dn2 = d0[...].astype(F32) + d2[...].astype(F32)
        dn2 = dn2 + jnp.concatenate([d1a[...], d1b[...]], axis=0).astype(F32)
        xhat, rstd = norm_parts(resid[...])
        sgrad[0:4, :] = (wr_a[...] + wr_b[...])[0:4]
        sgrad[4:6, :] = jnp.zeros((2, D), F32)
        sgrad[6:7, :] = jnp.sum(dn2 * xhat, 0, keepdims=True)
        sgrad[7:8, :] = jnp.sum(dn2, 0, keepdims=True)
        dresid = cot[...].astype(F32) + norm_back(xhat, rstd, dn2, small[6:7, :].astype(F32))
        dresid_out[...] = dresid
    else:
        dresid = dresid_in[...]
    dattn_s[...] = dresid.astype(BF)
    lane = lax.broadcasted_iota(jnp.int32, (PAD, 128), 1)
    key = lax.broadcasted_iota(jnp.int32, (PAD, PAD), 0)
    n1t_s[...] = n1[...].T
    dn1_s[...] = jnp.zeros_like(dn1_s) if first else dn1_in[...]

    def slot(j, carry):
        qkv, mix, wq, wo = (ref.at[j] for ref in (qkvs, mixes, wqs, wos))
        go_s[...] = tn(mix[...], dattn_s[...]).astype(BF)
        dmix = nt(dattn_s[...], wo[...]).astype(BF)
        for im in range(2):
            r = slice(im * PAD, (im + 1) * PAD)
            q, k, v = (qkv[r, i * 128 : (i + 1) * 128] for i in range(3))
            dm = dmix[r]
            dq, dk, dv = [], [], []
            for head in range(2):
                keep = lane // HD == head
                s = nt(k, jnp.where(keep, q, jnp.zeros_like(q))) * 0.125
                s = jnp.where(key < SEQ, s, -1e30)
                e = jnp.exp(s - jnp.max(s, 0, keepdims=True))
                p = e / jnp.sum(e, 0, keepdims=True)
                dp = nt(v, jnp.where(keep, dm, jnp.zeros_like(dm)))
                ds = (p * (dp - jnp.sum(p * dp, 0, keepdims=True))).astype(BF)
                dq.append(tn(ds, k))
                dk.append(nn(ds, q))
                dv.append(nn(p.astype(BF), dm))
            near = lane < HD
            dqkv_s[r, 0:128] = (jnp.where(near, dq[0], dq[1]) * 0.125).astype(BF)
            dqkv_s[r, 128:256] = (jnp.where(near, dk[0], dk[1]) * 0.125).astype(BF)
            dqkv_s[r, 256:384] = jnp.where(near, dv[0], dv[1]).astype(BF)
        dqkv = dqkv_s[...]
        gq_s[...] = nn(n1t_s[...], dqkv).astype(BF)
        dn1_s[...] += nt(dqkv, wq[...])
        for cr, dst, only in ((0, own.at[j], None), (1, sibs[0], 0), (1, sibs[1], 1)):

            def fill():
                for fr in range(2):
                    fa, ca = f ^ fr, c ^ cr
                    rows = pl.ds(pl.multiple_of(fa * 256 + ca * 128, 128), 128)
                    for i in range(3):
                        dst[fr, i * 128 : (i + 1) * 128, :] = gq_s[rows, i * 128 : (i + 1) * 128]
                    head = pl.ds(pl.multiple_of(ca * 64, 64), 64)
                    for i in range(2):
                        cols = pl.ds(pl.multiple_of(fa * 256 + i * 128, 128), 128)
                        dst[fr, 384 + 64 * i : 448 + 64 * i, :] = go_s[head, cols]

            if only is None:
                fill()
            else:
                pl.when(j == only)(fill)
        return carry

    lax.fori_loop(0, 2, slot, 0)
    if first:
        for j in range(2):
            for fr in range(2):
                own[j, fr, 512:528, :] = jnp.zeros((16, 128), BF)
                sibs[j][fr, 512:528, :] = jnp.zeros((16, 128), BF)
        return
    dn1 = dn1_s[...]
    xhat, rstd = norm_parts(tok[...].astype(F32))
    sgrad[...] = sgrad_in[...]
    sgrad[4:5, :] = jnp.sum(dn1 * xhat, 0, keepdims=True)
    sgrad[5:6, :] = jnp.sum(dn1, 0, keepdims=True)
    for fr in range(2):
        for cr in range(2):
            left = (f ^ fr) * 256 + (c ^ cr) * 128
            rows = sgrad[:, pl.ds(pl.multiple_of(left, 128), 128)]
            rows = jnp.concatenate([rows, jnp.zeros_like(rows)], axis=0).astype(BF)
            for j in range(2):
                (own.at[j], sibs[j])[cr][fr, 512:528, :] = rows
    grad = dresid + norm_back(xhat, rstd, dn1, small[4:5, :].astype(F32))
    igrad[...] = close(grad).astype(BF)


def out_kernel(resid, m0, m1, m2, out):
    total = resid[...] + m0[...].astype(F32) + m1[...].astype(F32) + m2[...].astype(F32)
    out[...] = close(total).astype(BF)


def assemble_kernel(at, e, own, oth, win, wout):
    f = at.f()
    for w, half in ((own, f), (oth, 1 - f)):
        half = pl.ds(pl.multiple_of(half * 256, 256), 256)
        win[half, :] = w[e, 0:256, :]
        wout[0:256, half] = w[e, 256:512, 0:256]
        wout[256:512, half] = w[e, 256:512, 256:512]


def assemble(at, e, own, oth, after=(), us=0.3):
    part, place = ((0, 0), (1, 0), (2, 0), (2, 1))[e]
    kernel = functools.partial(assemble_kernel, at, place)
    return call(kernel, [held(512, 512)] * 2, (own[part], oth[part]), after=after, mib=8, us=us)


def moe_kernel(start, end, fresh, e, base, at, win, wout, *refs):
    take = lambda k: (refs[:k], refs[k:])
    if start:
        (x0, x1, g0, g1, routes, small), refs = take(6)
    else:
        (xs, gs, xt, gt, gating, mix_in, dn_in, dp_in), refs = take(8)
    if end:
        (small,), refs = take(1)
    if not fresh:
        (gin_in, gout_in), refs = take(2)
    if start:
        (xs, gs, xt, gt, gating), refs = take(5)
    if end:
        (dn0, dn1a, dn1b, mix0, mix1, wrg), refs = take(6)
    else:
        (mix, dn, dprob), refs = take(3)
    out_a, out_b, hg_s, di_s = refs[:4]
    if end:
        mix, dn = refs[4:]
        wrg[...] = jnp.zeros_like(wrg)
    f = at.f()
    if start:
        xs[0], xs[1], gs[0], gs[1] = x0[...], x1[...], g0[...], g1[...]
    own = pl.ds(pl.multiple_of(f * 256, 256), 256)
    oth = pl.ds(pl.multiple_of((1 - f) * 256, 256), 256)

    def rows(b, carry):
        lane = lax.broadcasted_iota(jnp.int32, (ROWS, 8), 1)
        if start:
            xt[b] = xs[b].T
            gt[b] = gs[b].T
            logits = jnp.where(lane < EXPERTS, nt(xs[b], small[...]), -1e30)
            ex = jnp.exp(logits - jnp.max(logits, -1, keepdims=True))
            named = routes[at.t() ^ (base + b)]
            expert = lax.broadcasted_iota(jnp.int32, (8, ROWS), 0)
            gating[b, :, 0:8] = ex / jnp.sum(ex, -1, keepdims=True)
            gating[b, :, 8:16] = jnp.where((named[0:1] == expert) | (named[1:2] == expert), 1.0, 0.0).T
        inner = nn(xs[b], win[...])
        back = nt(gs[b], wout[...])
        gate = gating[b, :, e : e + 1] * gating[b, :, 8 + e : 9 + e]
        square = inner * inner
        th = jnp.tanh(inner * (square * (GELU_C * 0.044715) + GELU_C))
        half = th * 0.5 + 0.5
        hidden = inner * half
        slope = half * ((1.0 - half) * (inner * (square * (6 * GELU_C * 0.044715) + 2 * GELU_C)) + 1.0)
        dp = jnp.where(lane == e, jnp.sum(hidden * back, -1, keepdims=True), 0.0)
        hg = (gate * hidden).astype(BF)
        di = ((gate * back) * slope).astype(BF)
        hg_s[b] = hg
        di_s[b] = di
        mx, dx = nn(hg, wout[...]), nt(di, win[...])
        if not start:
            dp, mx, dx = dp + dp_in[b], mx + mix_in[b], dx + dn_in[b]
        if end:
            router = gating[b, :, 0:8]
            dp = dp * gating[b, :, 8:16]
            dl = router * (dp - jnp.sum(router * dp, -1, keepdims=True))
            dl = jnp.where(lane < EXPERTS, dl, 0.0).astype(BF)
            dn[b] = (dx + nn(dl, small[...])).astype(BF)
            mix[b] = mx.astype(BF)
            wrg[...] += tn(dl, xs[b])
        else:
            mix[b], dn[b], dprob[b] = mx, dx, dp
        return carry

    lax.fori_loop(0, 2, rows, 0)
    if end:
        dn0[...], dn1a[...], dn1b[...] = dn[0], dn[1, 0:PAD], dn[1, PAD:ROWS]
        mix0[...], mix1[...] = mix[0], mix[1]
    if fresh:
        out_a[...] = nn(xt[0], di_s[0]) + nn(xt[1], di_s[1])
        out_b[...] = nn(gt[0], hg_s[0]) + nn(gt[1], hg_s[1])
    else:
        for dst, half in ((out_a, own), (out_b, oth)):
            gin = gin_in[half, :] + nn(xt[0, half, :], di_s[0]) + nn(xt[1, half, :], di_s[1])
            gout = gout_in[half, :] + nn(gt[0, half, :], hg_s[0]) + nn(gt[1, half, :], hg_s[1])
            dst[0:256, :] = gin.astype(BF)
            dst[256:512, :] = gout.astype(BF)


def moe(e, base, at, rows, weights, state, shared, grads=(), end=False, after=(), us=3.8):
    start, fresh = not state, not grads
    routes, small = shared
    args = tuple(weights) + ((*rows, routes, small) if start else state) + ((small,) if end else ()) + grads
    outs = []
    if start:
        outs += [held(2, ROWS, D)] * 2 + [held(2, D, ROWS)] * 2 + [held(2, ROWS, 16, dtype=F32)]
    if end:
        outs += [held(ROWS, D), held(PAD, D), held(PAD, D), held(ROWS, D), held(ROWS, D), held(8, D, dtype=F32)]
    else:
        outs += [held(2, ROWS, D, dtype=F32)] * 2 + [held(2, ROWS, 8, dtype=F32)]
    outs += [held(D, FFT, dtype=F32) if fresh else held(512, 512)] * 2
    scratch = [pltpu.VMEM((2, ROWS, D), BF)] * (4 if end else 2)
    got = call(functools.partial(moe_kernel, start, end, fresh, e, base, at), outs, args, scratch, after, 16, us=us)
    made, grads = got[:-2], got[-2:]
    if not end:
        made = tuple(made) if start else tuple(state[:5]) + tuple(made)
    return made, tuple(grads)


def rows_kernel(whole, upper, lower, out):
    out[0:PAD, :] = (whole[0:PAD, :].astype(F32) + upper[...].astype(F32)).astype(BF)
    out[PAD:ROWS, :] = (whole[PAD:ROWS, :].astype(F32) + lower[...].astype(F32)).astype(BF)


def add_kernel(a, b, out):
    out[...] = (a[...].astype(F32) + b[...].astype(F32)).astype(BF)


def add(a, b, after=(), us=0.2):
    return call(add_kernel, [held(*a.shape)], (a, b), after=after, mib=8, us=us)[0]


def mixed_kernel(at, ends, middle, out):
    h = at.h()
    out[...] = jnp.where((h == 0) | (h == 3), ends[...], middle[...])


def mixed(at, ends, middle, after=(), us=0.2):
    return call(functools.partial(mixed_kernel, at), [held(512, 512)], (ends, middle), after=after, mib=8, us=us)[0]


def finish_kernel(at, mine, given, *refs):
    win_grad, wout_grad, done = refs[-3:]
    done[...] = jnp.zeros_like(done)
    h = at.h()
    total = jnp.where((h == 0) | (h == 3), given[...], mine[...]).astype(F32)
    win_grad[0] = total[0:256, :]
    wout_grad[0] = total[256:512, :].T


def finish(at, e, mine, given, into=(), after=(), us=1.2):
    block = lambda shape: pl.BlockSpec((1,) + shape, lambda i: (e, 0, 0))
    anywhere = [pl.BlockSpec(memory_space=pl.ANY)]
    pin = lambda x: pltpu.with_memory_space_constraint(x, pltpu.VMEM)
    return pl.pallas_call(
        skip(functools.partial(finish_kernel, at), 2, len(into) + len(after)),
        grid=(1,),
        out_shape=[pltpu.HBM((EXPERTS, 256, FFT), F32), pltpu.HBM((EXPERTS, FFT, 256), F32), held(8, 128, dtype=F32)],
        in_specs=[vmem(), vmem()] + anywhere * (len(into) + len(after)),
        out_specs=[block((256, FFT)), block((FFT, 256)), vmem()],
        input_output_aliases={2: 0, 3: 1} if into else {},
        cost_estimate=takes(us),
        compiler_params=params(mib=12),
    )(pin(mine), pin(given), *[pltpu.with_memory_space_constraint(x, pltpu.HBM) for x in into], *after)


def halves_kernel(own, sib0, sib1, keep, send):
    for j in range(2):
        sib = (sib0, sib1)[j]
        keep[j] = (own[j, 0].astype(F32) + sib[0].astype(F32)).astype(BF)
        send[j] = (own[j, 1].astype(F32) + sib[1].astype(F32)).astype(BF)


def slots_kernel(keep, got, first, second):
    first[...] = (keep[0].astype(F32) + got[0].astype(F32)).astype(BF)
    second[...] = (keep[1].astype(F32) + got[1].astype(F32)).astype(BF)


def both_slots_kernel(keep, got, slot3, first, given):
    slots_kernel(keep, got, first, given.at[0])
    given[1] = slot3[...]


def cross_kernel(mine, far, got, pair, over):
    total = (mine[...].astype(F32) + got[0].astype(F32)).astype(BF)
    pair[...] = total
    over[0:512, :] = (far[0:512, :].astype(F32) + got[1, 0:512, :].astype(F32)).astype(BF)
    over[512:528, :] = total[512:528]


def unpack_kernel(at, own, sib, qkv_grad, o_grad, wr_grad, g1, s1, g2, s2):
    c = at.c()
    for src, ca in ((own, c), (sib, 1 - c)):
        rows = pl.ds(pl.multiple_of(ca * 128, 128), 128)
        for i in range(3):
            qkv_grad[i, rows, :] = src[i * 128 : (i + 1) * 128, :].astype(F32)
        head = pl.ds(pl.multiple_of(ca * 64, 64), 64)
        o_grad[head, 0:128] = src[384:448, :].astype(F32)
        o_grad[head, 128:256] = src[448:512, :].astype(F32)
        small = src[512:528, :].astype(F32)
        wr_grad[:, rows] = small[0:4]
        for i, ref in enumerate((g1, s1, g2, s2)):
            ref[:, rows] = small[4 + i : 5 + i]


def flip(x, axis, bit):
    n = lax.axis_size(axis)
    return lax.ppermute(x, axis, [(i, i ^ bit) for i in range(n)])


def core(x):
    return flip(x, "tensor", 1)


def across(x):
    return flip(x, "tensor", 2)


def other(x):
    return flip(x, "fsdp", 1)


def packs_of_whole(qkv, out, small):
    def pack(j, fr, cr):
        at = fr * 256 + cr * 128
        head = out[j * 128 + cr * 64 : j * 128 + cr * 64 + 64, fr * 256 : fr * 256 + 256]
        return jnp.concatenate(
            [qkv[i, at : at + 128, j * 128 : (j + 1) * 128] for i in range(3)]
            + [head[:, :128], head[:, 128:]]
            + [small[:, fr * 256 : fr * 256 + 128], small[:, fr * 256 + 128 : fr * 256 + 256]]
        )

    return [
        [jnp.stack([pack(2 * p + j, fr, cr) for j in range(2)]) for cr in range(2) for fr in range(2)] for p in range(2)
    ]


def whole_of_packs(packs):
    qkv, out, small = jnp.zeros((3, D, D), F32), jnp.zeros((D, D), F32), jnp.zeros((8, D), F32)
    for j in range(4):
        for cr in range(2):
            for fr in range(2):
                pack = packs[j // 2][cr][j % 2, fr].astype(F32)
                at, hd = fr * 256 + cr * 128, j * 128 + cr * 64
                qkv = qkv.at[:, at : at + 128, j * 128 : (j + 1) * 128].set(pack[:384].reshape(3, 128, 128))
                out = out.at[hd : hd + 64, fr * 256 : fr * 256 + 128].set(pack[384:448])
                out = out.at[hd : hd + 64, fr * 256 + 128 : fr * 256 + 256].set(pack[448:512])
                if j == 0:
                    small = small.at[:, at : at + 128].set(pack[512:520])
    return qkv, out, small


def forward(kernel, outs, kept, args, scratch, after, us=4.0):
    return pl.pallas_call(
        skip(kernel, len(args), len(after)),
        out_shape=outs + kept,
        in_specs=[vmem()] * len(args) + [pl.BlockSpec(memory_space=pl.ANY)] * len(after),
        out_specs=[vmem()] * len(outs) + [pl.BlockSpec(memory_space=pl.ANY)] * len(kept),
        scratch_shapes=scratch,
        cost_estimate=takes(us),
        compiler_params=params(mib=20),
    )(*[pltpu.with_memory_space_constraint(x, pltpu.VMEM) for x in args], *after)


def local(
    tokens, gain_one, shift_one, w_qkv, w_attn_out, gain_two, shift_two, w_router, w_in, w_out, routes, cotangent
):
    nf, nh = lax.axis_size("fsdp"), lax.axis_size("heads")
    near = nf == 2 and nh == 4
    f = lax.axis_index("fsdp")
    at = Place(not near)

    w_own, w_oth = [None] * 3, [None] * 3
    rows = sds((ROWS, D), BF)
    if near:
        (pack,) = call(
            functools.partial(pack_kernel, at),
            [sds((PACK, 128), BF)],
            (w_qkv, w_attn_out, w_router.T, gain_one, shift_one, gain_two, shift_two),
            fetch=True,
            us=1.1,
        )
        slots = [pack] + [flip(pack, "heads", j) for j in range(1, 4)]
        w_own[0] = packed_weights(0, 1, w_in, w_out, after=(pack,), us=10)
        w_oth[0] = other(w_own[0])
        (tok,) = call(pad_kernel, [rows], (tokens,), after=(w_own[0],), fetch=True, us=6)
        pair = lambda a, b, after, us=0.2: call(pair_kernel, [held(2, PACK, 128)], (a, b), after=after, mib=8, us=us)[0]
        before = (tok,)
        w_own[1] = packed_weights(1, 1, w_in, w_out, after=(tok,))
        w_oth[1] = other(w_own[1])
        pair_b = pair(slots[2], slots[3], (w_own[1],))
        w_own[2] = packed_weights(2, 2, w_in, w_out, after=(pair_b,), us=1.5)
        w_oth[2] = other(w_own[2])
        (cot0,) = call(pad_kernel, [rows], (cotangent,), after=(w_own[2],), fetch=True, us=1.1)
        far = [other(slots[0]), other(slots[1])]
        far = [gate(far[0], (cot0, w_oth[0])), gate(far[1], (cot0,))]
        far_b = other(pair_b)
        pair_a = pair(slots[0], slots[1], (far[0],))
        far_a = pair(far[0], far[1], (pair_a,), 1.5)
        sib_a = pair(core(slots[0]), core(slots[1]), (far_a,))
        sib_far = pair(core(far[0]), core(far[1]), (sib_a,))
        packs = [[pair_a, far_a, sib_a, sib_far]]
        before = ()
    else:
        small_own = jnp.concatenate([w_router.T, jnp.stack([gain_one, shift_one, gain_two, shift_two])])
        small = lax.all_gather(small_own, "fsdp", axis=1, tiled=True)
        qkv_all = lax.all_gather(lax.all_gather(w_qkv, "fsdp", axis=1, tiled=True), "heads", axis=2, tiled=True)
        out_all = lax.all_gather(lax.all_gather(w_attn_out, "fsdp", axis=1, tiled=True), "heads", axis=0, tiled=True)
        packs = packs_of_whole(qkv_all, out_all, small)
        in_all = lax.all_gather(w_in, "fsdp", axis=1, tiled=True)
        o_all = lax.all_gather(w_out, "fsdp", axis=2, tiled=True)
        for i, (first, n) in enumerate(((0, 1), (1, 1), (2, 2))):
            w_own[i] = packed_weights(first, n, in_all[:, :256], o_all[:, :, :256])
            w_oth[i] = packed_weights(first, n, in_all[:, 256:], o_all[:, :, 256:])
        (tok,) = call(pad_kernel, [rows], (tokens,), fetch=True)
        (cot0,) = call(pad_kernel, [rows], (cotangent,), fetch=True)
        before = ()

    named = jnp.pad(routes.T.reshape(2, 8, SEQ), ((0, 0), (0, 0), (0, PAD - SEQ)), constant_values=-1)
    named = named.reshape(2, 4, ROWS).transpose(1, 0, 2)

    kept = [pltpu.HBM(shape, BF) for shape in ((2, ROWS, 384), (2, ROWS, 128), (2, D, 384), (2, 128, D))]
    scratch = [pltpu.VMEM(x.shape, BF) for x in kept] + [pltpu.SemaphoreType.DMA((4, 2))]
    small, n1, acc, qkv_a, mix_a, wq_a, wo_a = forward(
        functools.partial(attn_fwd_kernel, True, at),
        [held(8, D), held(ROWS, D), held(ROWS, D, dtype=F32)],
        kept,
        (tok, *packs[0]),
        scratch,
        before,
    )
    cot1, cot2 = core(cot0), across(cot0)
    before = (cot1,)
    if near:
        far_b = gate(far_b, (n1,), 2.2)
        before = (cot1,)
        packs.append([pair_b, far_b, core(pair_b), core(far_b)])
    n2_0, resid, qkv_b, mix_b, wq_b, wo_b = forward(
        functools.partial(attn_fwd_kernel, False, at),
        [held(ROWS, D), held(ROWS, D, dtype=F32)],
        kept,
        (tok, *packs[1], small, n1, acc),
        scratch,
        before,
        5.5,
    )
    n2_1, n2_2 = core(n2_0), across(n2_0)

    shared = (named, small)
    rows_a = (n2_0, n2_1, cot0, cot1)
    cot2 = gate(cot2, (n2_0,))
    weights = [assemble(at, 0, w_own, w_oth, (cot2,), 2)]
    state_a, grads0 = moe(0, 0, at, rows_a, weights[0], (), shared)
    weights.append(assemble(at, 1, w_own, w_oth, grads0[:1]))
    state_a, grads1 = moe(1, 0, at, rows_a, weights[1], state_a, shared, us=4)
    n2_2 = gate(n2_2, grads1[:1], 0.8)
    rows_b = (n2_2, core(n2_2), cot2, core(cot2))
    state_b, (keep0, send0) = moe(0, 2, at, rows_b, weights[0], (), shared, grads0)
    state_b, (keep1, send1) = moe(1, 2, at, rows_b, weights[1], state_b, shared, grads1)
    weights.append(assemble(at, 2, w_own, w_oth, (keep1,)))
    state_a, grads2 = moe(2, 0, at, rows_a, weights[2], state_a, shared)
    weights.append(assemble(at, 3, w_own, w_oth, grads2[:1], 1.0))
    state_b, (keep2, send2) = moe(2, 2, at, rows_b, weights[2], state_b, shared, grads2, after=weights[3])
    ones, twos, threes, before = [None] * 4, [None] * 4, [None] * 4, ()
    if near:
        got0 = other(send0)
        ones[0] = add(keep0, got0, after=(keep2,), us=2)
        before = (ones[0],)
    (d2, *d3, m2, m3, wr_b), grads3 = moe(
        3, 2, at, rows_b, weights[3], state_b, shared, end=True, after=before, us=5
    )
    (d_sum,) = call(rows_kernel, [held(ROWS, D)], (d2, core(d3[0]), core(d3[1])), after=grads3[:1], us=1.2)
    d_far = across(d_sum)
    before = (d_sum,)
    if near:
        got1 = other(send1)
        ones[1] = add(keep1, got1, after=before, us=1.5)
        before = (ones[1],)
    (d0, *d1, m0, m1, wr_a), (keep3, send3) = moe(
        3, 0, at, rows_a, weights[3], state_a, shared, grads3, True, before, us=5
    )
    keeps, sends = (keep0, keep1, keep2, keep3), (send0, send1, send2, send3)
    d_near = [core(d) for d in d1]
    inward = lambda x: lax.ppermute(x, "heads", [(0, 1), (3, 2)])
    middle = lambda x: lax.ppermute(x, "heads", [(1, 2), (2, 1)])
    outward = lambda x: lax.ppermute(x, "heads", [(1, 0), (2, 3)])
    before = ()
    if near:
        got = [got0, got1] + [other(send) for send in sends[2:]]
        twos[0] = add(ones[0], inward(ones[0]), after=(keep3,), us=4.3)
        before = (twos[0],)

    scratch = [pltpu.VMEM(shape, BF) for shape in ((ROWS, 384), (D, 384), (128, D), (D, ROWS), (ROWS, D))]
    both = [held(2, 2, PACK, 128)] + [held(2, PACK, 128)] * 2
    own_b, sib_2, sib_3, dresid, sgrad, dn1 = call(
        functools.partial(attn_bwd_kernel, True, at),
        both + [held(ROWS, D, dtype=F32), held(8, D, dtype=F32), held(ROWS, D, dtype=F32)],
        (d0, *d_near, d_far, resid, cot0, wr_a, wr_b, small, n1, qkv_b, mix_b, wq_b, wo_b),
        scratch,
        after=before,
        us=6.2,
    )
    if near:
        ones[2] = add(keeps[2], got[2], after=(dn1,), us=1.5)
        keep_b, send_b = call(
            halves_kernel, [held(2, PACK, 128)] * 2, (own_b, core(sib_2), core(sib_3)), after=(ones[2],), us=1.5
        )
        twos[1] = add(ones[1], inward(ones[1]), after=(keep_b,), us=1)
        threes[0] = add(twos[0], middle(twos[0]), after=(twos[1],), us=0.3)
        both_ways = mixed(at, ones[2], threes[0], us=1.5)
        neighbour0 = flip(both_ways, "heads", 1)
        ones[3] = add(keeps[3], got[3], after=(both_ways,), us=0.3)
        before = (ones[3],)
    own_a, sib_0, sib_1, input_grad = call(
        functools.partial(attn_bwd_kernel, False, at),
        both + [sds((SEQ * 2, D), BF)],
        (dresid, sgrad, dn1, tok, small, n1, qkv_a, mix_a, wq_a, wo_a),
        scratch + [pltpu.VMEM((8, D), F32), pltpu.VMEM((ROWS, D), F32)],
        after=before,
        us=8.2,
    )

    if near:
        one_pack = held(PACK, 128)
        slot2, slot3 = call(slots_kernel, [one_pack] * 2, (keep_b, other(send_b)), after=(own_a,))
        keep_a, send_a = call(
            halves_kernel, [held(2, PACK, 128)] * 2, (own_a, core(sib_0), core(sib_1)), after=(slot3,), us=1.5
        )
        threes[1] = add(twos[1], middle(twos[1]), after=(keep_a,), us=0.3)
        both_ways = mixed(at, ones[3], threes[1], us=2)
        neighbour1 = flip(both_ways, "heads", 1)
        twos[2] = add(ones[2], neighbour0, after=(both_ways,), us=2)
        *grads, done = finish(at, 0, threes[0], neighbour0, after=(twos[2],), us=2)
        slot0, given = call(
            both_slots_kernel, [one_pack, held(2, PACK, 128)], (keep_a, other(send_a), slot3), after=(done,), us=4
        )
        twos[3] = add(ones[3], neighbour1, after=(given,), us=0.3)
        *grads, done = finish(at, 1, threes[1], neighbour1, grads, after=(twos[3],), us=1.2)
        threes[2] = add(twos[2], middle(twos[2]), after=(done,), us=3)
        pair, over = call(
            cross_kernel, [one_pack] * 2, (slot0, slot2, flip(given, "heads", 1)), after=(threes[2],), us=1.5
        )
        threes[3] = add(twos[3], middle(twos[3]), after=(pair,), us=2)
        m_near = core(m1)
        m_sum = add(m2, core(m3), after=(threes[3],), us=5)
        m_far = across(m_sum)
        half = add(pair, flip(over, "heads", 2), after=(m_sum,))
        *grads, done = finish(at, 2, threes[2], outward(threes[2]), grads, after=(half,), us=6)
        half = add(half, across(half), after=(done,), us=2)
        vector = sds((1, 256), F32)
        qkv_grad, o_grad, wr_grad, *vectors = call(
            functools.partial(unpack_kernel, at),
            [sds((3, 256, 128), F32), sds((128, 256), F32), sds((4, 256), F32)] + [vector] * 4,
            (half, core(half)),
        )
        (output,) = call(out_kernel, [sds((SEQ * 2, D), BF)], (resid, m0, m_near, m_far), after=(half,))
        win_grad, wout_grad, _ = finish(at, 3, threes[3], outward(threes[3]), grads, after=(half,))
        vectors = [v.reshape(256) for v in vectors]
    else:
        m_near = core(m1)
        m_far = across(add(m2, core(m3)))
        (output,) = call(out_kernel, [sds((SEQ * 2, D), BF)], (resid, m0, m_near, m_far))
        keep, send = jnp.stack(keeps), jnp.stack(sends)
        gin = jnp.concatenate([keep[:, :256], send[:, :256]], 1)
        gout = jnp.concatenate([keep[:, 256:], send[:, 256:]], 1).transpose(0, 2, 1)
        win_grad = lax.psum_scatter(gin, "fsdp", scatter_dimension=1, tiled=True)
        wout_grad = lax.psum_scatter(gout, "fsdp", scatter_dimension=2, tiled=True)
        win_grad = lax.psum(win_grad, "heads").astype(F32)
        wout_grad = lax.psum(wout_grad, "heads").astype(F32)
        qkv_grad, o_grad, sgrad = whole_of_packs(((own_a, jnp.stack([sib_0, sib_1])), (own_b, jnp.stack([sib_2, sib_3]))))
        qkv_grad = lax.psum_scatter(qkv_grad, "fsdp", scatter_dimension=1, tiled=True)
        qkv_grad = lax.psum_scatter(qkv_grad, "heads", scatter_dimension=2, tiled=True)
        qkv_grad = lax.psum(qkv_grad, "tensor")
        o_grad = lax.psum_scatter(o_grad, "fsdp", scatter_dimension=1, tiled=True)
        o_grad = lax.psum_scatter(o_grad, "heads", scatter_dimension=0, tiled=True)
        o_grad = lax.psum(o_grad, "tensor")
        sgrad = lax.psum(sgrad, ("fsdp", "heads", "tensor"))
        sgrad = lax.dynamic_slice_in_dim(sgrad, f * gain_one.shape[0], gain_one.shape[0], 1)
        wr_grad, vectors = sgrad[0:4], [sgrad[4 + i] for i in range(4)]

    return (
        output,
        input_grad,
        vectors[0],
        vectors[1],
        qkv_grad,
        o_grad,
        vectors[2],
        vectors[3],
        wr_grad.T,
        win_grad,
        wout_grad,
    )


def solution(mesh):
    placed = (
        P(("fsdp", "heads", "tensor"), None),
        P("fsdp"),
        P("fsdp"),
        P(None, "fsdp", "heads"),
        P("heads", "fsdp"),
        P("fsdp"),
        P("fsdp"),
        P("fsdp", None),
        P(None, "fsdp", "tensor"),
        P(None, "tensor", "fsdp"),
        P(("fsdp", "heads"), None),
        P(("fsdp", "heads", "tensor"), None),
    )
    return jax.shard_map(
        local,
        mesh=mesh,
        in_specs=placed,
        out_specs=(
            P(("fsdp", "heads", "tensor"), None),
            P(("fsdp", "heads", "tensor"), None),
            P("fsdp"),
            P("fsdp"),
            P(None, "fsdp", "heads"),
            P("heads", "fsdp"),
            P("fsdp"),
            P("fsdp"),
            P("fsdp", None),
            P(None, "fsdp", "tensor"),
            P(None, "tensor", "fsdp"),
        ),
        check_vma=False,
    )
```

```python
import functools

import jax
import jax.numpy as jnp
from jax import lax
from jax.experimental import pallas as pl
from jax.experimental.pallas import tpu as pltpu
from jax.sharding import PartitionSpec as P

HD = 64
SEQ = 197
PAD = 208
ROWS = 2 * PAD
D = 512
FFT = 512
EXPERTS = 4
BF = jnp.bfloat16
F32 = jnp.float32
PACK = 528
GELU_C = 0.7978845608028654


def nn(a, b):
    return lax.dot_general(a, b, (((1,), (0,)), ((), ())), preferred_element_type=F32)


def nt(a, b):
    return lax.dot_general(a, b, (((1,), (1,)), ((), ())), preferred_element_type=F32)


def tn(a, b):
    return lax.dot_general(a, b, (((0,), (0,)), ((), ())), preferred_element_type=F32)


def params(sem=None, mib=24):
    return pltpu.CompilerParams(vmem_limit_bytes=mib * 1024 * 1024, dimension_semantics=sem)


class Place:
    def __init__(self, apart):
        self.apart = apart

    def f(self):
        return 0 if self.apart else lax.axis_index("fsdp")

    def c(self):
        return 0 if self.apart else lax.axis_index("tensor") & 1

    def t(self):
        return lax.axis_index("tensor")

    def h(self):
        return lax.axis_index("heads")


def repeat(body, unrolled):
    if unrolled:
        body(0, 0)
        body(1, 0)
    else:
        lax.fori_loop(0, 2, body, 0)


def vmem():
    return pl.BlockSpec(memory_space=pltpu.VMEM)


def sds(shape, dtype):
    return jax.ShapeDtypeStruct(shape, dtype)


def held(*shape, dtype=BF):
    return pltpu.VMEM(shape, dtype)


def skip(kernel, n_args, n_after):
    def run(*refs):
        kernel(*refs[:n_args], *refs[n_args + n_after :])

    return run


def takes(us):
    return pl.CostEstimate(flops=int(us * 230000000), transcendentals=0, bytes_accessed=0)


def call(kernel, outs, args, scratch=(), after=(), mib=16, fetch=False, us=0.2):
    spec = (lambda x: pl.BlockSpec(x.shape, lambda i: (0,) * len(x.shape))) if fetch else (lambda x: vmem())
    space = pltpu.HBM if fetch else pltpu.VMEM
    return pl.pallas_call(
        skip(kernel, len(args), len(after)),
        grid=(1,) if fetch else (),
        out_shape=outs,
        in_specs=[spec(x) for x in args] + [pl.BlockSpec(memory_space=pl.ANY)] * len(after),
        out_specs=[spec(x) for x in outs],
        scratch_shapes=list(scratch),
        cost_estimate=takes(us),
        compiler_params=params(mib=mib),
    )(*[pltpu.with_memory_space_constraint(x, space) for x in args], *after)


def pack_kernel(at, wqkv, wo, wr, g1, s1, g2, s2, out):
    c = at.c()
    rows = pl.ds(pl.multiple_of(c * 128, 128), 128)
    for i in range(3):
        out[i * 128 : (i + 1) * 128, :] = wqkv[i, rows, :]
    head = pl.ds(pl.multiple_of(c * 64, 64), 64)
    out[384:448, :] = wo[head, 0:128]
    out[448:512, :] = wo[head, 128:256]
    small = [wr[...].astype(F32)] + [r[...].reshape(1, 256).astype(F32) for r in (g1, s1, g2, s2)]
    small = jnp.concatenate(small, axis=0).astype(BF)
    out[512:520, :] = small[:, 0:128]
    out[520:528, :] = small[:, 128:256]


def copy_kernel(src, out):
    out[...] = src[...]


def gate(x, after, us=0.2):
    return call(copy_kernel, [held(*x.shape)], (x,), after=after, mib=8, us=us)[0]


def pair_kernel(own, oth, out):
    out[0] = own[...]
    out[1] = oth[...]


def weights_kernel(win, wout, out):
    for e in range(out.shape[0]):
        out[e, 0:256, :] = win[e]
        out[e, 256:512, 0:256] = wout[e, 0:256, :]
        out[e, 256:512, 256:512] = wout[e, 256:512, :]


def packed_weights(first, n, w_in, w_out, after=(), us=1.2):
    hbm = lambda x: pltpu.with_memory_space_constraint(x, pltpu.HBM)
    return pl.pallas_call(
        skip(weights_kernel, 2, len(after)),
        grid=(1,),
        out_shape=held(n, 512, 512),
        in_specs=[
            pl.BlockSpec((n, 256, 512), lambda i: (first // n, 0, 0)),
            pl.BlockSpec((n, 512, 256), lambda i: (first // n, 0, 0)),
        ]
        + [pl.BlockSpec(memory_space=pl.ANY)] * len(after),
        out_specs=vmem(),
        cost_estimate=takes(us),
        compiler_params=params(mib=8),
    )(hbm(w_in), hbm(w_out), *after)


def spread(v):
    zero = jnp.zeros((PAD - SEQ, v.shape[1]), v.dtype)
    return jnp.concatenate([v[:SEQ], zero, v[SEQ:], zero], axis=0)


def close(v):
    return jnp.concatenate([v[:SEQ], v[PAD : PAD + SEQ]], axis=0)


def pad_kernel(rows, out):
    out[...] = spread(rows[...].astype(F32)).astype(BF)


def norm_parts(x):
    center = jnp.mean(x, -1, keepdims=True)
    centered = x - center
    rstd = lax.rsqrt(jnp.mean(centered * centered, -1, keepdims=True) + 1e-06)
    return centered * rstd, rstd


def norm_back(xhat, rstd, grad, gain):
    dxhat = grad * gain
    m1 = jnp.mean(dxhat, -1, keepdims=True)
    m2 = jnp.mean(dxhat * xhat, -1, keepdims=True)
    return rstd * (dxhat - m1 - xhat * m2)


def attn_fwd_kernel(first, at, tok, *refs):
    packs, refs = (refs[0:2], refs[2:4]), refs[4:]
    if first:
        (small, n1_ref, acc_ref), refs = refs[:3], refs[3:]
    else:
        (small, n1_ref, acc_in, n2_ref, acc_ref), refs = refs[:5], refs[5:]
    kept, (qkv_ref, mix_ref, wq_ref, wo_ref), sems = refs[:4], refs[4:8], refs[8]

    def keep(which, j):
        src, dst = (qkv_ref, mix_ref, wq_ref, wo_ref)[which].at[j], kept[which].at[j]
        return pltpu.make_async_copy(src, dst, sems.at[which, j])

    f, c = at.f(), at.c()
    if first:
        for fr in range(2):
            left = (f ^ fr) * 256
            for i in range(2):
                cols = pl.ds(pl.multiple_of(left + i * 128, 128), 128)
                small[:, cols] = packs[0][fr][0, 512 + 8 * i : 520 + 8 * i, :]
        x = tok[...].astype(F32)
        xhat, _ = norm_parts(x)
        n1 = (xhat * small[4:5, :].astype(F32) + small[5:6, :].astype(F32)).astype(BF)
        n1_ref[...] = n1
        acc_ref[...] = x
    else:
        acc_ref[...] = acc_in[...]
    lane = lax.broadcasted_iota(jnp.int32, (PAD, 128), 1)
    key = lax.broadcasted_iota(jnp.int32, (PAD, PAD), 1)

    def slot(j, carry):
        for fr in range(2):
            fa = f ^ fr
            for cr in range(2):
                ca = c ^ cr
                src = packs[cr][fr]
                rows = pl.ds(pl.multiple_of(fa * 256 + ca * 128, 128), 128)
                for i in range(3):
                    wq_ref[j, rows, i * 128 : (i + 1) * 128] = src[j, i * 128 : (i + 1) * 128, :]
                head = pl.ds(pl.multiple_of(ca * 64, 64), 64)
                for i in range(2):
                    cols = pl.ds(pl.multiple_of(fa * 256 + i * 128, 128), 128)
                    wo_ref[j, head, cols] = src[j, 384 + 64 * i : 448 + 64 * i, :]
        keep(2, j).start()
        keep(3, j).start()
        qkv_ref[j] = nn(n1_ref[...], wq_ref[j]).astype(BF)
        keep(0, j).start()
        for im in range(2):
            r = slice(im * PAD, (im + 1) * PAD)
            q, k, v = (qkv_ref[j, r, i * 128 : (i + 1) * 128] for i in range(3))
            outs = []
            for head in range(2):
                s = nt(jnp.where(lane // HD == head, q, jnp.zeros_like(q)), k) * 0.125
                s = jnp.where(key < SEQ, s, -1e30)
                e = jnp.exp(s - jnp.max(s, -1, keepdims=True))
                p = e / jnp.sum(e, -1, keepdims=True)
                outs.append(nn(p.astype(BF), v))
            mix = jnp.where(lane < HD, outs[0], outs[1]).astype(BF)
            mix_ref[j, r, :] = mix
            acc_ref[r, :] += nn(mix, wo_ref[j])
        keep(1, j).start()
        return carry

    repeat(slot, False)
    if not first:
        for im in range(2):
            r = slice(im * PAD, (im + 1) * PAD)
            xhat, _ = norm_parts(acc_ref[r, :])
            n2_ref[r, :] = (xhat * small[6:7, :].astype(F32) + small[7:8, :].astype(F32)).astype(BF)
    for which in range(4):
        for j in range(2):
            keep(which, j).wait()


def attn_bwd_kernel(first, at, *refs):
    take = lambda k: (refs[:k], refs[k:])
    if first:
        (d0, d1a, d1b, d2, resid, cot, wr_a, wr_b, small), refs = take(9)
    else:
        (dresid_in, sgrad_in, dn1_in, tok, small), refs = take(5)
    (n1, qkvs, mixes, wqs, wos, own, *sibs), refs = take(8)
    if first:
        dresid_out, sgrad, dn1_s, dqkv_s, gq_s, go_s, n1t_s, dattn_s = refs
    else:
        igrad, dqkv_s, gq_s, go_s, n1t_s, dattn_s, sgrad, dn1_s = refs
    f, c = at.f(), at.c()
    if first:
        dn2 = d0[...].astype(F32) + d2[...].astype(F32)
        dn2 = dn2 + jnp.concatenate([d1a[...], d1b[...]], axis=0).astype(F32)
        xhat, rstd = norm_parts(resid[...])
        sgrad[0:4, :] = (wr_a[...] + wr_b[...])[0:4]
        sgrad[4:6, :] = jnp.zeros((2, D), F32)
        sgrad[6:7, :] = jnp.sum(dn2 * xhat, 0, keepdims=True)
        sgrad[7:8, :] = jnp.sum(dn2, 0, keepdims=True)
        dresid = cot[...].astype(F32) + norm_back(xhat, rstd, dn2, small[6:7, :].astype(F32))
        dresid_out[...] = dresid
    else:
        dresid = dresid_in[...]
    dattn_s[...] = dresid.astype(BF)
    lane = lax.broadcasted_iota(jnp.int32, (PAD, 128), 1)
    key = lax.broadcasted_iota(jnp.int32, (PAD, PAD), 0)
    n1t_s[...] = n1[...].T
    dn1_s[...] = jnp.zeros_like(dn1_s) if first else dn1_in[...]

    def slot(j, carry):
        qkv, mix, wq, wo = (ref.at[j] for ref in (qkvs, mixes, wqs, wos))
        go_s[...] = tn(mix[...], dattn_s[...]).astype(BF)
        dmix = nt(dattn_s[...], wo[...]).astype(BF)
        for im in range(2):
            r = slice(im * PAD, (im + 1) * PAD)
            q, k, v = (qkv[r, i * 128 : (i + 1) * 128] for i in range(3))
            dm = dmix[r]
            dq, dk, dv = [], [], []
            for head in range(2):
                keep = lane // HD == head
                s = nt(k, jnp.where(keep, q, jnp.zeros_like(q))) * 0.125
                s = jnp.where(key < SEQ, s, -1e30)
                e = jnp.exp(s - jnp.max(s, 0, keepdims=True))
                p = e / jnp.sum(e, 0, keepdims=True)
                dp = nt(v, jnp.where(keep, dm, jnp.zeros_like(dm)))
                ds = (p * (dp - jnp.sum(p * dp, 0, keepdims=True))).astype(BF)
                dq.append(tn(ds, k))
                dk.append(nn(ds, q))
                dv.append(nn(p.astype(BF), dm))
            near = lane < HD
            dqkv_s[r, 0:128] = (jnp.where(near, dq[0], dq[1]) * 0.125).astype(BF)
            dqkv_s[r, 128:256] = (jnp.where(near, dk[0], dk[1]) * 0.125).astype(BF)
            dqkv_s[r, 256:384] = jnp.where(near, dv[0], dv[1]).astype(BF)
        dqkv = dqkv_s[...]
        gq_s[...] = nn(n1t_s[...], dqkv).astype(BF)
        dn1_s[...] += nt(dqkv, wq[...])
        for cr, dst, only in ((0, own.at[j], None), (1, sibs[0], 0), (1, sibs[1], 1)):

            def fill():
                for fr in range(2):
                    fa, ca = f ^ fr, c ^ cr
                    rows = pl.ds(pl.multiple_of(fa * 256 + ca * 128, 128), 128)
                    for i in range(3):
                        dst[fr, i * 128 : (i + 1) * 128, :] = gq_s[rows, i * 128 : (i + 1) * 128]
                    head = pl.ds(pl.multiple_of(ca * 64, 64), 64)
                    for i in range(2):
                        cols = pl.ds(pl.multiple_of(fa * 256 + i * 128, 128), 128)
                        dst[fr, 384 + 64 * i : 448 + 64 * i, :] = go_s[head, cols]

            if only is None:
                fill()
            else:
                pl.when(j == only)(fill)
        return carry

    lax.fori_loop(0, 2, slot, 0)
    if first:
        for j in range(2):
            for fr in range(2):
                own[j, fr, 512:528, :] = jnp.zeros((16, 128), BF)
                sibs[j][fr, 512:528, :] = jnp.zeros((16, 128), BF)
        return
    dn1 = dn1_s[...]
    xhat, rstd = norm_parts(tok[...].astype(F32))
    sgrad[...] = sgrad_in[...]
    sgrad[4:5, :] = jnp.sum(dn1 * xhat, 0, keepdims=True)
    sgrad[5:6, :] = jnp.sum(dn1, 0, keepdims=True)
    for fr in range(2):
        for cr in range(2):
            left = (f ^ fr) * 256 + (c ^ cr) * 128
            rows = sgrad[:, pl.ds(pl.multiple_of(left, 128), 128)]
            rows = jnp.concatenate([rows, jnp.zeros_like(rows)], axis=0).astype(BF)
            for j in range(2):
                (own.at[j], sibs[j])[cr][fr, 512:528, :] = rows
    grad = dresid + norm_back(xhat, rstd, dn1, small[4:5, :].astype(F32))
    igrad[...] = close(grad).astype(BF)


def out_kernel(resid, m0, m1, m2, out):
    total = resid[...] + m0[...].astype(F32) + m1[...].astype(F32) + m2[...].astype(F32)
    out[...] = close(total).astype(BF)


def assemble_kernel(at, e, own, oth, win, wout):
    f = at.f()
    for w, half in ((own, f), (oth, 1 - f)):
        half = pl.ds(pl.multiple_of(half * 256, 256), 256)
        win[half, :] = w[e, 0:256, :]
        wout[0:256, half] = w[e, 256:512, 0:256]
        wout[256:512, half] = w[e, 256:512, 256:512]


def assemble(at, e, own, oth, after=(), us=0.3):
    part, place = ((0, 0), (1, 0), (2, 0), (2, 1))[e]
    kernel = functools.partial(assemble_kernel, at, place)
    return call(kernel, [held(512, 512)] * 2, (own[part], oth[part]), after=after, mib=8, us=us)


def moe_kernel(start, end, fresh, e, base, at, win, wout, *refs):
    take = lambda k: (refs[:k], refs[k:])
    if start:
        (x0, x1, g0, g1, routes, small), refs = take(6)
    else:
        (xs, gs, xt, gt, gating, mix_in, dn_in, dp_in), refs = take(8)
    if end:
        (small,), refs = take(1)
    if not fresh:
        (gin_in, gout_in), refs = take(2)
    if start:
        (xs, gs, xt, gt, gating), refs = take(5)
    if end:
        (dn0, dn1a, dn1b, mix0, mix1, wrg), refs = take(6)
    else:
        (mix, dn, dprob), refs = take(3)
    out_a, out_b, hg_s, di_s = refs[:4]
    if end:
        mix, dn = refs[4:]
        wrg[...] = jnp.zeros_like(wrg)
    f = at.f()
    if start:
        xs[0], xs[1], gs[0], gs[1] = x0[...], x1[...], g0[...], g1[...]

    def rows(b, carry):
        lane = lax.broadcasted_iota(jnp.int32, (ROWS, 8), 1)
        if start:
            xt[b] = xs[b].T
            gt[b] = gs[b].T
            logits = jnp.where(lane < EXPERTS, nt(xs[b], small[...]), -1e30)
            ex = jnp.exp(logits - jnp.max(logits, -1, keepdims=True))
            named = routes[at.t() ^ (base + b)]
            expert = lax.broadcasted_iota(jnp.int32, (8, ROWS), 0)
            gating[b, :, 0:8] = ex / jnp.sum(ex, -1, keepdims=True)
            gating[b, :, 8:16] = jnp.where((named[0:1] == expert) | (named[1:2] == expert), 1.0, 0.0).T
        inner = nn(xs[b], win[...])
        back = nt(gs[b], wout[...])
        gate = gating[b, :, e : e + 1] * gating[b, :, 8 + e : 9 + e]
        square = inner * inner
        th = jnp.tanh(inner * (square * (GELU_C * 0.044715) + GELU_C))
        half = th * 0.5 + 0.5
        hidden = inner * half
        slope = half * ((1.0 - half) * (inner * (square * (6 * GELU_C * 0.044715) + 2 * GELU_C)) + 1.0)
        dp = jnp.where(lane == e, jnp.sum(hidden * back, -1, keepdims=True), 0.0)
        hg = (gate * hidden).astype(BF)
        di = ((gate * back) * slope).astype(BF)
        hg_s[b] = hg
        di_s[b] = di
        mx, dx = nn(hg, wout[...]), nt(di, win[...])
        if not start:
            dp, mx, dx = dp + dp_in[b], mx + mix_in[b], dx + dn_in[b]
        if end:
            router = gating[b, :, 0:8]
            dp = dp * gating[b, :, 8:16]
            dl = router * (dp - jnp.sum(router * dp, -1, keepdims=True))
            dl = jnp.where(lane < EXPERTS, dl, 0.0).astype(BF)
            dn[b] = (dx + nn(dl, small[...])).astype(BF)
            mix[b] = mx.astype(BF)
            wrg[...] += tn(dl, xs[b])
        else:
            mix[b], dn[b], dprob[b] = mx, dx, dp
        return carry

    repeat(rows, start and base == 2)
    if end:
        dn0[...], dn1a[...], dn1b[...] = dn[0], dn[1, 0:PAD], dn[1, PAD:ROWS]
        mix0[...], mix1[...] = mix[0], mix[1]

    def half_of_rows(i, carry):
        half = pl.ds(pl.multiple_of((i if fresh else f ^ i) * 256, 256), 256)
        gin = nn(xt[0, half, :], di_s[0]) + nn(xt[1, half, :], di_s[1])
        gout = nn(gt[0, half, :], hg_s[0]) + nn(gt[1, half, :], hg_s[1])
        if fresh:
            out_a[half, :], out_b[half, :] = gin, gout
            return carry
        gin, gout = (gin + gin_in[half, :]).astype(BF), (gout + gout_in[half, :]).astype(BF)
        for k, dst in enumerate((out_a, out_b)):

            @pl.when(i == k)
            def _():
                dst[0:256, :] = gin
                dst[256:512, :] = gout

        return carry

    lax.fori_loop(0, 2, half_of_rows, 0)


def moe(e, base, at, rows, weights, state, shared, grads=(), end=False, after=(), us=3.8):
    start, fresh = not state, not grads
    routes, small = shared
    args = tuple(weights) + ((*rows, routes, small) if start else state) + ((small,) if end else ()) + grads
    outs = []
    if start:
        outs += [held(2, ROWS, D)] * 2 + [held(2, D, ROWS)] * 2 + [held(2, ROWS, 16, dtype=F32)]
    if end:
        outs += [held(ROWS, D), held(PAD, D), held(PAD, D), held(ROWS, D), held(ROWS, D), held(8, D, dtype=F32)]
    else:
        outs += [held(2, ROWS, D, dtype=F32)] * 2 + [held(2, ROWS, 8, dtype=F32)]
    outs += [held(D, FFT, dtype=F32) if fresh else held(512, 512)] * 2
    scratch = [pltpu.VMEM((2, ROWS, D), BF)] * (4 if end else 2)
    got = call(functools.partial(moe_kernel, start, end, fresh, e, base, at), outs, args, scratch, after, 16, us=us)
    made, grads = got[:-2], got[-2:]
    if not end:
        made = tuple(made) if start else tuple(state[:5]) + tuple(made)
    return made, tuple(grads)


def rows_kernel(whole, upper, lower, out):
    out[0:PAD, :] = (whole[0:PAD, :].astype(F32) + upper[...].astype(F32)).astype(BF)
    out[PAD:ROWS, :] = (whole[PAD:ROWS, :].astype(F32) + lower[...].astype(F32)).astype(BF)


def add_kernel(a, b, out):
    out[...] = (a[...].astype(F32) + b[...].astype(F32)).astype(BF)


def add(a, b, after=(), us=0.2):
    return call(add_kernel, [held(*a.shape)], (a, b), after=after, mib=8, us=us)[0]


def mixed_kernel(at, ends, middle, out):
    h = at.h()
    out[...] = jnp.where((h == 0) | (h == 3), ends[...], middle[...])


def mixed(at, ends, middle, after=(), us=0.2):
    return call(functools.partial(mixed_kernel, at), [held(512, 512)], (ends, middle), after=after, mib=8, us=us)[0]


def finish_kernel(at, mine, given, *refs):
    win_grad, wout_grad, done = refs[-3:]
    done[...] = jnp.zeros_like(done)
    h = at.h()
    total = jnp.where((h == 0) | (h == 3), given[...], mine[...]).astype(F32)
    win_grad[0] = total[0:256, :]
    wout_grad[0] = total[256:512, :].T


def finish(at, e, mine, given, into=(), after=(), us=1.2):
    block = lambda shape: pl.BlockSpec((1,) + shape, lambda i: (e, 0, 0))
    anywhere = [pl.BlockSpec(memory_space=pl.ANY)]
    pin = lambda x: pltpu.with_memory_space_constraint(x, pltpu.VMEM)
    return pl.pallas_call(
        skip(functools.partial(finish_kernel, at), 2, len(into) + len(after)),
        grid=(1,),
        out_shape=[pltpu.HBM((EXPERTS, 256, FFT), F32), pltpu.HBM((EXPERTS, FFT, 256), F32), held(8, 128, dtype=F32)],
        in_specs=[vmem(), vmem()] + anywhere * (len(into) + len(after)),
        out_specs=[block((256, FFT)), block((FFT, 256)), vmem()],
        input_output_aliases={2: 0, 3: 1} if into else {},
        cost_estimate=takes(us),
        compiler_params=params(mib=12),
    )(pin(mine), pin(given), *[pltpu.with_memory_space_constraint(x, pltpu.HBM) for x in into], *after)


def halves_kernel(own, sib0, sib1, keep, send):
    for j in range(2):
        sib = (sib0, sib1)[j]
        keep[j] = (own[j, 0].astype(F32) + sib[0].astype(F32)).astype(BF)
        send[j] = (own[j, 1].astype(F32) + sib[1].astype(F32)).astype(BF)


def slots_kernel(keep, got, first, second):
    first[...] = (keep[0].astype(F32) + got[0].astype(F32)).astype(BF)
    second[...] = (keep[1].astype(F32) + got[1].astype(F32)).astype(BF)


def both_slots_kernel(keep, got, slot3, first, given):
    slots_kernel(keep, got, first, given.at[0])
    given[1] = slot3[...]


def cross_kernel(mine, far, got, pair, over):
    total = (mine[...].astype(F32) + got[0].astype(F32)).astype(BF)
    pair[...] = total
    over[0:512, :] = (far[0:512, :].astype(F32) + got[1, 0:512, :].astype(F32)).astype(BF)
    over[512:528, :] = total[512:528]


def unpack_kernel(at, own, sib, qkv_grad, o_grad, wr_grad, g1, s1, g2, s2):
    c = at.c()
    for src, ca in ((own, c), (sib, 1 - c)):
        rows = pl.ds(pl.multiple_of(ca * 128, 128), 128)
        for i in range(3):
            qkv_grad[i, rows, :] = src[i * 128 : (i + 1) * 128, :].astype(F32)
        head = pl.ds(pl.multiple_of(ca * 64, 64), 64)
        o_grad[head, 0:128] = src[384:448, :].astype(F32)
        o_grad[head, 128:256] = src[448:512, :].astype(F32)
        small = src[512:528, :].astype(F32)
        wr_grad[:, rows] = small[0:4]
        for i, ref in enumerate((g1, s1, g2, s2)):
            ref[:, rows] = small[4 + i : 5 + i]


def flip(x, axis, bit):
    n = lax.axis_size(axis)
    return lax.ppermute(x, axis, [(i, i ^ bit) for i in range(n)])


def core(x):
    return flip(x, "tensor", 1)


def across(x):
    return flip(x, "tensor", 2)


def other(x):
    return flip(x, "fsdp", 1)


def packs_of_whole(qkv, out, small):
    def pack(j, fr, cr):
        at = fr * 256 + cr * 128
        head = out[j * 128 + cr * 64 : j * 128 + cr * 64 + 64, fr * 256 : fr * 256 + 256]
        return jnp.concatenate(
            [qkv[i, at : at + 128, j * 128 : (j + 1) * 128] for i in range(3)]
            + [head[:, :128], head[:, 128:]]
            + [small[:, fr * 256 : fr * 256 + 128], small[:, fr * 256 + 128 : fr * 256 + 256]]
        )

    return [
        [jnp.stack([pack(2 * p + j, fr, cr) for j in range(2)]) for cr in range(2) for fr in range(2)] for p in range(2)
    ]


def whole_of_packs(packs):
    qkv, out, small = jnp.zeros((3, D, D), F32), jnp.zeros((D, D), F32), jnp.zeros((8, D), F32)
    for j in range(4):
        for cr in range(2):
            for fr in range(2):
                pack = packs[j // 2][cr][j % 2, fr].astype(F32)
                at, hd = fr * 256 + cr * 128, j * 128 + cr * 64
                qkv = qkv.at[:, at : at + 128, j * 128 : (j + 1) * 128].set(pack[:384].reshape(3, 128, 128))
                out = out.at[hd : hd + 64, fr * 256 : fr * 256 + 128].set(pack[384:448])
                out = out.at[hd : hd + 64, fr * 256 + 128 : fr * 256 + 256].set(pack[448:512])
                if j == 0:
                    small = small.at[:, at : at + 128].set(pack[512:520])
    return qkv, out, small


def forward(kernel, outs, kept, args, scratch, after, us=4.0):
    return pl.pallas_call(
        skip(kernel, len(args), len(after)),
        out_shape=outs + kept,
        in_specs=[vmem()] * len(args) + [pl.BlockSpec(memory_space=pl.ANY)] * len(after),
        out_specs=[vmem()] * len(outs) + [pl.BlockSpec(memory_space=pl.ANY)] * len(kept),
        scratch_shapes=scratch,
        cost_estimate=takes(us),
        compiler_params=params(mib=20),
    )(*[pltpu.with_memory_space_constraint(x, pltpu.VMEM) for x in args], *after)


def local(
    tokens, gain_one, shift_one, w_qkv, w_attn_out, gain_two, shift_two, w_router, w_in, w_out, routes, cotangent
):
    nf, nh = lax.axis_size("fsdp"), lax.axis_size("heads")
    near = nf == 2 and nh == 4
    f = lax.axis_index("fsdp")
    at = Place(not near)

    w_own, w_oth = [None] * 3, [None] * 3
    rows = sds((ROWS, D), BF)
    if near:
        (pack,) = call(
            functools.partial(pack_kernel, at),
            [sds((PACK, 128), BF)],
            (w_qkv, w_attn_out, w_router.T, gain_one, shift_one, gain_two, shift_two),
            fetch=True,
            us=1.1,
        )
        slots = [pack] + [flip(pack, "heads", j) for j in range(1, 4)]
        w_own[0] = packed_weights(0, 1, w_in, w_out, after=(pack,), us=10)
        w_oth[0] = other(w_own[0])
        (tok,) = call(pad_kernel, [rows], (tokens,), after=(w_own[0],), fetch=True, us=6)
        pair = lambda a, b, after, us=0.2: call(pair_kernel, [held(2, PACK, 128)], (a, b), after=after, mib=8, us=us)[0]
        before = (tok,)
        w_own[1] = packed_weights(1, 1, w_in, w_out, after=(tok,))
        w_oth[1] = other(w_own[1])
        pair_b = pair(slots[2], slots[3], (w_own[1],))
        w_own[2] = packed_weights(2, 2, w_in, w_out, after=(pair_b,), us=1.5)
        w_oth[2] = other(w_own[2])
        (cot0,) = call(pad_kernel, [rows], (cotangent,), after=(w_own[2],), fetch=True, us=1.1)
        far = [other(slots[0]), other(slots[1])]
        far = [gate(far[0], (cot0, w_oth[0])), gate(far[1], (cot0,))]
        far_b = other(pair_b)
        pair_a = pair(slots[0], slots[1], (far[0],))
        far_a = pair(far[0], far[1], (pair_a,), 1.5)
        sib_a = pair(core(slots[0]), core(slots[1]), (far_a,))
        sib_far = pair(core(far[0]), core(far[1]), (sib_a,))
        packs = [[pair_a, far_a, sib_a, sib_far]]
        before = ()
    else:
        small_own = jnp.concatenate([w_router.T, jnp.stack([gain_one, shift_one, gain_two, shift_two])])
        small = lax.all_gather(small_own, "fsdp", axis=1, tiled=True)
        qkv_all = lax.all_gather(lax.all_gather(w_qkv, "fsdp", axis=1, tiled=True), "heads", axis=2, tiled=True)
        out_all = lax.all_gather(lax.all_gather(w_attn_out, "fsdp", axis=1, tiled=True), "heads", axis=0, tiled=True)
        packs = packs_of_whole(qkv_all, out_all, small)
        in_all = lax.all_gather(w_in, "fsdp", axis=1, tiled=True)
        o_all = lax.all_gather(w_out, "fsdp", axis=2, tiled=True)
        for i, (first, n) in enumerate(((0, 1), (1, 1), (2, 2))):
            w_own[i] = packed_weights(first, n, in_all[:, :256], o_all[:, :, :256])
            w_oth[i] = packed_weights(first, n, in_all[:, 256:], o_all[:, :, 256:])
        (tok,) = call(pad_kernel, [rows], (tokens,), fetch=True)
        (cot0,) = call(pad_kernel, [rows], (cotangent,), fetch=True)
        before = ()

    named = jnp.pad(routes.T.reshape(2, 8, SEQ), ((0, 0), (0, 0), (0, PAD - SEQ)), constant_values=-1)
    named = named.reshape(2, 4, ROWS).transpose(1, 0, 2)

    kept = [pltpu.HBM(shape, BF) for shape in ((2, ROWS, 384), (2, ROWS, 128), (2, D, 384), (2, 128, D))]
    scratch = [pltpu.VMEM(x.shape, BF) for x in kept] + [pltpu.SemaphoreType.DMA((4, 2))]
    small, n1, acc, qkv_a, mix_a, wq_a, wo_a = forward(
        functools.partial(attn_fwd_kernel, True, at),
        [held(8, D), held(ROWS, D), held(ROWS, D, dtype=F32)],
        kept,
        (tok, *packs[0]),
        scratch,
        before,
    )
    cot1, cot2 = core(cot0), across(cot0)
    before = (cot1,)
    if near:
        far_b = gate(far_b, (n1,), 2.2)
        before = (cot1,)
        packs.append([pair_b, far_b, core(pair_b), core(far_b)])
    n2_0, resid, qkv_b, mix_b, wq_b, wo_b = forward(
        functools.partial(attn_fwd_kernel, False, at),
        [held(ROWS, D), held(ROWS, D, dtype=F32)],
        kept,
        (tok, *packs[1], small, n1, acc),
        scratch,
        before,
        5.5,
    )
    n2_1, n2_2 = core(n2_0), across(n2_0)

    shared = (named, small)
    rows_a = (n2_0, n2_1, cot0, cot1)
    cot2 = gate(cot2, (n2_0,))
    weights = [assemble(at, 0, w_own, w_oth, (cot2,), 2)]
    state_a, grads0 = moe(0, 0, at, rows_a, weights[0], (), shared)
    weights.append(assemble(at, 1, w_own, w_oth, grads0[:1]))
    state_a, grads1 = moe(1, 0, at, rows_a, weights[1], state_a, shared, us=4)
    n2_2 = gate(n2_2, grads1[:1], 0.8)
    rows_b = (n2_2, core(n2_2), cot2, core(cot2))
    state_b, (keep0, send0) = moe(0, 2, at, rows_b, weights[0], (), shared, grads0)
    state_b, (keep1, send1) = moe(1, 2, at, rows_b, weights[1], state_b, shared, grads1)
    weights.append(assemble(at, 2, w_own, w_oth, (keep1,)))
    state_a, grads2 = moe(2, 0, at, rows_a, weights[2], state_a, shared)
    weights.append(assemble(at, 3, w_own, w_oth, grads2[:1], 1.0))
    state_b, (keep2, send2) = moe(2, 2, at, rows_b, weights[2], state_b, shared, grads2, after=weights[3])
    ones, twos, threes, before = [None] * 4, [None] * 4, [None] * 4, ()
    if near:
        got0 = other(send0)
        ones[0] = add(keep0, got0, after=(keep2,), us=2)
        before = (ones[0],)
    (d2, *d3, m2, m3, wr_b), grads3 = moe(
        3, 2, at, rows_b, weights[3], state_b, shared, end=True, after=before, us=5
    )
    (d_sum,) = call(rows_kernel, [held(ROWS, D)], (d2, core(d3[0]), core(d3[1])), after=grads3[:1], us=1.2)
    d_far = across(d_sum)
    before = (d_sum,)
    if near:
        got1 = other(send1)
        ones[1] = add(keep1, got1, after=before, us=1.5)
        before = (ones[1],)
    (d0, *d1, m0, m1, wr_a), (keep3, send3) = moe(
        3, 0, at, rows_a, weights[3], state_a, shared, grads3, True, before, us=5
    )
    keeps, sends = (keep0, keep1, keep2, keep3), (send0, send1, send2, send3)
    d_near = [core(d) for d in d1]
    inward = lambda x: lax.ppermute(x, "heads", [(0, 1), (3, 2)])
    middle = lambda x: lax.ppermute(x, "heads", [(1, 2), (2, 1)])
    outward = lambda x: lax.ppermute(x, "heads", [(1, 0), (2, 3)])
    before = ()
    if near:
        got = [got0, got1] + [other(send) for send in sends[2:]]
        twos[0] = add(ones[0], inward(ones[0]), after=(keep3,), us=4.3)
        before = (twos[0],)

    scratch = [pltpu.VMEM(shape, BF) for shape in ((ROWS, 384), (D, 384), (128, D), (D, ROWS), (ROWS, D))]
    both = [held(2, 2, PACK, 128)] + [held(2, PACK, 128)] * 2
    own_b, sib_2, sib_3, dresid, sgrad, dn1 = call(
        functools.partial(attn_bwd_kernel, True, at),
        both + [held(ROWS, D, dtype=F32), held(8, D, dtype=F32), held(ROWS, D, dtype=F32)],
        (d0, *d_near, d_far, resid, cot0, wr_a, wr_b, small, n1, qkv_b, mix_b, wq_b, wo_b),
        scratch,
        after=before,
        us=6.2,
    )
    if near:
        ones[2] = add(keeps[2], got[2], after=(dn1,), us=1.5)
        keep_b, send_b = call(
            halves_kernel, [held(2, PACK, 128)] * 2, (own_b, core(sib_2), core(sib_3)), after=(ones[2],), us=1.5
        )
        twos[1] = add(ones[1], inward(ones[1]), after=(keep_b,), us=1)
        threes[0] = add(twos[0], middle(twos[0]), after=(twos[1],), us=0.3)
        both_ways = mixed(at, ones[2], threes[0], us=1.5)
        neighbour0 = flip(both_ways, "heads", 1)
        ones[3] = add(keeps[3], got[3], after=(both_ways,), us=0.3)
        before = (ones[3],)
    own_a, sib_0, sib_1, input_grad = call(
        functools.partial(attn_bwd_kernel, False, at),
        both + [sds((SEQ * 2, D), BF)],
        (dresid, sgrad, dn1, tok, small, n1, qkv_a, mix_a, wq_a, wo_a),
        scratch + [pltpu.VMEM((8, D), F32), pltpu.VMEM((ROWS, D), F32)],
        after=before,
        us=8.2,
    )

    if near:
        one_pack = held(PACK, 128)
        slot2, slot3 = call(slots_kernel, [one_pack] * 2, (keep_b, other(send_b)), after=(own_a,))
        keep_a, send_a = call(
            halves_kernel, [held(2, PACK, 128)] * 2, (own_a, core(sib_0), core(sib_1)), after=(slot3,), us=1.5
        )
        threes[1] = add(twos[1], middle(twos[1]), after=(keep_a,), us=0.3)
        both_ways = mixed(at, ones[3], threes[1], us=2)
        neighbour1 = flip(both_ways, "heads", 1)
        twos[2] = add(ones[2], neighbour0, after=(both_ways,), us=2)
        *grads, done = finish(at, 0, threes[0], neighbour0, after=(twos[2],), us=2)
        slot0, given = call(
            both_slots_kernel, [one_pack, held(2, PACK, 128)], (keep_a, other(send_a), slot3), after=(done,), us=4
        )
        twos[3] = add(ones[3], neighbour1, after=(given,), us=0.3)
        *grads, done = finish(at, 1, threes[1], neighbour1, grads, after=(twos[3],), us=1.2)
        threes[2] = add(twos[2], middle(twos[2]), after=(done,), us=3)
        pair, over = call(
            cross_kernel, [one_pack] * 2, (slot0, slot2, flip(given, "heads", 1)), after=(threes[2],), us=1.5
        )
        threes[3] = add(twos[3], middle(twos[3]), after=(pair,), us=2)
        m_near = core(m1)
        m_sum = add(m2, core(m3), after=(threes[3],), us=5)
        m_far = across(m_sum)
        half = add(pair, flip(over, "heads", 2), after=(m_sum,))
        *grads, done = finish(at, 2, threes[2], outward(threes[2]), grads, after=(half,), us=6)
        half = add(half, across(half), after=(done,), us=2)
        vector = sds((1, 256), F32)
        qkv_grad, o_grad, wr_grad, *vectors = call(
            functools.partial(unpack_kernel, at),
            [sds((3, 256, 128), F32), sds((128, 256), F32), sds((4, 256), F32)] + [vector] * 4,
            (half, core(half)),
        )
        (output,) = call(out_kernel, [sds((SEQ * 2, D), BF)], (resid, m0, m_near, m_far), after=(half,))
        win_grad, wout_grad, _ = finish(at, 3, threes[3], outward(threes[3]), grads, after=(half,))
        vectors = [v.reshape(256) for v in vectors]
    else:
        m_near = core(m1)
        m_far = across(add(m2, core(m3)))
        (output,) = call(out_kernel, [sds((SEQ * 2, D), BF)], (resid, m0, m_near, m_far))
        keep, send = jnp.stack(keeps), jnp.stack(sends)
        gin = jnp.concatenate([keep[:, :256], send[:, :256]], 1)
        gout = jnp.concatenate([keep[:, 256:], send[:, 256:]], 1).transpose(0, 2, 1)
        win_grad = lax.psum_scatter(gin, "fsdp", scatter_dimension=1, tiled=True)
        wout_grad = lax.psum_scatter(gout, "fsdp", scatter_dimension=2, tiled=True)
        win_grad = lax.psum(win_grad, "heads").astype(F32)
        wout_grad = lax.psum(wout_grad, "heads").astype(F32)
        qkv_grad, o_grad, sgrad = whole_of_packs(((own_a, jnp.stack([sib_0, sib_1])), (own_b, jnp.stack([sib_2, sib_3]))))
        qkv_grad = lax.psum_scatter(qkv_grad, "fsdp", scatter_dimension=1, tiled=True)
        qkv_grad = lax.psum_scatter(qkv_grad, "heads", scatter_dimension=2, tiled=True)
        qkv_grad = lax.psum(qkv_grad, "tensor")
        o_grad = lax.psum_scatter(o_grad, "fsdp", scatter_dimension=1, tiled=True)
        o_grad = lax.psum_scatter(o_grad, "heads", scatter_dimension=0, tiled=True)
        o_grad = lax.psum(o_grad, "tensor")
        sgrad = lax.psum(sgrad, ("fsdp", "heads", "tensor"))
        sgrad = lax.dynamic_slice_in_dim(sgrad, f * gain_one.shape[0], gain_one.shape[0], 1)
        wr_grad, vectors = sgrad[0:4], [sgrad[4 + i] for i in range(4)]

    return (
        output,
        input_grad,
        vectors[0],
        vectors[1],
        qkv_grad,
        o_grad,
        vectors[2],
        vectors[3],
        wr_grad.T,
        win_grad,
        wout_grad,
    )


def solution(mesh):
    placed = (
        P(("fsdp", "heads", "tensor"), None),
        P("fsdp"),
        P("fsdp"),
        P(None, "fsdp", "heads"),
        P("heads", "fsdp"),
        P("fsdp"),
        P("fsdp"),
        P("fsdp", None),
        P(None, "fsdp", "tensor"),
        P(None, "tensor", "fsdp"),
        P(("fsdp", "heads"), None),
        P(("fsdp", "heads", "tensor"), None),
    )
    return jax.shard_map(
        local,
        mesh=mesh,
        in_specs=placed,
        out_specs=(
            P(("fsdp", "heads", "tensor"), None),
            P(("fsdp", "heads", "tensor"), None),
            P("fsdp"),
            P("fsdp"),
            P(None, "fsdp", "heads"),
            P("heads", "fsdp"),
            P("fsdp"),
            P("fsdp"),
            P("fsdp", None),
            P(None, "fsdp", "tensor"),
            P(None, "tensor", "fsdp"),
        ),
        check_vma=False,
    )
```
